32 devices in a mesh: fsdp: 4 (over x, core), ctx: 2 (over y), tp: 4 (over z).
Axes of the slice: x: 2, y: 2, z: 4, core: 2. Of those that a mesh axis runs over, the one named last changes fastest.
Arguments:
- stream: bfloat16 [4, 1024, 2048], P('fsdp', 'ctx'), may hold values from -6 to 6
- cotangent: bfloat16 [4, 1024, 2048], P('fsdp', 'ctx'), may hold values from -6 to 6
- lengths: int32 [4], P('fsdp'), may hold values from 512 to 1024, as said below
- first_gain: bfloat16 [2048], P('fsdp'), may hold values from 0.25 to 1.75
- first_shift: bfloat16 [2048], P('fsdp'), may hold values from -3 to 3
- query_weight: bfloat16 [2048, 2048], P('fsdp', 'tp'), may hold values from -0.125 to 0.125
- query_bias: bfloat16 [16, 128], P('tp', 'fsdp'), may hold values from -3 to 3
- pair_weight: bfloat16 [2048, 256], P('fsdp'), may hold values from -0.125 to 0.125
- value_bias: bfloat16 [128], P('fsdp'), may hold values from -0.3125 to 0.3125
- output_weight: bfloat16 [2048, 2048], P('tp', 'fsdp'), may hold values from -1 to 1
- output_bias: bfloat16 [2048], P('fsdp'), may hold values from -1.75 to 1.75
- second_gain: bfloat16 [2048], P('fsdp'), may hold values from 0.25 to 1.75
- second_shift: bfloat16 [2048], P('fsdp'), may hold values from -3 to 3
- up_weight: bfloat16 [2048, 8192], P('fsdp', 'tp'), may hold values from -0.20992233 to 0.20992233
- up_bias: bfloat16 [64, 128], P('tp', 'fsdp'), may hold values from -3 to 3
- down_weight: bfloat16 [8192, 2048], P('tp', 'fsdp'), may hold values from -0.0625 to 0.0625
- down_bias: bfloat16 [2048], P('fsdp'), may hold values from -1.75 to 1.75
Outputs:
- result: bfloat16 [4, 1024, 2048], P('fsdp', 'ctx')
- stream_grad: bfloat16 [4, 1024, 2048], P('fsdp', 'ctx')
- first_gain_grad: float32 [2048], P('fsdp')
- first_shift_grad: float32 [2048], P('fsdp')
- query_weight_grad: float32 [2048, 2048], P('fsdp', 'tp')
- query_bias_grad: float32 [16, 128], P('tp', 'fsdp')
- pair_weight_grad: float32 [2048, 256], P('fsdp')
- value_bias_grad: float32 [128], P('fsdp')
- output_weight_grad: float32 [2048, 2048], P('tp', 'fsdp')
- output_bias_grad: float32 [2048], P('fsdp')
- second_gain_grad: float32 [2048], P('fsdp')
- second_shift_grad: float32 [2048], P('fsdp')
- up_weight_grad: float32 [2048, 8192], P('fsdp', 'tp')
- up_bias_grad: float32 [64, 128], P('tp', 'fsdp')
- down_weight_grad: float32 [8192, 2048], P('tp', 'fsdp')
- down_bias_grad: float32 [2048], P('fsdp')
- root_means: float32 [3], replicated
The draws below stay inside these ranges and needn't reach their ends.
Inputs may be any that keep to these rules, and one draw needn't show every extreme that they name: `lengths`: the number of valid leading slots of each sequence; some sequence is full and some is half full.
All inputs are finite; a program needn't handle non-finite values.
Results may differ from the reference program's by a relative error of at most 0.013.
Values may be sent and summed in bfloat16 or wider, within the bound.
A program may use at most 192 MiB of HBM per device.

```python
import math
import jax
import jax.numpy as jnp
from jax import lax

D = 2048
HEADS = 16
HD = 128
FF = 8192
LEN = 1024
SEQS = 4


def draw_lengths(key, part):
    drawn = jax.random.randint(key, (SEQS,), LEN // 2, LEN + 1).astype(jnp.int32)
    drawn = drawn.at[0].set(LEN)
    return drawn.at[SEQS - 1].set(LEN // 2)


def draw_up_weight(key, part):
    key = jax.random.fold_in(key, 7)
    own_key, shared_key = jax.random.split(key)
    scale = D ** (-0.5)
    own_part = jnp.clip(jax.random.normal(own_key, (D, FF), jnp.float32), -6.0, 6.0) * scale
    shared_part = jnp.clip(jax.random.normal(shared_key, (FF,), jnp.float32), -6.0, 6.0) * (0.5 * scale)
    return (own_part + shared_part[None, :]).astype(jnp.bfloat16)


def level_of(rng, extent, shards, least, high):
    factor_of, own = 1.0, jax.random.fold_in(rng, 6)
    for position, parts in shards:
        draws = jnp.exp(jax.random.uniform(jax.random.fold_in(own, position), (parts,), jnp.float32, least / len(shards), high / len(shards)))
        factor_of = factor_of * jnp.repeat(draws, extent[position] // parts).reshape([-1 if axis == position else 1 for axis in range(len(extent))])
    return factor_of


def scatter_about(stream_key, extent, deviation, bound, shards=(), kind=jnp.bfloat16):
    values = jax.random.normal(stream_key, extent, jnp.float32) * deviation
    if len(shards) > 0:
        values = level_of(stream_key, extent, shards, -0.22, 0.18) * values
    return jnp.clip(values, min=-bound, max=bound).astype(kind)


def setup_inputs(seed: int = 0) -> dict:
    splits = jax.random.split(jax.random.key(seed), 18)
    return {
        "stream": scatter_about(splits[0], (SEQS, LEN, D), 1.0, 6.0, ((0, 4), (1, 2))),
        "cotangent": scatter_about(splits[1], (SEQS, LEN, D), 1.0, 6.0, ((0, 4), (1, 2))),
        "lengths": draw_lengths(jax.random.fold_in(splits[17], 71), 0),
        "first_gain": jnp.clip(1.0 + 0.15 * jax.random.normal(splits[3], (D,), jnp.float32), 0.25, 1.75).astype(jnp.bfloat16),
        "first_shift": scatter_about(splits[4], (D,), 0.5, 3.0, ((0, 4),)),
        "query_weight": scatter_about(splits[5], (D, D), D ** -0.5, 0.125, ((0, 4), (1, 4))),
        "query_bias": scatter_about(splits[6], (HEADS, HD), 0.5, 3.0, ((0, 4), (1, 4))),
        "pair_weight": scatter_about(splits[7], (D, 2 * HD), D ** -0.5, 0.125, ((0, 4),)),
        "value_bias": scatter_about(splits[8], (HD,), 0.05, 0.3125, ((0, 4),)),
        "output_weight": scatter_about(splits[9], (D, D), (D // 64) ** -0.5, 1.0, ((0, 4), (1, 4))),
        "output_bias": scatter_about(splits[10], (D,), 0.3, 1.75, ((0, 4),)),
        "second_gain": jnp.clip(1.0 + 0.15 * jax.random.normal(splits[11], (D,), jnp.float32), 0.25, 1.75).astype(jnp.bfloat16),
        "second_shift": scatter_about(splits[12], (D,), 0.5, 3.0, ((0, 4),)),
        "up_weight": draw_up_weight(jax.random.fold_in(splits[17], 71), 0),
        "up_bias": scatter_about(splits[14], (FF // HD, HD), 0.5, 3.0, ((0, 4), (1, 4))),
        "down_weight": scatter_about(splits[15], (FF, D), FF ** -0.5, 0.0625, ((0, 4), (1, 4))),
        "down_bias": scatter_about(splits[16], (D,), 0.3, 1.75, ((0, 4),)),
    }


EPSILON = 1e-05
NEGATIVE = -1e+30
HIGHEST = lax.Precision.HIGHEST

@jax.custom_vjp
def low(v):
    return lax.optimization_barrier(v.astype(jnp.bfloat16)).astype(jnp.float32)

@jax.custom_vjp
def low_back(v):
    return v

def low_keep(v):
    return (low(v), None)

def low_pass(kept, grad):
    return (grad,)

def back_keep(v):
    return (v, None)

def back_low(kept, grad):
    return (low(grad),)
low.defvjp(low_keep, low_pass)
low_back.defvjp(back_keep, back_low)

def layer_norm(inputs, norm_gain, norm_shift):
    center = inputs - lax.optimization_barrier(jnp.mean(inputs, -1, keepdims=True))
    spread = lax.optimization_barrier(jnp.mean(center * center, -1, keepdims=True))
    return center * lax.rsqrt(spread + EPSILON) * norm_gain + norm_shift

def product(left_side, right_side):
    return jnp.dot(left_side, right_side, precision=HIGHEST)

def one_sequence(params, token_rows, length):
    first_gain, first_shift, query_weight, query_bias, pair_weight, value_bias, output_weight, output_bias, second_gain, second_shift, up_weight, up_bias, down_weight, down_bias = params
    normed = low(layer_norm(token_rows, first_gain, first_shift))
    queries = low_back(low(product(normed, query_weight) + query_bias.reshape(-1)))
    pair_bias = jnp.concatenate([jnp.zeros_like(value_bias), value_bias])
    key_values = low_back(low(product(normed, pair_weight) + pair_bias))
    key_rows = key_values[:, :HD]
    value_rows = key_values[:, HD:]
    heads_view = queries.reshape(LEN, HEADS, HD)
    raw_scores = jnp.einsum('thd,kd->htk', heads_view, key_rows, precision=HIGHEST)
    places = jnp.arange(LEN)
    allowed = (places[None, :] <= places[:, None]) & (places[None, :] < length)
    scores = jnp.where(allowed[None], low_back(raw_scores) * (1.0 / math.sqrt(HD)), NEGATIVE)
    soft_weights = low(jax.nn.softmax(scores, axis=-1))
    mixture = jnp.einsum('htk,kd->thd', soft_weights, value_rows, precision=HIGHEST).reshape(LEN, HEADS * HD)
    mixture = low_back(low(mixture))
    branch = low_back(product(mixture, output_weight) + output_bias)
    middle = token_rows + branch
    normed_two = low(layer_norm(middle, second_gain, second_shift))
    hidden_pre = low_back(product(normed_two, up_weight) + up_bias.reshape(-1))
    hidden = low(jax.nn.gelu(hidden_pre, approximate=True))
    feed_branch = low_back(product(hidden, down_weight) + down_bias)
    return (middle + feed_branch, branch, feed_branch)

def reference(stream, cotangent, lengths, first_gain, first_shift, query_weight, query_bias, pair_weight, value_bias, output_weight, output_bias, second_gain, second_shift, up_weight, up_bias, down_weight, down_bias):
    params = tuple((weight.astype(jnp.float32) for weight in (first_gain, first_shift, query_weight, query_bias, pair_weight, value_bias, output_weight, output_bias, second_gain, second_shift, up_weight, up_bias, down_weight, down_bias)))
    inputs_wide = stream.astype(jnp.float32)

    def forward(token_rows, weight_set):

        def apply_one(packed):
            return one_sequence(weight_set, packed[0], packed[1])
        return lax.map(jax.checkpoint(apply_one), (token_rows, lengths))
    (result, branch, feed_branch), pullback = jax.vjp(forward, inputs_wide, params)
    valid = (jnp.arange(LEN)[None, :] < lengths[:, None]).astype(jnp.float32)[..., None]
    grad_total = cotangent.astype(jnp.float32) * valid
    stream_grad, grads = pullback((grad_total, jnp.zeros_like(branch), jnp.zeros_like(feed_branch)))
    count = jnp.sum(valid)

    def root_mean(field):
        return jnp.sqrt(jnp.sum(valid * field * field) / (count * D))
    root_means = jnp.stack([root_mean(result), root_mean(branch), root_mean(feed_branch)])
    return ((result * valid).astype(jnp.bfloat16), stream_grad.astype(jnp.bfloat16), grads[0], grads[1], grads[2], grads[3], grads[4], grads[5], grads[6], grads[7], grads[8], grads[9], grads[10], grads[11], grads[12], grads[13], root_means)
```

```python
import math

import jax
import jax.numpy as jnp
from jax import lax
from jax.sharding import PartitionSpec as P

HD = 128


EPSILON = 1e-05
NEGATIVE = -1e30


def norm_forward(inputs, norm_gain, norm_shift):
    center = inputs - jnp.mean(inputs, -1, keepdims=True)
    spread = jnp.mean(center * center, -1, keepdims=True)
    scaled = lax.rsqrt(spread + EPSILON)
    unit_rows = center * scaled
    return (unit_rows * norm_gain + norm_shift, unit_rows, scaled)


def norm_backward(upstream, unit_rows, scaled, norm_gain):
    gained = upstream * norm_gain
    return scaled * (
        gained
        - jnp.mean(gained, -1, keepdims=True)
        - unit_rows * jnp.mean(gained * unit_rows, -1, keepdims=True)
    )


def score_block(query_block, key_rows, length, query_places):
    raw_scores = jnp.einsum("qd,kd->qk", query_block, key_rows, preferred_element_type=jnp.float32)
    key_places = jnp.arange(key_rows.shape[0])
    allowed = (key_places[None, :] <= query_places[:, None]) & (key_places[None, :] < length)
    return jnp.where(allowed, raw_scores * (1.0 / math.sqrt(HD)), NEGATIVE)


def attend(query_block, pair_block, length, query_places):
    scores = score_block(query_block, pair_block[:, :HD], length, query_places)
    peak = jnp.max(scores, -1, keepdims=True)
    exponent = jnp.exp(scores - peak)
    row_total = jnp.sum(exponent, -1, keepdims=True)
    soft_weights = (exponent / row_total).astype(jnp.bfloat16)
    mixture = jnp.dot(soft_weights, pair_block[:, HD:], preferred_element_type=jnp.float32)
    return (mixture.astype(jnp.bfloat16), (peak + jnp.log(row_total))[:, 0])


def attend_back(query_block, pair_block, length, query_places, log_total, grad_mixture):
    key_rows = pair_block[:, :HD]
    value_rows = pair_block[:, HD:]
    scores = score_block(query_block, key_rows, length, query_places)
    soft_weights = jnp.exp(scores - log_total[:, None])
    grad_weights = jnp.einsum(
        "qd,kd->qk", grad_mixture, value_rows, preferred_element_type=jnp.float32
    )
    row_dot = jnp.sum(soft_weights * grad_weights, -1, keepdims=True)
    grad_scores = (soft_weights * (grad_weights - row_dot) * (1.0 / math.sqrt(HD))).astype(
        jnp.bfloat16
    )
    grad_query = jnp.dot(grad_scores, key_rows, preferred_element_type=jnp.float32)
    grad_keys = jnp.einsum(
        "qk,qd->kd", grad_scores, query_block, preferred_element_type=jnp.float32
    )
    grad_values = jnp.einsum(
        "qk,qd->kd",
        soft_weights.astype(jnp.bfloat16),
        grad_mixture,
        preferred_element_type=jnp.float32,
    )
    return (grad_query, jnp.concatenate([grad_keys, grad_values], -1))


def swap(block, axis, bit):
    count = lax.axis_size(axis)
    return lax.ppermute(block, axis, [(place, place ^ bit) for place in range(count)])


def bits_of(axis):
    count, bit, found = lax.axis_size(axis), 1, []
    while bit < count:
        found.append(bit)
        bit *= 2
    return found


def pick(array, index, size, axis):
    return lax.dynamic_slice_in_dim(array, index * size, size, axis)


def over_ctx(part, axis):
    held = [(0, part)]
    for bit in bits_of("ctx"):
        held = held + [(mask ^ bit, swap(block, "ctx", bit)) for mask, block in held]
    place = lax.axis_index("ctx")
    size = part.shape[axis]
    shape = list(part.shape)
    shape[axis] = size * len(held)
    whole = jnp.zeros(shape, part.dtype)
    for mask, block in held:
        whole = lax.dynamic_update_slice_in_dim(whole, block, (place ^ mask) * size, axis)
    return whole


def gather_blocks(shard):
    count, split = lax.axis_size("fsdp"), lax.axis_size("ctx")
    blocks = {0: shard}
    for bit in bits_of("fsdp"):
        if bit == 1:
            blocks[1] = swap(shard, "fsdp", 1)
        else:
            size = shard.shape[0] // split
            part = pick(shard, lax.axis_index("ctx"), size, 0)
            for mask in [m for m in list(blocks) if m < bit and m % 2 == 0]:
                source = part if mask == 0 else pick(blocks[mask], lax.axis_index("ctx"), size, 0)
                blocks[mask ^ bit] = over_ctx(swap(source, "fsdp", bit), 0)
                blocks[mask ^ bit ^ 1] = swap(blocks[mask ^ bit], "fsdp", 1)
    return [blocks[r] for r in range(count)]


def join_blocks(blocks, axis):
    place = lax.axis_index("fsdp")
    size = blocks[0].shape[axis]
    shape = list(blocks[0].shape)
    shape[axis] = size * len(blocks)
    whole = jnp.zeros(shape, blocks[0].dtype)
    for r, block in enumerate(blocks):
        whole = lax.dynamic_update_slice_in_dim(whole, block, (place ^ r) * size, axis)
    return whole


def reduce_blocks(parts):
    held = list(parts)
    for bit in bits_of("fsdp"):
        kept = {}
        for r in range(len(held)):
            if held[r] is None or not r & bit:
                continue
            came = swap(held[r].astype(jnp.bfloat16), "fsdp", bit)
            kept[r ^ bit] = came
            held[r] = None
        for r, came in kept.items():
            held[r] = held[r] + came.astype(jnp.float32)
    total = held[0]
    for bit in bits_of("ctx"):
        sent = total.astype(jnp.bfloat16)
        total = sent.astype(jnp.float32) + swap(sent, "ctx", bit).astype(jnp.float32)
    return total


def line_reduce(own):
    count, place = lax.axis_size("tp"), lax.axis_index("tp")
    right = left = None
    for step in range(1, count):
        index = jnp.minimum(count - step + place, count - 1)
        value = lax.dynamic_index_in_dim(own, index, 0, False)
        if right is not None:
            value = (value.astype(jnp.float32) + right.astype(jnp.float32)).astype(own.dtype)
        right = lax.ppermute(value, "tp", [(i, i + 1) for i in range(step)])
        index = jnp.maximum(place - (count - step), 0)
        value = lax.dynamic_index_in_dim(own, index, 0, False)
        if left is not None:
            value = (value.astype(jnp.float32) + left.astype(jnp.float32)).astype(own.dtype)
        left = lax.ppermute(value, "tp", [(count - 1 - i, count - 2 - i) for i in range(step)])
    total = lax.dynamic_index_in_dim(own, place, 0, False).astype(jnp.float32)
    return total + right.astype(jnp.float32) + left.astype(jnp.float32)


def line_gather(own):
    count, place = lax.axis_size("tp"), lax.axis_index("tp")
    rights, lefts = [], []
    right = left = own
    for step in range(1, count):
        right = lax.ppermute(right, "tp", [(i, i + 1) for i in range(step - 1, count - 1)])
        left = lax.ppermute(
            left, "tp", [(count - 1 - i, count - 2 - i) for i in range(step - 1, count - 1)]
        )
        rights.append(right)
        lefts.append(left)
    stacked = jnp.concatenate(rights[::-1] + [own] + lefts, 0)
    size = own.shape[0]
    return lax.dynamic_slice_in_dim(stacked, (count - 1 - place) * size, count * size, 0)


def sum_over(values, axes):
    for axis in axes:
        for bit in bits_of(axis):
            values = values + swap(values, axis, bit)
    return values


def body(
    stream,
    cotangent,
    lengths,
    first_gain,
    first_shift,
    query_weight,
    query_bias,
    pair_weight,
    value_bias,
    output_weight,
    output_bias,
    second_gain,
    second_shift,
    up_weight,
    up_bias,
    down_weight,
    down_bias,
):
    low, wide = jnp.bfloat16, jnp.float32
    fsdp, tp = lax.axis_size("fsdp"), lax.axis_size("tp")
    me, place, zone = lax.axis_index("fsdp"), lax.axis_index("ctx"), lax.axis_index("tp")
    seq_count, group_len, model_width = stream.shape
    token_count = seq_count * group_len
    local_heads = query_weight.shape[1] // HD
    share = token_count // tp

    smalls = (first_gain, first_shift, output_bias, second_gain, second_shift, down_bias)
    piece = first_gain.shape[0]
    flat = [s for s in smalls] + [query_bias.reshape(-1), value_bias, up_bias.reshape(-1)]
    packed = jnp.concatenate(flat)
    small_blocks = [packed]
    for bit in bits_of("fsdp"):
        small_blocks = small_blocks + [swap(block, "fsdp", bit) for block in small_blocks]
    small_all = join_blocks([block[None] for block in small_blocks], 0)
    offsets, start = [], 0
    for s in flat:
        offsets.append((start, s.size))
        start += s.size

    def small(index):
        start, size = offsets[index]
        return small_all[:, start : start + size]

    gain_one, shift_one, output_add, gain_two, shift_two, down_add = [
        small(k).reshape(-1).astype(wide) for k in range(6)
    ]
    query_add = (
        small(6).reshape((fsdp,) + query_bias.shape).transpose(1, 0, 2).reshape(-1).astype(wide)
    )
    value_add = small(7).reshape(-1)
    up_add = small(8).reshape((fsdp,) + up_bias.shape).transpose(1, 0, 2).reshape(-1).astype(wide)

    query_full = join_blocks(gather_blocks(query_weight), 0)
    pair_full = join_blocks(gather_blocks(pair_weight), 0)
    output_full = join_blocks(gather_blocks(output_weight), 1)
    up_full = join_blocks(gather_blocks(up_weight), 0)
    down_full = join_blocks(gather_blocks(down_weight), 1)

    offset = place * group_len
    token_places = offset + jnp.arange(group_len)
    keep_rows = (token_places[None, :] < lengths[:, None]).astype(wide).reshape(token_count, 1)
    keep_share = pick(keep_rows, zone, share, 0)
    query_places = offset + jnp.arange(group_len * local_heads) // local_heads
    flat_stream = stream.reshape(token_count, model_width)
    token_rows = flat_stream.astype(wide)
    normed_one, unit_one, scaled_one = norm_forward(token_rows, gain_one, shift_one)
    input_one = normed_one.astype(low)
    queries = (jnp.dot(input_one, query_full, preferred_element_type=wide) + query_add).astype(low)
    pair_add = jnp.concatenate([jnp.zeros_like(value_add), value_add]).astype(wide)
    key_values = (jnp.dot(input_one, pair_full, preferred_element_type=wide) + pair_add).astype(low)
    all_pairs = over_ctx(key_values.reshape(seq_count, group_len, 2 * HD), 1)
    query_seqs = queries.reshape(seq_count, group_len * local_heads, HD)
    mixture, log_total = lax.map(
        lambda packed: attend(packed[0], packed[1], packed[2], query_places),
        (query_seqs, all_pairs, lengths),
    )
    mixture = mixture.reshape(token_count, local_heads * HD)
    stream_share = pick(flat_stream, zone, share, 0).astype(wide)
    branch_part = jnp.dot(mixture, output_full, preferred_element_type=wide).astype(low)
    branch = line_reduce(branch_part.reshape(tp, share, model_width)) + output_add
    middle = stream_share + branch
    normed_two, unit_two, scaled_two = norm_forward(middle, gain_two, shift_two)
    input_two = line_gather(normed_two.astype(low))

    grad_total = cotangent.reshape(token_count, model_width).astype(wide) * keep_rows
    grad_feed = grad_total.astype(low)
    grad_total_share = pick(grad_total, zone, share, 0)
    hidden_pre = jnp.dot(input_two, up_full, preferred_element_type=wide) + up_add
    hidden = jax.nn.gelu(hidden_pre, approximate=True).astype(low)
    feed_part = jnp.dot(hidden, down_full, preferred_element_type=wide).astype(low)
    grad_hidden = jnp.einsum("td,fd->tf", grad_feed, down_full, preferred_element_type=wide)
    unused_value, gelu_pull = jax.vjp(
        lambda inner: jax.nn.gelu(inner, approximate=True), hidden_pre
    )
    grad_pre = gelu_pull(grad_hidden)[0].astype(low)
    grad_two_part = jnp.einsum("tf,df->td", grad_pre, up_full, preferred_element_type=wide).astype(
        low
    )
    columns = model_width // fsdp

    def turned(rows, r):
        return pick(rows, me ^ r, columns, 1)

    down_grad = reduce_blocks(
        [
            jnp.einsum("tf,td->fd", hidden, turned(grad_feed, r), preferred_element_type=wide)
            for r in range(fsdp)
        ]
    )
    up_grad = reduce_blocks(
        [
            jnp.einsum("td,tf->df", turned(input_two, r), grad_pre, preferred_element_type=wide)
            for r in range(fsdp)
        ]
    )
    grad_normed_two = line_reduce(grad_two_part.reshape(tp, share, model_width))
    grad_middle = grad_total_share + norm_backward(grad_normed_two, unit_two, scaled_two, gain_two)
    grad_branch_share = grad_middle.astype(low)
    grad_branch = line_gather(grad_branch_share)
    output_grad = reduce_blocks(
        [
            jnp.einsum("tq,td->qd", mixture, turned(grad_branch, r), preferred_element_type=wide)
            for r in range(fsdp)
        ]
    )
    grad_mixture = jnp.einsum("td,qd->tq", grad_branch, output_full, preferred_element_type=wide)
    grad_mixture = grad_mixture.astype(low).reshape(seq_count, group_len * local_heads, HD)
    grad_query, grad_pairs = lax.map(
        lambda packed: attend_back(
            packed[0], packed[1], packed[2], query_places, packed[3], packed[4]
        ),
        (query_seqs, all_pairs, lengths, log_total, grad_mixture),
    )
    pair_part = pick(grad_pairs, place, group_len, 1)
    ctx = lax.axis_size("ctx")
    for other in range(1, ctx):
        sent = pick(grad_pairs, lax.rem(place + other, ctx), group_len, 1).astype(low)
        pair_part = pair_part + lax.ppermute(
            sent, "ctx", [(i, (i + other) % ctx) for i in range(ctx)]
        ).astype(wide)
    pair_share = line_reduce(pair_part.astype(low).reshape(tp, share, 2 * HD)).astype(low)
    grad_key_values = line_gather(pair_share)
    grad_queries = grad_query.reshape(token_count, local_heads * HD).astype(low)
    query_grad = reduce_blocks(
        [
            jnp.einsum("td,tq->dq", turned(input_one, r), grad_queries, preferred_element_type=wide)
            for r in range(fsdp)
        ]
    )
    pair_grad = reduce_blocks(
        [
            jnp.einsum(
                "td,tk->dk", turned(input_one, r), grad_key_values, preferred_element_type=wide
            )
            for r in range(fsdp)
        ]
    )
    grad_one_part = jnp.einsum(
        "tq,dq->td", grad_queries, query_full, preferred_element_type=wide
    ).astype(low)
    grad_normed_one = line_reduce(grad_one_part.reshape(tp, share, model_width)) + jnp.einsum(
        "tk,dk->td", pair_share, pair_full, preferred_element_type=wide
    )
    unit_share = pick(unit_one, zone, share, 0)
    scaled_share = pick(scaled_one, zone, share, 0)
    stream_grad = grad_middle + norm_backward(grad_normed_one, unit_share, scaled_share, gain_one)
    stream_grad = line_gather(stream_grad.astype(low))

    feed_branch = line_reduce(feed_part.reshape(tp, share, model_width)) + down_add
    total = middle + feed_branch
    result = line_gather((total * keep_share).astype(low))

    shared = jnp.concatenate(
        [
            jnp.sum(grad_normed_two * unit_two, 0),
            jnp.sum(grad_normed_two, 0),
            jnp.sum(grad_branch_share.astype(wide), 0),
            jnp.sum(pick(grad_feed, zone, share, 0).astype(wide), 0),
            jnp.stack(
                [
                    jnp.sum(keep_share * total * total),
                    jnp.sum(keep_share * branch * branch),
                    jnp.sum(keep_share * feed_branch * feed_branch),
                    jnp.sum(keep_share),
                ]
            ),
        ]
    )
    shared = sum_over(shared, ("tp", "fsdp", "ctx"))
    late = jnp.concatenate(
        [
            jnp.sum(grad_normed_one * unit_share, 0),
            jnp.sum(grad_normed_one, 0),
            jnp.sum(pair_share[:, HD:].astype(wide), 0),
        ]
    )
    late = sum_over(late, ("tp", "fsdp", "ctx"))
    own = jnp.concatenate(
        [jnp.sum(grad_pre.astype(wide), 0), jnp.sum(grad_queries.astype(wide), 0)]
    )
    own = sum_over(own, ("fsdp", "ctx"))
    up_bias_all = own[: up_add.shape[0]].reshape(up_bias.shape[0], fsdp, -1)
    query_bias_all = own[up_add.shape[0] :].reshape(query_bias.shape[0], fsdp, -1)
    width = model_width

    def mine(row, size):
        return pick(row, me, size, 0)

    totals = shared[4 * width :]
    root_means = jnp.sqrt(totals[:3] / (totals[3] * width))
    return (
        result.reshape(stream.shape),
        stream_grad.reshape(stream.shape),
        mine(late[:width], piece),
        mine(late[width : 2 * width], piece),
        query_grad,
        lax.dynamic_index_in_dim(query_bias_all, me, 1, False),
        pair_grad,
        mine(late[2 * width :], value_bias.shape[0]),
        output_grad,
        mine(shared[2 * width : 3 * width], piece),
        mine(shared[:width], piece),
        mine(shared[width : 2 * width], piece),
        up_grad,
        lax.dynamic_index_in_dim(up_bias_all, me, 1, False),
        down_grad,
        mine(shared[3 * width : 4 * width], piece),
        root_means,
    )


def solution(mesh):
    in_specs = (
        P("fsdp", "ctx", None),
        P("fsdp", "ctx", None),
        P("fsdp"),
        P("fsdp"),
        P("fsdp"),
        P("fsdp", "tp"),
        P("tp", "fsdp"),
        P("fsdp", None),
        P("fsdp"),
        P("tp", "fsdp"),
        P("fsdp"),
        P("fsdp"),
        P("fsdp"),
        P("fsdp", "tp"),
        P("tp", "fsdp"),
        P("tp", "fsdp"),
        P("fsdp"),
    )
    out_specs = (
        P("fsdp", "ctx", None),
        P("fsdp", "ctx", None),
        P("fsdp"),
        P("fsdp"),
        P("fsdp", "tp"),
        P("tp", "fsdp"),
        P("fsdp", None),
        P("fsdp"),
        P("tp", "fsdp"),
        P("fsdp"),
        P("fsdp"),
        P("fsdp"),
        P("fsdp", "tp"),
        P("tp", "fsdp"),
        P("tp", "fsdp"),
        P("fsdp"),
        P(),
    )
    return jax.shard_map(body, mesh=mesh, in_specs=in_specs, out_specs=out_specs, check_vma=False)
```

```python
import functools
import math
import types

import jax
import jax.numpy as jnp
from jax import lax
from jax.experimental import pallas as pl
from jax.experimental.pallas import tpu as pltpu
from jax.sharding import PartitionSpec as P

HD = 128
EPSILON = 1e-05
NEGATIVE = -1e30
FSDP, CTX, TP = "fsdp", "ctx", "tp"
LOW, WIDE = jnp.bfloat16, jnp.float32
MESH = pl.DeviceIdType.MESH
VMEM_BYTES = 60 << 20


def flip(place, bit):
    return place + bit - 2 * bit * lax.rem(lax.div(place, bit), 2)


def bits_of(axis):
    count, bit, found = lax.axis_size(axis), 1, []
    while bit < count:
        found.append(bit)
        bit *= 2
    return found


def mm(left, right):
    return jnp.dot(left, right, preferred_element_type=WIDE)


def mm_nt(left, right):
    return lax.dot_general(left, right, (((1,), (1,)), ((), ())), preferred_element_type=WIDE)


def mm_tn(left, right):
    return lax.dot_general(left, right, (((0,), (0,)), ((), ())), preferred_element_type=WIDE)


def tiles(count, step):
    def run(work):
        def once(index, carry):
            work(pl.multiple_of(index * step, step))
            return carry

        lax.fori_loop(0, count // step, once, 0)

    return run


def norm_of(values):
    center = values - jnp.mean(values, -1, keepdims=True)
    scaled = lax.rsqrt(jnp.mean(center * center, -1, keepdims=True) + EPSILON)
    return center * scaled, scaled


def norm_backward(upstream, unit_rows, scaled, norm_gain):
    gained = upstream * norm_gain
    return scaled * (
        gained
        - jnp.mean(gained, -1, keepdims=True)
        - unit_rows * jnp.mean(gained * unit_rows, -1, keepdims=True)
    )


def send(source, target, outgo, income, axis, place):
    return pltpu.make_async_remote_copy(
        src_ref=source,
        dst_ref=target,
        send_sem=outgo,
        recv_sem=income,
        device_id={axis: place},
        device_id_type=MESH,
    )


def all_peers():
    me, place, zone = lax.axis_index(FSDP), lax.axis_index(CTX), lax.axis_index(TP)
    ctx, tp = lax.axis_size(CTX), lax.axis_size(TP)
    peers = [(FSDP, flip(me, 1)), (FSDP, flip(me, 2)), (FSDP, flip(flip(me, 1), 2))]
    peers += [(CTX, lax.rem(place + k, ctx)) for k in range(1, ctx)]
    peers += [(TP, lax.rem(zone + k, tp)) for k in range(1, tp)]
    return peers


def greet(peers):
    barrier = pltpu.get_barrier_semaphore()
    for axis, place in peers:
        pl.semaphore_signal(barrier, inc=1, device_id={axis: place}, device_id_type=MESH)
    return lambda: pl.semaphore_wait(barrier, len(peers))


def split_rows(tokens):
    rows = 32 if tokens % 512 == 0 else 16
    return rows, tokens // 2 // rows


class Line:
    def __init__(self, tokens):
        self.place, self.count = lax.axis_index(TP), lax.axis_size(TP)
        self.rows, self.chunks = split_rows(tokens)
        self.half = tokens // 2

    def at(self, half, k):
        start = half * self.half + k * self.rows
        return pl.ds(start if isinstance(start, int) else pl.multiple_of(start, self.rows), self.rows)

    def is_home(self, half):
        return self.place == (0 if half == 0 else self.count - 1)

    def is_far(self, half):
        return self.place == (self.count - 1 if half == 0 else 0)

    def toward(self, half):
        move = self.count - 1 if half == 0 else 1
        return lax.rem(self.place + move, self.count)

    def away(self, half):
        return self.toward(1 - half)


class LineSum(Line):
    def __init__(self, own, slots, sems):
        super().__init__(own.shape[0])
        self.own, self.slots = own, slots
        self.outgo, self.income = sems

    def copy(self, half, k):
        rows = self.at(half, k)
        return send(
            self.own.at[rows],
            self.slots.at[rows],
            self.outgo.at[half, k],
            self.income.at[half, k],
            TP,
            self.toward(half),
        )

    def launch(self, half, first=0, last=None):
        @pl.when(self.is_far(half))
        def _():
            for k in range(first, self.chunks if last is None else last):
                self.copy(half, k).start()

    def total(self, half, k):
        rows = self.at(half, k)
        return self.own[rows, :].astype(WIDE) + self.slots[rows, :].astype(WIDE)

    def pass_on(self, half, k):
        self.copy(half, k).wait_recv()
        self.own[self.at(half, k), :] = self.total(half, k).astype(LOW)
        self.copy(half, k).start()

    def drain(self):
        for half in range(2):

            @pl.when(jnp.logical_not(self.is_home(half)))
            def _():
                for k in range(self.chunks):
                    self.copy(half, k).wait_send()


class LineSpread(Line):
    def __init__(self, held, sems):
        super().__init__(held.shape[0])
        self.held = held
        self.outgo, self.income = sems

    def copy(self, half, k, source=None):
        rows = self.at(half, k)
        return send(
            self.held.at[rows] if source is None else source.at[rows],
            self.held.at[rows],
            self.outgo.at[half, k],
            self.income.at[half, k],
            TP,
            self.away(half),
        )

    def begin(self, half, k, source=None):
        self.copy(half, k, source).start()

    def serve(self, half, k):
        self.copy(half, k).wait_recv()

        @pl.when(jnp.logical_not(self.is_far(half)))
        def _():
            self.copy(half, k).start()

    def drain(self):
        for half in range(2):

            @pl.when(jnp.logical_not(self.is_far(half)))
            def _():
                for k in range(self.chunks):
                    self.copy(half, k).wait_send()


class Flow(Line):
    def __init__(self, line_sum, spread, home, lag):
        super().__init__(line_sum.own.shape[0])
        self.sum, self.spread, self.home, self.lag = line_sum, spread, home, lag
        self.now = 0
        self.steps = self.chunks + lag + 2 * (self.count - 1) - 1

    def launch(self, first=0, last=None):
        for half in range(2):
            self.sum.launch(half, first, last)

    def inside(self, k):
        return (k >= 0) & (k < self.chunks)

    def advance(self, count=1):
        for n in range(self.now, min(self.now + count, self.steps)):
            self.step(n)
        self.now = min(self.now + count, self.steps)

    def step(self, n):
        last = self.count - 1
        at_home = n - (last - 1)
        for half in range(2):
            hops = last - self.place if half == 0 else self.place
            k = n - (hops - 1)

            @pl.when((hops >= 1) & (hops < last) & self.inside(k))
            def _():
                self.sum.pass_on(half, k)

            if 0 <= at_home < self.chunks:

                @pl.when(self.is_home(half))
                def _():
                    self.sum.copy(half, at_home).wait_recv()
                    self.home(half, at_home)

        for half in range(2):
            hops = self.place if half == 0 else last - self.place
            k = at_home - self.lag - (hops - 1)

            @pl.when((hops >= 1) & self.inside(k))
            def _():
                self.spread.serve(half, k)

    def ready(self, chunk):
        return chunk + self.lag + 2 * (self.count - 1) - 2


class Gather:
    def __init__(self, shard, held, sems, cut):
        self.shard, self.held = shard, held
        self.me, self.place = lax.axis_index(FSDP), lax.axis_index(CTX)
        self.ctx = lax.axis_size(CTX)
        self.cut = cut
        self.rows = shard.shape[0] // self.ctx // cut
        self.near_sem, self.far_sem, self.side_sem, self.pass_sem, self.local = sems

    def part(self, place, k):
        return pl.ds(pl.multiple_of((place * self.cut + k) * self.rows, self.rows), self.rows)

    def keep(self):
        every = pl.ds(0, self.shard.shape[0])
        return pltpu.make_async_copy(self.shard, self.held(self.me, every), self.local.at[0])

    def near(self):
        every = pl.ds(0, self.shard.shape[0])
        return send(
            self.shard,
            self.held(self.me, every),
            self.near_sem.at[0],
            self.near_sem.at[1],
            FSDP,
            flip(self.me, 1),
        )

    def far(self, k):
        part = self.part(self.place, k)
        return send(
            self.shard.at[part],
            self.held(self.me, part),
            self.far_sem.at[0, k],
            self.far_sem.at[1, k],
            FSDP,
            flip(self.me, 2),
        )

    def side(self, other, k):
        held = self.held(flip(self.me, 2), self.part(self.place, k))
        return send(
            held,
            held,
            self.side_sem.at[0, other - 1, k],
            self.side_sem.at[1, other - 1, k],
            CTX,
            lax.rem(self.place + other, self.ctx),
        )

    def over(self, other, k):
        place = lax.rem(self.place + self.ctx - other, self.ctx)
        held = self.held(flip(self.me, 2), self.part(place, k))
        return send(
            held,
            held,
            self.pass_sem.at[0, other, k],
            self.pass_sem.at[1, other, k],
            FSDP,
            flip(self.me, 1),
        )

    def start(self):
        for k in range(self.cut):
            self.far(k).start()
        self.near().start()
        self.keep().start()

    def cross(self, k):
        self.far(k).wait_recv()
        for other in range(1, self.ctx):
            self.side(other, k).start()
        self.over(0, k).start()

    def pass_on(self, k):
        for other in range(1, self.ctx):
            self.side(other, k).wait_recv()
            self.over(other, k).start()

    def ready(self):
        self.keep().wait()
        self.near().wait_recv()
        for k in range(self.cut):
            for other in range(self.ctx):
                self.over(other, k).wait_recv()

    def drain(self):
        self.near().wait_send()
        for k in range(self.cut):
            self.far(k).wait_send()
            for other in range(self.ctx):
                self.over(other, k).wait_send()
                if other > 0:
                    self.side(other, k).wait_send()

    @staticmethod
    def sems(cut):
        ctx = lax.axis_size(CTX)
        shapes = ((2,), (2, cut), (2, ctx - 1, cut), (2, ctx, cut), (1,))
        return tuple(pltpu.SemaphoreType.DMA(shape) for shape in shapes)


class PieceSum:
    def __init__(self, piece, near, far, last, stages, sems, chunks):
        self.piece, self.near, self.far, self.last = piece, near, far, last
        self.stages, self.chunks = stages, chunks
        self.rows = far.shape[0] // chunks
        self.near_sem, self.far_sem, self.last_sem, self.local = sems
        self.me, self.place = lax.axis_index(FSDP), lax.axis_index(CTX)
        self.ctx = lax.axis_size(CTX)

    def part(self, k):
        return pl.ds(k * self.rows, self.rows)

    def near_copy(self, which, k):
        return send(
            self.piece(2 * which + 1, k),
            self.near.at[which, self.part(k)],
            self.near_sem.at[0, which, k],
            self.near_sem.at[1, which, k],
            FSDP,
            flip(self.me, 1),
        )

    def far_copy(self, k):
        return send(
            self.piece(2, k),
            self.far.at[self.part(k)],
            self.far_sem.at[0, k],
            self.far_sem.at[1, k],
            FSDP,
            flip(self.me, 2),
        )

    def last_copy(self, other, k):
        return send(
            self.piece(0, k),
            self.last.at[self.place, self.part(k)],
            self.last_sem.at[0, other - 1, k],
            self.last_sem.at[1, other - 1, k],
            CTX,
            lax.rem(self.place + other, self.ctx),
        )

    def own_copy(self, k):
        return pltpu.make_async_copy(
            self.piece(0, k), self.last.at[self.place, self.part(k)], self.local.at[2 + k]
        )

    def start(self, which):
        for k in range(self.chunks):
            self.near_copy(which, k).start()

    def load(self, source, index):
        copy = pltpu.make_async_copy(source, self.stages[index], self.local.at[index])
        copy.start()
        return copy

    def add(self, r, k, index):
        step = 32 if self.rows % 32 == 0 else 16
        piece, stage = self.piece(r, k), self.stages[index]

        @tiles(self.rows, step)
        def _(at):
            here = pl.ds(at, step)
            total = piece[here].astype(WIDE) + stage[here].astype(WIDE)
            piece[here] = total.astype(LOW)

    def first(self, k):
        for which in range(2):
            self.near_copy(which, k).wait_recv()
        copies = [self.load(self.near.at[which, self.part(k)], which) for which in range(2)]
        copies[1].wait()
        self.add(2, k, 1)
        self.far_copy(k).start()
        copies[0].wait()
        self.add(0, k, 0)

    def second(self, k):
        self.far_copy(k).wait_recv()
        self.load(self.far.at[self.part(k)], 0).wait()
        self.add(0, k, 0)
        for other in range(1, self.ctx):
            self.last_copy(other, k).start()
        self.own_copy(k).start()

    def finish(self):
        for k in range(self.chunks):
            for other in range(1, self.ctx):
                self.last_copy(other, k).wait_recv()
                self.last_copy(other, k).wait_send()
            self.own_copy(k).wait()
            self.far_copy(k).wait_send()
            for which in range(2):
                self.near_copy(which, k).wait_send()

    @staticmethod
    def sems(chunks):
        ctx = lax.axis_size(CTX)
        shapes = ((2, 2, chunks), (2, chunks), (2, ctx - 1, chunks), (2 + chunks,))
        return tuple(pltpu.SemaphoreType.DMA(shape) for shape in shapes)


class RowSum:
    def __init__(self, rows, came, sems, axes):
        self.rows, self.came, self.sems = rows, came, sems
        self.hops = [(axis, bit) for axis in axes for bit in bits_of(axis)]

    def copy(self, n):
        axis, bit = self.hops[n]
        return send(
            self.rows,
            self.came.at[n],
            self.sems.at[0, n],
            self.sems.at[1, n],
            axis,
            flip(lax.axis_index(axis), bit),
        )

    def start(self, n):
        if n < len(self.hops):
            self.copy(n).start()

    def move(self, n):
        if n < len(self.hops):
            self.copy(n).wait()
            self.rows[...] += self.came[n]
            self.start(n + 1)


def line_sems(tokens):
    rows, chunks = split_rows(tokens)
    return tuple(pltpu.SemaphoreType.DMA((2, chunks)) for _ in range(2))


def call_kernel(body, ident, far, near, scalars, far_outs, near_outs, scratch):
    groups = (far, near, scalars)
    spaces = (pl.ANY, pltpu.VMEM, pltpu.SMEM)
    arrays, in_specs = [], []
    for group, space in zip(groups, spaces):
        arrays += list(group.values())
        in_specs += [pl.BlockSpec(memory_space=space)] * len(group)
    outs = dict(far_outs, **near_outs)
    out_specs = [pl.BlockSpec(memory_space=pl.ANY)] * len(far_outs)
    out_specs += [pl.BlockSpec(memory_space=pltpu.VMEM)] * len(near_outs)
    shapes, tree = jax.tree.flatten(scratch)
    ins = [name for group in groups for name in group]

    def kernel(*refs):
        held = dict(zip(ins + list(outs), refs))
        held.update(jax.tree.unflatten(tree, refs[len(ins) + len(outs) :]))
        body(types.SimpleNamespace(**held))

    given = pl.pallas_call(
        kernel,
        out_shape=[jax.ShapeDtypeStruct(shape, kind) for shape, kind in outs.values()],
        in_specs=in_specs,
        out_specs=out_specs,
        scratch_shapes=shapes,
        compiler_params=pltpu.CompilerParams(
            collective_id=ident, has_side_effects=True, vmem_limit_bytes=VMEM_BYTES
        ),
    )(*arrays)
    return dict(zip(outs, given))


def front_body(r):
    me, place, zone = lax.axis_index(FSDP), lax.axis_index(CTX), lax.axis_index(TP)
    fsdp, ctx, tp = lax.axis_size(FSDP), lax.axis_size(CTX), lax.axis_size(TP)
    tokens, width = r.stream_hbm.shape
    columns = width // fsdp
    query_width = r.query.shape[1]
    heads = query_width // HD
    inner = r.up_shard.shape[1]
    length = r.lengths[0]
    line = Line(tokens)
    step_rows, chunks = line.rows, line.chunks

    ready = greet(all_peers())
    stream_load = pltpu.make_async_copy(r.stream_hbm, r.stream, r.load_sem.at[0])
    stream_load.start()

    def block_rows(held):
        size = held.shape[0] // fsdp

        def view(block, rows):
            start = pl.multiple_of(block * size + rows.start, 16)
            return held.at[pl.ds(start, rows.size)]

        return view

    gathers = types.SimpleNamespace(
        query=Gather(r.query_shard, block_rows(r.query), r.query_sems, 1),
        pair=Gather(r.pair_shard, block_rows(r.pair), r.pair_sems, 1),
        output=Gather(r.output_shard, lambda b, rows: r.output.at[b, rows], r.output_sems, 1),
        up=Gather(r.up_shard, block_rows(r.up_all), r.up_sems, r.up_sems[1].shape[1]),
        down=Gather(
            r.down_shard, lambda b, rows: r.down_all.at[b, rows], r.down_sems, r.down_sems[1].shape[1]
        ),
    )

    def small_copy(k):
        target = flip(me, k) if k < 3 else flip(flip(me, 1), 2)
        return send(
            r.smalls.at[0], r.smalls.at[k], r.small_sem.at[0, k - 1], r.small_sem.at[1, k - 1],
            FSDP, target,
        )

    r.smalls[0] = r.packed[...]
    ready()
    for k in range(1, fsdp):
        small_copy(k).start()
    gathers.pair.start()
    gathers.query.start()
    for k in range(1, fsdp):
        small_copy(k).wait()
    query_add = jnp.zeros((1, query_width), WIDE)
    value_add = jnp.zeros((1, HD), WIDE)
    for k in range(fsdp):
        block = me if k == 0 else flip(me, k) if k < 3 else flip(flip(me, 1), 2)
        at = pl.ds(pl.multiple_of(block * columns, columns), columns)
        r.vectors[pl.ds(0, 6), at] = r.smalls[k, pl.ds(0, 6), :]
        query_add += r.smalls[k, pl.ds(6, 1), pl.ds(0, query_width)]
        value_add += r.smalls[k, pl.ds(7, 1), pl.ds(0, HD)]
    for q in range(inner // columns):
        total = jnp.zeros((1, columns), WIDE)
        for k in range(fsdp):
            total += r.smalls[k, pl.ds(8 + q, 1), :]
        r.vectors[pl.ds(6, 1), pl.ds(q * columns, columns)] = total
    r.vectors[pl.ds(7, 1), :] = jnp.zeros((1, r.vectors.shape[1]), WIDE)

    def vector(n):
        return r.vectors[pl.ds(n, 1), pl.ds(0, width)]

    stream_load.wait()
    norm_step = min(32, tokens)

    @tiles(tokens, norm_step)
    def _(row):
        rows = pl.ds(row, norm_step)
        unit, scaled = norm_of(r.stream[rows, :].astype(WIDE))
        r.input_one[rows, :] = (unit * vector(0) + vector(1)).astype(LOW)

    early = (gathers.pair, gathers.query)
    for one in early:
        one.cross(0)
    for one in early:
        one.pass_on(0)
    for one in (gathers.output, gathers.up, gathers.down):
        one.start()
    gathers.pair.ready()
    own_rows = pl.ds(pl.multiple_of(place * tokens, tokens), tokens)
    key_half = mm(r.input_one[...], r.pair[...])
    r.pairs[own_rows, pl.ds(0, HD)] = key_half[:, :HD].astype(LOW)
    r.pairs[own_rows, pl.ds(HD, HD)] = (key_half[:, HD:] + value_add).astype(LOW)

    def pair_copy(other):
        return send(
            r.pairs.at[own_rows],
            r.pairs.at[own_rows],
            r.exchange_sem.at[0, other - 1],
            r.exchange_sem.at[1, other - 1],
            CTX,
            lax.rem(place + other, ctx),
        )

    for other in range(1, ctx):
        pair_copy(other).start()
    gathers.query.ready()
    r.queries[...] = (mm(r.input_one[...], r.query[...]) + query_add).astype(LOW)
    gathers.output.cross(0)
    for other in range(1, ctx):
        pair_copy(other).wait_recv()
    gathers.output.pass_on(0)

    share = 4 * step_rows
    factor = 1.0 / math.sqrt(HD)

    def attend(start):
        rows = pl.ds(start, share)
        keys = r.pairs[:, pl.ds(0, HD)]
        values = r.pairs[:, pl.ds(HD, HD)]
        shape = (share, keys.shape[0])
        query_at = place * tokens + start + lax.broadcasted_iota(jnp.int32, shape, 0)
        key_at = lax.broadcasted_iota(jnp.int32, shape, 1)
        allowed = (key_at <= query_at) & (key_at < length)
        for head in range(heads):
            at = pl.ds(head * HD, HD)
            scores = jnp.where(allowed, mm_nt(r.queries[rows, at], keys) * factor, NEGATIVE)
            peak = jnp.max(scores, -1, keepdims=True)
            soft = jnp.exp(scores - peak)
            total = jnp.sum(soft, -1, keepdims=True)
            r.mixture[rows, at] = mm((soft / total).astype(LOW), values).astype(LOW)
            r.log_total[rows, pl.ds(head, 1)] = peak + jnp.log(total)

    def project(start):
        rows = pl.ds(start, share)
        for block in range(fsdp):
            at = pl.ds(block * columns, columns)
            r.sum_own[rows, at] = mm(r.mixture[rows, :], r.output[block]).astype(LOW)

    branch_sum = LineSum(r.sum_own, r.sum_slots, r.sum_sems)
    spread = LineSpread(r.input_two, r.spread_sems)
    r.squares[...] = jnp.zeros_like(r.squares)

    def home(half, k):
        branch = branch_sum.total(half, k) + vector(2)
        middle = r.stream[line.at(half, k), :].astype(WIDE) + branch
        r.middle[pl.ds(k * step_rows, step_rows), :] = middle
        unit, scaled = norm_of(middle)
        r.input_two[line.at(half, k), :] = (unit * vector(3) + vector(4)).astype(LOW)
        spread.begin(half, k)
        slot = place * tokens + half * line.half + k * step_rows
        slots = slot + lax.broadcasted_iota(jnp.int32, (step_rows, width), 0)
        keep = jnp.where(slots < length, 1.0, 0.0)
        r.squares[...] += jnp.sum(keep * branch * branch, 0, keepdims=True)

    big = [(gathers.up, k) for k in range(gathers.up.cut)]
    big += [(gathers.down, k) for k in range(gathers.down.cut)]
    events = []
    for index, (one, k) in enumerate(big):
        events.append(functools.partial(one.cross, k))
        if index > 0:
            before, last = big[index - 1]
            events.append(functools.partial(before.pass_on, last))
    events.append(functools.partial(big[-1][0].pass_on, big[-1][1]))

    def move_on(count):
        for event in events[:count]:
            event()
        del events[:count]

    flow = Flow(branch_sum, spread, home, 1)
    groups = line.half // share
    for group in range(groups):
        for half in range(2):
            start = half * line.half + group * share
            attend(start)
            if group == 0 and half == 0:
                gathers.output.ready()
            project(start)
        flow.launch(4 * group, 4 * group + 4)
        if group < groups - 1:
            flow.advance(1)
            move_on(1)
    while flow.now < flow.steps:
        flow.advance(1)
        move_on(1)
    move_on(len(events))
    keeps = [
        pltpu.make_async_copy(source, target, r.load_sem.at[1 + n])
        for n, (source, target) in enumerate(
            ((r.query, r.query_all), (r.pair, r.pair_all), (r.output, r.output_all))
        )
    ]
    for copy in keeps:
        copy.start()
    for one in (gathers.up, gathers.down):
        one.ready()
    for copy in keeps:
        copy.wait()
    for other in range(1, ctx):
        pair_copy(other).wait_send()
    for one in vars(gathers).values():
        one.drain()
    branch_sum.drain()
    spread.drain()


def front(values, tokens):
    fsdp, ctx = lax.axis_size(FSDP), lax.axis_size(CTX)
    stream = values.stream
    width = stream.shape[1]
    columns = width // fsdp
    inner = values.up.shape[1]
    query_width = values.query.shape[1]
    pair_width = 2 * HD
    dma = pltpu.SemaphoreType.DMA
    wide_row = max(width, inner)
    return call_kernel(
        front_body,
        1,
        dict(stream_hbm=stream),
        dict(
            packed=values.packed,
            query_shard=values.query,
            pair_shard=values.pair,
            output_shard=values.output,
            up_shard=values.up,
            down_shard=values.down,
        ),
        dict(lengths=values.lengths),
        dict(
            up_all=((width, inner), LOW),
            down_all=((fsdp, inner, columns), LOW),
            query_all=((width, query_width), LOW),
            pair_all=((width, pair_width), LOW),
            output_all=((fsdp, query_width, columns), LOW),
        ),
        dict(
            vectors=((8, wide_row), WIDE),
            input_one=((tokens, width), LOW),
            input_two=((tokens, width), LOW),
            queries=((tokens, query_width), LOW),
            pairs=((tokens * ctx, pair_width), LOW),
            mixture=((tokens, query_width), LOW),
            log_total=((tokens, query_width // HD), WIDE),
            middle=((tokens // 2, width), WIDE),
            squares=((1, width), WIDE),
        ),
        dict(
            stream=pltpu.VMEM((tokens, width), LOW),
            smalls=pltpu.VMEM((fsdp,) + values.packed.shape, WIDE),
            query=pltpu.VMEM((width, query_width), LOW),
            pair=pltpu.VMEM((width, pair_width), LOW),
            output=pltpu.VMEM((fsdp, query_width, columns), LOW),
            sum_own=pltpu.VMEM((tokens, width), LOW),
            sum_slots=pltpu.VMEM((tokens, width), LOW),
            sum_sems=line_sems(tokens),
            spread_sems=line_sems(tokens),
            query_sems=Gather.sems(1),
            pair_sems=Gather.sems(1),
            output_sems=Gather.sems(1),
            up_sems=Gather.sems(2),
            down_sems=Gather.sems(2),
            load_sem=dma((4,)),
            small_sem=dma((2, fsdp - 1)),
            exchange_sem=dma((2, ctx - 1)),
        ),
    )


def back_body(r):
    me, place, zone = lax.axis_index(FSDP), lax.axis_index(CTX), lax.axis_index(TP)
    fsdp, ctx, tp = lax.axis_size(FSDP), lax.axis_size(CTX), lax.axis_size(TP)
    tokens, width = r.input_two_hbm.shape
    inner = r.up_hbm.shape[1]
    columns = width // fsdp
    share = tokens // tp
    query_width = r.queries_hbm.shape[1]
    heads = query_width // HD
    length = r.lengths[0]
    line = Line(tokens)
    step_rows, chunks = line.rows, line.chunks
    step = columns
    blocks = inner // step

    ready = greet(all_peers())

    def up_load(q):
        at = pl.ds(q, step)
        return pltpu.make_async_copy(r.up_hbm.at[:, at], r.up.at[:, at], r.weight_sem.at[0, q // step])

    def down_load(q):
        at = pl.ds(q, step)
        return pltpu.make_async_copy(
            r.down_hbm.at[:, at], r.down.at[:, at], r.weight_sem.at[1, q // step]
        )

    at_end = jnp.where(zone == tp - 1, tokens // 2, 0)
    pairs_of = dict(
        input_two=(r.input_two_hbm, r.input_two),
        cotangent=(r.cotangent_hbm, r.grad_feed),
        output=(r.output_hbm, r.output),
        queries=(r.queries_hbm, r.queries),
        pairs=(r.pairs_hbm, r.pairs),
        mixture=(r.mixture_hbm, r.mixture),
        query=(r.query_hbm, r.query),
        pair=(r.pair_hbm, r.pair),
        middle=(r.middle_hbm, r.middle),
        stream=(r.stream_hbm.at[pl.ds(pl.multiple_of(at_end, tokens // 2), tokens // 2)], r.stream),
    )
    loads = {}
    for index, (name, (source, target)) in enumerate(pairs_of.items()):
        loads[name] = pltpu.make_async_copy(source, target, r.load_sem.at[index])
    loads = types.SimpleNamespace(**loads)
    loads.input_two.start()
    loads.cotangent.start()
    for q in range(blocks):
        up_load(q * step).start()
        down_load(q * step).start()
    for name, copy in vars(loads).items():
        if copy is not loads.input_two and copy is not loads.cotangent:
            copy.start()
    r.rows[...] = jnp.zeros_like(r.rows)
    loads.cotangent.wait()

    @tiles(tokens, step_rows)
    def _(row):
        rows = pl.ds(row, step_rows)
        slots = place * tokens + row + lax.broadcasted_iota(jnp.int32, (step_rows, width), 0)
        keep = jnp.where(slots < length, 1.0, 0.0)
        r.grad_feed[rows, :] = (keep * r.grad_feed[rows, :].astype(WIDE)).astype(LOW)

    loads.input_two.wait()

    def vector(n):
        return r.vectors[pl.ds(n, 1), pl.ds(0, width)]

    def note(row, values):
        r.rows[pl.ds(row, 1), pl.ds(0, width)] += jnp.sum(values, 0, keepdims=True)

    @tiles(inner, step)
    def _(q):
        up_load(q).wait()
        down_load(q).wait()
        at = pl.ds(q, step)
        r.work_one[...] = mm(r.input_two[...], r.up[:, at])
        total = mm_nt(r.grad_feed[:, pl.ds(0, columns)], r.down[0, at, :])
        for block in range(1, fsdp):
            total += mm_nt(r.grad_feed[:, pl.ds(block * columns, columns)], r.down[block, at, :])
        r.work_two[...] = total
        bias = r.vectors[pl.ds(6, 1), at]

        @tiles(tokens, 32)
        def _(row):
            here = pl.ds(row, 32)
            v = r.work_one[here, :] + bias
            square = v * v
            reach = math.sqrt(2.0 / math.pi)
            t = jnp.tanh(reach * v * (1.0 + 0.044715 * square))
            gate = 0.5 * (1.0 + t)
            slope = gate + 0.5 * v * (1.0 - t * t) * reach * (1.0 + 3 * 0.044715 * square)
            r.hidden[here, at] = (v * gate).astype(LOW)
            grad = (r.work_two[here, :] * slope).astype(LOW)
            r.grad_pre[here, at] = grad
            r.rows[pl.ds(9, 1), at] += jnp.sum(grad.astype(WIDE), 0, keepdims=True)

    ready()
    sum_two = LineSum(r.sum_own, r.sum_slots, r.two_sems)
    sum_feed = LineSum(r.feed_own, r.feed_slots, r.feed_sems)
    sum_one = LineSum(r.sum_own, r.sum_slots, r.one_sems)
    spread_branch = LineSpread(r.grad_branch, r.branch_sems)
    spread_result = LineSpread(r.result, r.result_sems)
    spread_stream = LineSpread(r.stream_grad, r.stream_sems)

    @tiles(width, step)
    def _(col):
        at = pl.ds(col, step)
        r.sum_own[:, at] = mm_nt(r.grad_pre[...], r.up[at, :]).astype(LOW)

    for half in range(2):
        sum_two.launch(half)

    def turn(n):
        target = me
        for bit in (1, 2):
            if n & bit:
                target = flip(target, bit)
        return pl.ds(pl.multiple_of(target * columns, columns), columns)

    up_chunks, down_chunks = r.up_sems[1].shape[1], r.down_sems[1].shape[1]
    up_rows, down_rows = columns // up_chunks, inner // down_chunks

    def whole_piece(held, kept, size):
        if held is not None:
            return lambda n, k: held.at[n]
        return lambda n, k: kept.at[:, pl.ds(n * size, size)]

    def stage_part(rows, size):
        return [r.stage_down.at[n, pl.ds(0, rows), pl.ds(0, size)] for n in range(2)]

    sums = types.SimpleNamespace(
        up=PieceSum(
            lambda n, k: r.up.at[pl.ds(n * columns + k * up_rows, up_rows)],
            r.up_near,
            r.up_far,
            r.up_last,
            [r.stage_up.at[n] for n in range(2)],
            r.up_sems,
            up_chunks,
        ),
        down=PieceSum(
            lambda n, k: r.down.at[n, pl.ds(k * down_rows, down_rows)],
            r.down_near,
            r.down_far,
            r.down_last,
            [r.stage_down.at[n] for n in range(2)],
            r.down_sems,
            down_chunks,
        ),
        output=PieceSum(
            whole_piece(getattr(r, "output_piece", None), r.grad_pre, columns),
            r.output_near,
            r.output_far,
            r.output_last,
            stage_part(query_width, columns),
            r.output_sems,
            1,
        ),
        query=PieceSum(
            whole_piece(getattr(r, "query_piece", None), r.hidden, query_width),
            r.query_near,
            r.query_far,
            r.query_last,
            stage_part(columns, query_width),
            r.query_sems,
            1,
        ),
        pair=PieceSum(
            lambda n, k: r.pair_piece.at[n],
            r.pair_near,
            r.pair_far,
            r.pair_last,
            stage_part(columns, 2 * HD),
            r.pair_sems,
            1,
        ),
    )

    def up_terms(n):
        left = r.input_two[:, turn(n)]

        @tiles(inner, step)
        def _(q):
            part = mm_tn(left, r.grad_pre[:, pl.ds(q, step)])
            r.up[pl.ds(n * columns, columns), pl.ds(q, step)] = part.astype(LOW)

    def down_terms(n):
        right = r.grad_feed[:, turn(n)]

        @tiles(inner, step)
        def _(q):
            r.down[n, pl.ds(q, step), :] = mm_tn(r.hidden[:, pl.ds(q, step)], right).astype(LOW)

    def feed_terms(block):
        at = pl.ds(block * columns, columns)
        r.feed_own[:, at] = mm(r.hidden[...], r.down[block]).astype(LOW)

    def home_two(half, k):
        rows = line.at(half, k)
        unit, scaled = norm_of(r.middle[pl.ds(k * step_rows, step_rows), :])
        upstream = sum_two.total(half, k)
        note(0, upstream * unit)
        note(1, upstream)
        own = r.grad_feed[rows, :].astype(WIDE)
        note(3, own)
        grad = own + norm_backward(upstream, unit, scaled, vector(3))
        r.grad_middle[pl.ds(k * step_rows, step_rows), :] = grad
        rounded = grad.astype(LOW)
        note(2, rounded.astype(WIDE))
        r.grad_branch[rows, :] = rounded
        spread_branch.begin(half, k)

    tasks, late = [], []

    def first(one, k):
        one.first(k)
        late.append((one, k))

    def plan(work, *given):
        tasks.append(functools.partial(work, *given))

    def work_on(count):
        for task in tasks[:count]:
            task()
        del tasks[:count]

    plan(up_terms, 1)
    plan(sums.up.start, 0)
    plan(up_terms, 3)
    plan(sums.up.start, 1)
    plan(up_terms, 2)
    plan(up_terms, 0)
    for k in range(up_chunks):
        plan(first, sums.up, k)
    for block in range(fsdp):
        plan(feed_terms, block)
    plan(down_terms, 1)
    plan(sums.down.start, 0)
    plan(down_terms, 3)
    plan(sums.down.start, 1)
    plan(down_terms, 2)
    plan(down_terms, 0)
    for k in range(down_chunks):
        plan(first, sums.down, k)

    loads.middle.wait()
    work_on(4)
    for copy in (loads.output, loads.queries, loads.pairs, loads.mixture):
        copy.wait()
    r.grad_pairs[...] = jnp.zeros_like(r.grad_pairs)

    def home_feed(half, k):
        rows = line.at(half, k)
        feed = sum_feed.total(half, k) + vector(5)
        total = r.middle[pl.ds(k * step_rows, step_rows), :] + feed
        slot = place * tokens + half * line.half + k * step_rows
        slots = slot + lax.broadcasted_iota(jnp.int32, (step_rows, width), 0)
        keep = jnp.where(slots < length, 1.0, 0.0)
        note(6, keep * total * total)
        note(7, keep * feed * feed)
        r.feed_own[rows, :] = (keep * total).astype(LOW)
        spread_result.begin(half, k, r.feed_own)

    def attend_share(start):
        rows = pl.ds(start, share)
        total = mm_nt(r.grad_branch[rows, pl.ds(0, columns)], r.output[0])
        for block in range(1, fsdp):
            total += mm_nt(r.grad_branch[rows, pl.ds(block * columns, columns)], r.output[block])
        r.grad_mixture[...] = total.astype(LOW)
        keys = r.pairs[:, pl.ds(0, HD)]
        values = r.pairs[:, pl.ds(HD, HD)]
        shape = (share, keys.shape[0])
        query_at = place * tokens + start + lax.broadcasted_iota(jnp.int32, shape, 0)
        key_at = lax.broadcasted_iota(jnp.int32, shape, 1)
        allowed = (key_at <= query_at) & (key_at < length)
        factor = 1.0 / math.sqrt(HD)
        for head in range(heads):
            at = pl.ds(head * HD, HD)
            query = r.queries[rows, at]
            grad_mix = r.grad_mixture[:, at]
            scores = jnp.where(allowed, mm_nt(query, keys) * factor, NEGATIVE)
            soft = jnp.exp(scores - r.log_total[rows, pl.ds(head, 1)])
            grad_soft = mm_nt(grad_mix, values)
            dot_rows = jnp.sum(soft * grad_soft, -1, keepdims=True)
            grad_scores = (soft * (grad_soft - dot_rows) * factor).astype(LOW)
            r.grad_queries[rows, at] = mm(grad_scores, keys).astype(LOW)
            r.grad_pairs[:, pl.ds(0, HD)] += mm_tn(grad_scores, query)
            r.grad_pairs[:, pl.ds(HD, HD)] += mm_tn(soft.astype(LOW), grad_mix)

    def move_on(count):
        for one, k in late[:count]:
            one.second(k)
        del late[:count]

    flow_two = Flow(sum_two, spread_branch, home_two, 1)
    flow_feed = Flow(sum_feed, spread_result, home_feed, 1)
    starts = [half * line.half + group * share for group in range(tp // 2) for half in range(2)]
    per_share = share // step_rows
    while flow_two.now < flow_two.steps:
        flow_two.advance(1)
        work_on(2)
        if flow_two.now > 2:
            move_on(1)
        group = tp // 2 - (len(starts) + 1) // 2
        if starts and flow_two.now > flow_two.ready((group + 1) * per_share - 1):
            attend_share(starts.pop(0))
    work_on(len(tasks))
    flow_feed.launch()
    for start in starts:
        attend_share(start)
        flow_feed.advance(1)
    loads.query.wait()
    loads.pair.wait()

    def pair_out(other):
        target = lax.rem(place + other, ctx)
        rows = pl.ds(pl.multiple_of(target * tokens, tokens), tokens)
        r.pair_sent[other - 1] = r.grad_pairs[rows, :].astype(LOW)
        return send(
            r.pair_sent.at[other - 1],
            r.pair_came.at[other - 1],
            r.pair_ctx_sem.at[0, other - 1],
            r.pair_ctx_sem.at[1, other - 1],
            CTX,
            target,
        )

    ctx_copies = [pair_out(other) for other in range(1, ctx)]
    for copy in ctx_copies:
        copy.start()
    sum_two.drain()

    @tiles(width, step)
    def _(col):
        at = pl.ds(col, step)
        r.sum_own[:, at] = mm_nt(r.grad_queries[...], r.query[at, :]).astype(LOW)

    flow_one = Flow(sum_one, spread_stream, lambda half, k: home_one(half, k), 1)
    flow_one.launch()
    for copy in ctx_copies:
        copy.wait()
    own_rows = pl.ds(pl.multiple_of(place * tokens, tokens), tokens)
    own_pairs = r.grad_pairs[own_rows, :]
    for other in range(1, ctx):
        own_pairs += r.pair_came[other - 1].astype(WIDE)
    r.pair_own[...] = own_pairs.astype(LOW).reshape(r.pair_own.shape)

    def pair_line(other):
        target = lax.rem(zone + other, tp)
        return send(
            r.pair_own.at[target],
            r.pair_terms.at[other - 1],
            r.pair_line_sem.at[0, other - 1],
            r.pair_line_sem.at[1, other - 1],
            TP,
            target,
        )

    def pair_spread(other):
        return send(
            r.pair_all.at[zone],
            r.pair_all.at[zone],
            r.pair_line_sem.at[2, other - 1],
            r.pair_line_sem.at[3, other - 1],
            TP,
            lax.rem(zone + other, tp),
        )

    for other in range(1, tp):
        pair_line(other).start()

    r.rows[pl.ds(10, 1), pl.ds(0, query_width)] = jnp.sum(
        r.grad_queries[...].astype(WIDE), 0, keepdims=True
    )
    loads_one = pltpu.make_async_copy(r.input_one_hbm, r.input_two, r.load_sem.at[0])
    loads_one.start()

    def output_terms(n):
        terms = mm_tn(r.mixture[...], r.grad_branch[:, turn(n)])
        sums.output.piece(n, 0)[...] = terms.astype(LOW)

    def query_terms(n):
        terms = mm_tn(r.input_two[:, turn(n)], r.grad_queries[...])
        sums.query.piece(n, 0)[...] = terms.astype(LOW)

    def pair_terms(n):
        terms = mm_tn(r.input_two[:, turn(n)], r.pair_all[...].reshape(tokens, 2 * HD))
        r.pair_piece[n] = terms.astype(LOW)

    def begin(one, terms):
        plan(terms, 1)
        plan(one.start, 0)
        plan(terms, 3)
        plan(one.start, 1)
        plan(terms, 2)
        plan(terms, 0)

    def pair_shares():
        total = r.pair_own[zone].astype(WIDE)
        for other in range(1, tp):
            pair_line(other).wait_recv()
            total += r.pair_terms[other - 1].astype(WIDE)
        r.pair_all[zone] = total.astype(LOW)
        for other in range(1, tp):
            pair_spread(other).start()

    def pair_gathered():
        for other in range(1, tp):
            pair_spread(other).wait_recv()
        values = r.pair_all[...].reshape(tokens, 2 * HD)[:, HD:]
        r.rows[pl.ds(11, 1), pl.ds(0, HD)] = jnp.sum(values.astype(WIDE), 0, keepdims=True)

    def home_one(half, k):
        rows = line.at(half, k)
        here = pl.ds(k * step_rows, step_rows)
        unit, scaled = norm_of(r.stream[here, :].astype(WIDE))
        at = half * line.half + k * step_rows
        pair_rows = r.pair_all[at // share, pl.ds(at % share, step_rows), :]
        upstream = sum_one.total(half, k) + mm_nt(pair_rows, r.pair[...])
        note(4, upstream * unit)
        note(5, upstream)
        grad = r.grad_middle[here, :] + norm_backward(upstream, unit, scaled, vector(0))
        r.sum_own[rows, :] = grad.astype(LOW)
        spread_stream.begin(half, k, r.sum_own)

    begin(sums.output, output_terms)
    plan(loads_one.wait)
    begin(sums.query, query_terms)
    plan(first, sums.output, 0)
    plan(first, sums.query, 0)
    begin(sums.pair, pair_terms)
    plan(first, sums.pair, 0)
    loads.stream.wait()
    work_on(3)
    pair_shares()
    work_on(4)
    pair_gathered()
    while flow_one.now < flow_one.steps:
        flow_one.advance(1)
        work_on(3)
        flow_feed.advance(1)
        if flow_one.now % 3 == 2:
            move_on(1)
    work_on(len(tasks))
    flow_feed.advance(flow_feed.steps)
    move_on(len(late))

    for half in range(2):

        @pl.when(line.is_home(half))
        def _():
            rows = pl.ds(half * line.half, line.half)
            copies = [
                pltpu.make_async_copy(r.feed_own.at[rows], r.result.at[rows], r.keep_sem.at[0]),
                pltpu.make_async_copy(r.sum_own.at[rows], r.stream_grad.at[rows], r.keep_sem.at[1]),
            ]
            for copy in copies:
                copy.start()
            for copy in copies:
                copy.wait()

    for one in (sum_feed, sum_one, spread_branch, spread_result, spread_stream):
        one.drain()
    for other in range(1, tp):
        pair_line(other).wait_send()
        pair_spread(other).wait_send()
    for one in vars(sums).values():
        one.finish()


def back(values, front_given):
    fsdp, ctx, tp = lax.axis_size(FSDP), lax.axis_size(CTX), lax.axis_size(TP)
    g = types.SimpleNamespace(**front_given)
    tokens, width = g.input_two.shape
    inner = g.up_all.shape[1]
    columns = width // fsdp
    share = tokens // tp
    query_width = g.queries.shape[1]
    pair_width = 2 * HD
    key_count = g.pairs.shape[0]
    dma = pltpu.SemaphoreType.DMA
    far_outs = dict(
        result=((tokens, width), LOW),
        stream_grad=((tokens, width), LOW),
        up_last=((ctx, columns, inner), LOW),
        up_near=((2, columns, inner), LOW),
        up_far=((columns, inner), LOW),
        down_last=((ctx, inner, columns), LOW),
        down_near=((2, inner, columns), LOW),
        down_far=((inner, columns), LOW),
        output_last=((ctx, query_width, columns), LOW),
        output_near=((2, query_width, columns), LOW),
        output_far=((query_width, columns), LOW),
        query_last=((ctx, columns, query_width), LOW),
        query_near=((2, columns, query_width), LOW),
        query_far=((columns, query_width), LOW),
        pair_last=((ctx, columns, pair_width), LOW),
        pair_near=((2, columns, pair_width), LOW),
        pair_far=((columns, pair_width), LOW),
    )
    scratch = dict(
        up=pltpu.VMEM((width, inner), LOW),
        down=pltpu.VMEM((fsdp, inner, columns), LOW),
        input_two=pltpu.VMEM((tokens, width), LOW),
        grad_feed=pltpu.VMEM((tokens, width), LOW),
        hidden=pltpu.VMEM((tokens, inner), LOW),
        grad_pre=pltpu.VMEM((tokens, inner), LOW),
        work_one=pltpu.VMEM((tokens, columns), WIDE),
        work_two=pltpu.VMEM((tokens, columns), WIDE),
        sum_own=pltpu.VMEM((tokens, width), LOW),
        sum_slots=pltpu.VMEM((tokens, width), LOW),
        feed_own=pltpu.VMEM((tokens, width), LOW),
        feed_slots=pltpu.VMEM((tokens, width), LOW),
        grad_branch=pltpu.VMEM((tokens, width), LOW),
        middle=pltpu.VMEM((tokens // 2, width), WIDE),
        grad_middle=pltpu.VMEM((tokens // 2, width), WIDE),
        stream=pltpu.VMEM((tokens // 2, width), LOW),
        output=pltpu.VMEM((fsdp, query_width, columns), LOW),
        query=pltpu.VMEM((width, query_width), LOW),
        pair=pltpu.VMEM((width, pair_width), LOW),
        queries=pltpu.VMEM((tokens, query_width), LOW),
        pairs=pltpu.VMEM((key_count, pair_width), LOW),
        mixture=pltpu.VMEM((tokens, query_width), LOW),
        grad_mixture=pltpu.VMEM((share, query_width), LOW),
        grad_queries=pltpu.VMEM((tokens, query_width), LOW),
        grad_pairs=pltpu.VMEM((key_count, pair_width), WIDE),
        pair_sent=pltpu.VMEM((ctx - 1, tokens, pair_width), LOW),
        pair_came=pltpu.VMEM((ctx - 1, tokens, pair_width), LOW),
        pair_own=pltpu.VMEM((tp, share, pair_width), LOW),
        pair_terms=pltpu.VMEM((tp - 1, share, pair_width), LOW),
        pair_all=pltpu.VMEM((tp, share, pair_width), LOW),
        pair_piece=pltpu.VMEM((fsdp, columns, pair_width), LOW),
        stage_up=pltpu.VMEM((2, columns // 4, inner), LOW),
        stage_down=pltpu.VMEM((2, inner // 4, columns), LOW),
        weight_sem=dma((2, inner // columns)),
        load_sem=dma((10,)),
        keep_sem=dma((2,)),
        pair_ctx_sem=dma((2, ctx - 1)),
        pair_line_sem=dma((4, tp - 1)),
        two_sems=line_sems(tokens),
        feed_sems=line_sems(tokens),
        one_sems=line_sems(tokens),
        branch_sems=line_sems(tokens),
        result_sems=line_sems(tokens),
        stream_sems=line_sems(tokens),
        up_sems=PieceSum.sems(4),
        down_sems=PieceSum.sems(4),
        output_sems=PieceSum.sems(1),
        query_sems=PieceSum.sems(1),
        pair_sems=PieceSum.sems(1),
    )
    if tokens != query_width or inner < width:
        scratch.update(output_piece=pltpu.VMEM((fsdp, query_width, columns), LOW))
    if tokens != columns or inner < fsdp * query_width:
        scratch.update(query_piece=pltpu.VMEM((fsdp, columns, query_width), LOW))
    return call_kernel(
        back_body,
        2,
        dict(
            input_two_hbm=g.input_two,
            cotangent_hbm=values.cotangent,
            up_hbm=g.up_all,
            down_hbm=g.down_all,
            output_hbm=g.output_all,
            queries_hbm=g.queries,
            pairs_hbm=g.pairs,
            mixture_hbm=g.mixture,
            query_hbm=g.query_all,
            pair_hbm=g.pair_all,
            middle_hbm=g.middle,
            stream_hbm=values.stream,
            input_one_hbm=g.input_one,
        ),
        dict(vectors=g.vectors, log_total=g.log_total),
        dict(lengths=values.lengths),
        far_outs,
        dict(rows=((16, max(width, inner)), WIDE)),
        scratch,
    )


def swap(block, axis, bit):
    count = lax.axis_size(axis)
    return lax.ppermute(block, axis, [(place, place ^ bit) for place in range(count)])


def sum_over(values, axes):
    for axis in axes:
        for bit in bits_of(axis):
            values = values + swap(values, axis, bit)
    return values


def body(
    stream,
    cotangent,
    lengths,
    first_gain,
    first_shift,
    query_weight,
    query_bias,
    pair_weight,
    value_bias,
    output_weight,
    output_bias,
    second_gain,
    second_shift,
    up_weight,
    up_bias,
    down_weight,
    down_bias,
):
    fsdp = lax.axis_size(FSDP)
    me, place = lax.axis_index(FSDP), lax.axis_index(CTX)
    seq_count, group_len, width = stream.shape
    tokens = seq_count * group_len
    columns, inner = first_gain.shape[0], up_weight.shape[1]

    def placed(bias):
        spots = jnp.arange(fsdp)[None, :, None] == me
        return jnp.where(spots, bias.reshape(-1, 1, bias.shape[-1]).astype(WIDE), 0.0).reshape(-1)

    def row(values):
        return jnp.pad(values.astype(WIDE), (0, columns - values.shape[0]))[None]

    vectors = (first_gain, first_shift, output_bias, second_gain, second_shift, down_bias)
    packed = jnp.concatenate(
        [row(vector) for vector in vectors]
        + [row(placed(query_bias)), row(placed(value_bias.reshape(1, -1)))]
        + [placed(up_bias).reshape(-1, columns)]
    )
    packed = jnp.pad(packed, ((0, -packed.shape[0] % 8), (0, 0)))
    values = types.SimpleNamespace(
        stream=stream.reshape(tokens, width),
        cotangent=cotangent.reshape(tokens, width),
        lengths=lengths,
        packed=packed,
        query=query_weight,
        pair=pair_weight,
        output=output_weight,
        up=up_weight,
        down=down_weight,
    )
    given = front(values, tokens)
    ended = types.SimpleNamespace(**back(values, given))
    rows = ended.rows
    query_width = query_weight.shape[1]

    def finished(last):
        return jnp.sum(last.astype(WIDE), 0)

    held = place * tokens + jnp.arange(tokens) < lengths[0]
    end = jnp.where(lax.axis_index(TP) == 0, 1.0, 0.0)
    at_home = jnp.where(
        (lax.axis_index(TP) == 0) | (lax.axis_index(TP) == lax.axis_size(TP) - 1), 1.0, 0.0
    )
    shared = jnp.concatenate(
        [rows[k, :width] for k in range(6)]
        + [
            jnp.stack(
                [
                    jnp.sum(rows[6, :width]),
                    jnp.sum(given["squares"]) * at_home,
                    jnp.sum(rows[7, :width]),
                    jnp.sum(held.astype(WIDE)) * end,
                ]
            )
        ]
    )
    shared = sum_over(shared, (TP, FSDP, CTX))
    own = jnp.concatenate([rows[9, :inner], rows[10, :query_width], rows[11, :HD]])
    own = sum_over(own, (FSDP, CTX))
    up_bias_all = own[:inner].reshape(up_bias.shape[0], fsdp, -1)
    query_bias_all = own[inner : inner + query_width].reshape(query_bias.shape[0], fsdp, -1)

    def mine(row, size):
        return lax.dynamic_slice_in_dim(row, me * size, size, 0)

    totals = shared[6 * width :]
    root_means = jnp.sqrt(totals[:3] / (totals[3] * width))
    return (
        ended.result.reshape(stream.shape),
        ended.stream_grad.reshape(stream.shape),
        mine(shared[4 * width : 5 * width], columns),
        mine(shared[5 * width : 6 * width], columns),
        finished(ended.query_last),
        lax.dynamic_index_in_dim(query_bias_all, me, 1, False),
        finished(ended.pair_last),
        mine(own[inner + query_width :], value_bias.shape[0]),
        finished(ended.output_last),
        mine(shared[2 * width : 3 * width], columns),
        mine(shared[:width], columns),
        mine(shared[width : 2 * width], columns),
        finished(ended.up_last),
        lax.dynamic_index_in_dim(up_bias_all, me, 1, False),
        finished(ended.down_last),
        mine(shared[3 * width : 4 * width], columns),
        root_means,
    )


def solution(mesh):
    in_specs = (
        P(FSDP, CTX, None),
        P(FSDP, CTX, None),
        P(FSDP),
        P(FSDP),
        P(FSDP),
        P(FSDP, TP),
        P(TP, FSDP),
        P(FSDP, None),
        P(FSDP),
        P(TP, FSDP),
        P(FSDP),
        P(FSDP),
        P(FSDP),
        P(FSDP, TP),
        P(TP, FSDP),
        P(TP, FSDP),
        P(FSDP),
    )
    out_specs = (
        P(FSDP, CTX, None),
        P(FSDP, CTX, None),
        P(FSDP),
        P(FSDP),
        P(FSDP, TP),
        P(TP, FSDP),
        P(FSDP, None),
        P(FSDP),
        P(TP, FSDP),
        P(FSDP),
        P(FSDP),
        P(FSDP),
        P(FSDP, TP),
        P(TP, FSDP),
        P(TP, FSDP),
        P(FSDP),
        P(),
    )
    return jax.shard_map(body, mesh=mesh, in_specs=in_specs, out_specs=out_specs, check_vma=False)
```

```python
import functools
import math
import types

import jax
import jax.numpy as jnp
from jax import lax
from jax.experimental import pallas as pl
from jax.experimental.pallas import tpu as pltpu
from jax.sharding import PartitionSpec as P

HD = 128
EPSILON = 1e-05
NEGATIVE = -1e30
FSDP, CTX, TP = "fsdp", "ctx", "tp"
LOW, WIDE = jnp.bfloat16, jnp.float32
MESH = pl.DeviceIdType.MESH
VMEM_BYTES = 60 << 20
SKEW, LAG = 2, 2


def flip(place, bit):
    return place + bit - 2 * bit * lax.rem(lax.div(place, bit), 2)


def bits_of(axis):
    count, bit, found = lax.axis_size(axis), 1, []
    while bit < count:
        found.append(bit)
        bit *= 2
    return found


def mm(left, right):
    return jnp.dot(left, right, preferred_element_type=WIDE)


def mm_nt(left, right):
    return lax.dot_general(left, right, (((1,), (1,)), ((), ())), preferred_element_type=WIDE)


def mm_tn(left, right):
    return lax.dot_general(left, right, (((0,), (0,)), ((), ())), preferred_element_type=WIDE)


def tiles(count, step):
    def run(work):
        def once(index, carry):
            work(pl.multiple_of(index * step, step))
            return carry

        lax.fori_loop(0, count // step, once, 0)

    return run


def norm_of(values):
    center = values - jnp.mean(values, -1, keepdims=True)
    scaled = lax.rsqrt(jnp.mean(center * center, -1, keepdims=True) + EPSILON)
    return center * scaled, scaled


def norm_backward(upstream, unit_rows, scaled, norm_gain):
    gained = upstream * norm_gain
    return scaled * (
        gained
        - jnp.mean(gained, -1, keepdims=True)
        - unit_rows * jnp.mean(gained * unit_rows, -1, keepdims=True)
    )


def send(source, target, outgo, income, axis, place):
    return pltpu.make_async_remote_copy(
        src_ref=source,
        dst_ref=target,
        send_sem=outgo,
        recv_sem=income,
        device_id={axis: place},
        device_id_type=MESH,
    )


def all_peers():
    me, place, zone = lax.axis_index(FSDP), lax.axis_index(CTX), lax.axis_index(TP)
    ctx, tp = lax.axis_size(CTX), lax.axis_size(TP)
    peers = [(FSDP, flip(me, 1)), (FSDP, flip(me, 2)), (FSDP, flip(flip(me, 1), 2))]
    peers += [(CTX, lax.rem(place + k, ctx)) for k in range(1, ctx)]
    peers += [(TP, lax.rem(zone + k, tp)) for k in range(1, tp)]
    return peers


def greet(peers):
    barrier = pltpu.get_barrier_semaphore()
    for axis, place in peers:
        pl.semaphore_signal(barrier, inc=1, device_id={axis: place}, device_id_type=MESH)
    return lambda: pl.semaphore_wait(barrier, len(peers))


def split_rows(tokens):
    rows = 32 if tokens % 512 == 0 else 16
    return rows, tokens // 2 // rows


class Line:
    def __init__(self, tokens):
        self.place, self.count = lax.axis_index(TP), lax.axis_size(TP)
        self.rows, self.chunks = split_rows(tokens)
        self.half = tokens // 2

    def at(self, half, k):
        start = half * self.half + k * self.rows
        return pl.ds(start if isinstance(start, int) else pl.multiple_of(start, self.rows), self.rows)

    def is_home(self, half):
        return self.place == (0 if half == 0 else self.count - 1)

    def is_far(self, half):
        return self.place == (self.count - 1 if half == 0 else 0)

    def toward(self, half):
        move = self.count - 1 if half == 0 else 1
        return lax.rem(self.place + move, self.count)

    def away(self, half):
        return self.toward(1 - half)


class LineSum(Line):
    def __init__(self, own, slots, sems):
        super().__init__(own.shape[0])
        self.own, self.slots = own, slots
        self.outgo, self.income = sems

    def copy(self, half, k):
        rows = self.at(half, k)
        return send(
            self.own.at[rows],
            self.slots.at[rows],
            self.outgo.at[half, k],
            self.income.at[half, k],
            TP,
            self.toward(half),
        )

    def launch(self, half, first=0, last=None):
        @pl.when(self.is_far(half))
        def _():
            for k in range(first, self.chunks if last is None else last):
                self.copy(half, k).start()

    def total(self, half, k):
        rows = self.at(half, k)
        return self.own[rows, :].astype(WIDE) + self.slots[rows, :].astype(WIDE)

    def pass_on(self, half, k):
        self.copy(half, k).wait_recv()
        self.own[self.at(half, k), :] = self.total(half, k).astype(LOW)
        self.copy(half, k).start()

    def drain(self):
        for half in range(2):

            @pl.when(jnp.logical_not(self.is_home(half)))
            def _():
                for k in range(self.chunks):
                    self.copy(half, k).wait_send()


class LineSpread(Line):
    def __init__(self, held, sems):
        super().__init__(held.shape[0])
        self.held = held
        self.outgo, self.income = sems

    def copy(self, half, k, source=None):
        rows = self.at(half, k)
        return send(
            self.held.at[rows] if source is None else source.at[rows],
            self.held.at[rows],
            self.outgo.at[half, k],
            self.income.at[half, k],
            TP,
            self.away(half),
        )

    def begin(self, half, k, source=None):
        self.copy(half, k, source).start()

    def serve(self, half, k):
        self.copy(half, k).wait_recv()

        @pl.when(jnp.logical_not(self.is_far(half)))
        def _():
            self.copy(half, k).start()

    def drain(self):
        for half in range(2):

            @pl.when(jnp.logical_not(self.is_far(half)))
            def _():
                for k in range(self.chunks):
                    self.copy(half, k).wait_send()


class Flow(Line):
    def __init__(self, line_sum, spread, home, lag):
        super().__init__(line_sum.own.shape[0])
        self.sum, self.spread, self.home, self.lag = line_sum, spread, home, lag
        self.now = 0
        self.to_home = SKEW * (self.count - 2)
        self.steps = self.chunks + lag + 2 * self.to_home

    def launch(self, first=0, last=None):
        for half in range(2):
            self.sum.launch(half, first, last)

    def inside(self, k):
        return (k >= 0) & (k < self.chunks)

    def advance(self, count=1):
        for n in range(self.now, min(self.now + count, self.steps)):
            self.step(n)
        self.now = min(self.now + count, self.steps)

    def step(self, n):
        last = self.count - 1
        at_home = n - self.to_home
        for half in range(2):
            hops = last - self.place if half == 0 else self.place
            k = n - SKEW * (hops - 1)

            @pl.when((hops >= 1) & (hops < last) & self.inside(k))
            def _():
                self.sum.pass_on(half, k)

            if 0 <= at_home < self.chunks:

                @pl.when(self.is_home(half))
                def _():
                    self.sum.copy(half, at_home).wait_recv()
                    self.home(half, at_home)

        for half in range(2):
            hops = self.place if half == 0 else last - self.place
            k = at_home - self.lag - SKEW * (hops - 1)

            @pl.when((hops >= 1) & self.inside(k))
            def _():
                self.spread.serve(half, k)

    def all_home(self):
        return self.now >= self.chunks + self.to_home

    def ready(self, chunk):
        return chunk + self.lag + 2 * self.to_home


class Gather:
    def __init__(self, shard, held, sems, cut):
        self.shard, self.held = shard, held
        self.me, self.place = lax.axis_index(FSDP), lax.axis_index(CTX)
        self.ctx = lax.axis_size(CTX)
        self.cut = cut
        self.rows = shard.shape[0] // self.ctx // cut
        self.near_sem, self.far_sem, self.side_sem, self.pass_sem, self.local = sems

    def part(self, place, k):
        return pl.ds(pl.multiple_of((place * self.cut + k) * self.rows, self.rows), self.rows)

    def keep(self):
        every = pl.ds(0, self.shard.shape[0])
        return pltpu.make_async_copy(self.shard, self.held(self.me, every), self.local.at[0])

    def near(self):
        every = pl.ds(0, self.shard.shape[0])
        return send(
            self.shard,
            self.held(self.me, every),
            self.near_sem.at[0],
            self.near_sem.at[1],
            FSDP,
            flip(self.me, 1),
        )

    def far(self, k):
        part = self.part(self.place, k)
        return send(
            self.shard.at[part],
            self.held(self.me, part),
            self.far_sem.at[0, k],
            self.far_sem.at[1, k],
            FSDP,
            flip(self.me, 2),
        )

    def side(self, other, k):
        held = self.held(flip(self.me, 2), self.part(self.place, k))
        return send(
            held,
            held,
            self.side_sem.at[0, other - 1, k],
            self.side_sem.at[1, other - 1, k],
            CTX,
            lax.rem(self.place + other, self.ctx),
        )

    def over(self, other, k):
        place = lax.rem(self.place + self.ctx - other, self.ctx)
        held = self.held(flip(self.me, 2), self.part(place, k))
        return send(
            held,
            held,
            self.pass_sem.at[0, other, k],
            self.pass_sem.at[1, other, k],
            FSDP,
            flip(self.me, 1),
        )

    def start(self):
        for k in range(self.cut):
            self.far(k).start()
        self.near().start()
        self.keep().start()

    def cross(self, k):
        self.far(k).wait_recv()
        for other in range(1, self.ctx):
            self.side(other, k).start()
        self.over(0, k).start()

    def pass_on(self, k):
        for other in range(1, self.ctx):
            self.side(other, k).wait_recv()
            self.over(other, k).start()

    def ready(self):
        self.keep().wait()
        self.near().wait_recv()
        for k in range(self.cut):
            for other in range(self.ctx):
                self.over(other, k).wait_recv()

    def drain(self):
        self.near().wait_send()
        for k in range(self.cut):
            self.far(k).wait_send()
            for other in range(self.ctx):
                self.over(other, k).wait_send()
                if other > 0:
                    self.side(other, k).wait_send()

    @staticmethod
    def sems(cut):
        ctx = lax.axis_size(CTX)
        shapes = ((2,), (2, cut), (2, ctx - 1, cut), (2, ctx, cut), (1,))
        return tuple(pltpu.SemaphoreType.DMA(shape) for shape in shapes)


class PieceSum:
    def __init__(self, piece, near, far, last, stages, sems, chunks):
        self.piece, self.near, self.far, self.last = piece, near, far, last
        self.stages, self.chunks = stages, chunks
        self.rows = far.shape[0] // chunks
        self.near_sem, self.far_sem, self.last_sem, self.local = sems
        self.me, self.place = lax.axis_index(FSDP), lax.axis_index(CTX)
        self.ctx = lax.axis_size(CTX)

    def part(self, k):
        return pl.ds(k * self.rows, self.rows)

    def near_copy(self, which, k):
        return send(
            self.piece(2 * which + 1, k),
            self.near.at[which, self.part(k)],
            self.near_sem.at[0, which, k],
            self.near_sem.at[1, which, k],
            FSDP,
            flip(self.me, 1),
        )

    def far_copy(self, k):
        return send(
            self.piece(2, k),
            self.far.at[self.part(k)],
            self.far_sem.at[0, k],
            self.far_sem.at[1, k],
            FSDP,
            flip(self.me, 2),
        )

    def last_copy(self, other, k):
        return send(
            self.piece(0, k),
            self.last.at[self.place, self.part(k)],
            self.last_sem.at[0, other - 1, k],
            self.last_sem.at[1, other - 1, k],
            CTX,
            lax.rem(self.place + other, self.ctx),
        )

    def own_copy(self, k):
        return pltpu.make_async_copy(
            self.piece(0, k), self.last.at[self.place, self.part(k)], self.local.at[3 + k]
        )

    def start(self, which):
        for k in range(self.chunks):
            self.near_copy(which, k).start()

    def load(self, source, index):
        return pltpu.make_async_copy(source, self.stages[index], self.local.at[index])

    def add(self, r, k, index):
        step = 32 if self.rows % 32 == 0 else 16
        piece, stage = self.piece(r, k), self.stages[index]

        @tiles(self.rows, step)
        def _(at):
            here = pl.ds(at, step)
            total = piece[here].astype(WIDE) + stage[here].astype(WIDE)
            piece[here] = total.astype(LOW)

    def fetch_first(self, k):
        for which in range(2):
            self.near_copy(which, k).wait_recv()
        for which in range(2):
            self.load(self.near.at[which, self.part(k)], which).start()

    def add_first(self, k):
        self.load(self.near.at[1, self.part(k)], 1).wait()
        self.add(2, k, 1)
        self.far_copy(k).start()
        self.load(self.near.at[0, self.part(k)], 0).wait()
        self.add(0, k, 0)

    def fetch_second(self, k):
        self.far_copy(k).wait_recv()
        self.load(self.far.at[self.part(k)], 2).start()

    def add_second(self, k):
        self.load(self.far.at[self.part(k)], 2).wait()
        self.add(0, k, 2)
        for other in range(1, self.ctx):
            self.last_copy(other, k).start()
        self.own_copy(k).start()

    def finish(self):
        for k in range(self.chunks):
            for other in range(1, self.ctx):
                self.last_copy(other, k).wait_recv()
                self.last_copy(other, k).wait_send()
            self.own_copy(k).wait()
            self.far_copy(k).wait_send()
            for which in range(2):
                self.near_copy(which, k).wait_send()

    @staticmethod
    def sems(chunks):
        ctx = lax.axis_size(CTX)
        shapes = ((2, 2, chunks), (2, chunks), (2, ctx - 1, chunks), (3 + chunks,))
        return tuple(pltpu.SemaphoreType.DMA(shape) for shape in shapes)


class RowSum:
    def __init__(self, rows, came, sems, axes):
        self.rows, self.came, self.sems = rows, came, sems
        self.hops = [(axis, bit) for axis in axes for bit in bits_of(axis)]
        self.now = len(self.hops)

    def copy(self, n):
        axis, bit = self.hops[n]
        return send(
            self.rows,
            self.came.at[n],
            self.sems.at[0, n],
            self.sems.at[1, n],
            axis,
            flip(lax.axis_index(axis), bit),
        )

    def start(self):
        self.now = 0
        self.copy(0).start()

    def move(self):
        if self.now == len(self.hops):
            return False
        self.copy(self.now).wait()
        self.rows[...] += self.came[self.now]
        self.now += 1
        if self.now < len(self.hops):
            self.copy(self.now).start()
        return True

    def finish(self):
        while self.move():
            pass


def line_sems(tokens):
    rows, chunks = split_rows(tokens)
    return tuple(pltpu.SemaphoreType.DMA((2, chunks)) for _ in range(2))


def call_kernel(body, ident, far, near, scalars, far_outs, near_outs, scratch):
    groups = (far, near, scalars)
    spaces = (pl.ANY, pltpu.VMEM, pltpu.SMEM)
    arrays, in_specs = [], []
    for group, space in zip(groups, spaces):
        arrays += list(group.values())
        in_specs += [pl.BlockSpec(memory_space=space)] * len(group)
    outs = dict(far_outs, **near_outs)
    out_specs = [pl.BlockSpec(memory_space=pl.ANY)] * len(far_outs)
    out_specs += [pl.BlockSpec(memory_space=pltpu.VMEM)] * len(near_outs)
    shapes, tree = jax.tree.flatten(scratch)
    ins = [name for group in groups for name in group]

    def kernel(*refs):
        held = dict(zip(ins + list(outs), refs))
        held.update(jax.tree.unflatten(tree, refs[len(ins) + len(outs) :]))
        body(types.SimpleNamespace(**held))

    given = pl.pallas_call(
        kernel,
        out_shape=[jax.ShapeDtypeStruct(shape, kind) for shape, kind in outs.values()],
        in_specs=in_specs,
        out_specs=out_specs,
        scratch_shapes=shapes,
        compiler_params=pltpu.CompilerParams(
            collective_id=ident, has_side_effects=True, vmem_limit_bytes=VMEM_BYTES
        ),
    )(*arrays)
    return dict(zip(outs, given))


def front_body(r):
    me, place, zone = lax.axis_index(FSDP), lax.axis_index(CTX), lax.axis_index(TP)
    fsdp, ctx, tp = lax.axis_size(FSDP), lax.axis_size(CTX), lax.axis_size(TP)
    tokens, width = r.stream_hbm.shape
    columns = width // fsdp
    query_width = r.query.shape[1]
    heads = query_width // HD
    inner = r.up_shard.shape[1]
    length = r.lengths[0]
    line = Line(tokens)
    step_rows, chunks = line.rows, line.chunks

    ready = greet(all_peers())
    stream_load = pltpu.make_async_copy(r.stream_hbm, r.stream, r.load_sem.at[0])
    stream_load.start()

    def block_rows(held):
        size = held.shape[0] // fsdp

        def view(block, rows):
            start = pl.multiple_of(block * size + rows.start, 16)
            return held.at[pl.ds(start, rows.size)]

        return view

    gathers = types.SimpleNamespace(
        query=Gather(r.query_shard, block_rows(r.query), r.query_sems, r.query_sems[1].shape[1]),
        pair=Gather(r.pair_shard, block_rows(r.pair), r.pair_sems, r.pair_sems[1].shape[1]),
        output=Gather(r.output_shard, lambda b, rows: r.output.at[b, rows], r.output_sems, r.output_sems[1].shape[1]),
        up=Gather(r.up_shard, block_rows(r.up_all), r.up_sems, r.up_sems[1].shape[1]),
        down=Gather(
            r.down_shard, lambda b, rows: r.down_all.at[b, rows], r.down_sems, r.down_sems[1].shape[1]
        ),
    )

    def small_copy(k):
        target = flip(me, k) if k < 3 else flip(flip(me, 1), 2)
        return send(
            r.smalls.at[0], r.smalls.at[k], r.small_sem.at[0, k - 1], r.small_sem.at[1, k - 1],
            FSDP, target,
        )

    r.smalls[0] = r.packed[...]
    ready()
    for k in range(1, fsdp):
        small_copy(k).start()
    gathers.pair.start()
    gathers.query.start()
    for k in range(1, fsdp):
        small_copy(k).wait()
    query_add = jnp.zeros((1, query_width), WIDE)
    value_add = jnp.zeros((1, HD), WIDE)
    for k in range(fsdp):
        block = me if k == 0 else flip(me, k) if k < 3 else flip(flip(me, 1), 2)
        at = pl.ds(pl.multiple_of(block * columns, columns), columns)
        r.vectors[pl.ds(0, 6), at] = r.smalls[k, pl.ds(0, 6), :]
        query_add += r.smalls[k, pl.ds(6, 1), pl.ds(0, query_width)]
        value_add += r.smalls[k, pl.ds(7, 1), pl.ds(0, HD)]
    for q in range(inner // columns):
        total = jnp.zeros((1, columns), WIDE)
        for k in range(fsdp):
            total += r.smalls[k, pl.ds(8 + q, 1), :]
        r.vectors[pl.ds(6, 1), pl.ds(q * columns, columns)] = total
    r.vectors[pl.ds(7, 1), :] = jnp.zeros((1, r.vectors.shape[1]), WIDE)

    def vector(n):
        return r.vectors[pl.ds(n, 1), pl.ds(0, width)]

    stream_load.wait()
    norm_step = min(32, tokens)

    @tiles(tokens, norm_step)
    def _(row):
        rows = pl.ds(row, norm_step)
        unit, scaled = norm_of(r.stream[rows, :].astype(WIDE))
        r.input_one[rows, :] = (unit * vector(0) + vector(1)).astype(LOW)

    early = (gathers.pair, gathers.query)
    for k in range(2):
        for one in early:
            one.cross(k)
    for k in range(2):
        for one in early:
            one.pass_on(k)
    for one in (gathers.output, gathers.up, gathers.down):
        one.start()
    gathers.pair.ready()
    own_rows = pl.ds(pl.multiple_of(place * tokens, tokens), tokens)
    key_half = mm(r.input_one[...], r.pair[...])
    r.pairs[own_rows, pl.ds(0, HD)] = key_half[:, :HD].astype(LOW)
    r.pairs[own_rows, pl.ds(HD, HD)] = (key_half[:, HD:] + value_add).astype(LOW)

    def pair_copy(other):
        return send(
            r.pairs.at[own_rows],
            r.pairs.at[own_rows],
            r.exchange_sem.at[0, other - 1],
            r.exchange_sem.at[1, other - 1],
            CTX,
            lax.rem(place + other, ctx),
        )

    for other in range(1, ctx):
        pair_copy(other).start()
    gathers.query.ready()
    r.queries[...] = (mm(r.input_one[...], r.query[...]) + query_add).astype(LOW)
    gathers.output.cross(0)
    for other in range(1, ctx):
        pair_copy(other).wait_recv()
    gathers.output.pass_on(0)

    share = min(HD, line.half)
    per_share = share // step_rows
    factor = 1.0 / math.sqrt(HD)

    def attend(start):
        rows = pl.ds(start, share)
        keys = r.pairs[:, pl.ds(0, HD)]
        values = r.pairs[:, pl.ds(HD, HD)]
        shape = (share, keys.shape[0])
        query_at = place * tokens + start + lax.broadcasted_iota(jnp.int32, shape, 0)
        key_at = lax.broadcasted_iota(jnp.int32, shape, 1)
        allowed = (key_at <= query_at) & (key_at < length)
        for head in range(heads):
            at = pl.ds(head * HD, HD)
            scores = jnp.where(allowed, mm_nt(r.queries[rows, at], keys) * factor, NEGATIVE)
            peak = jnp.max(scores, -1, keepdims=True)
            soft = jnp.exp(scores - peak)
            total = jnp.sum(soft, -1, keepdims=True)
            r.mixture[rows, at] = mm((soft / total).astype(LOW), values).astype(LOW)
            r.log_total[rows, pl.ds(head, 1)] = peak + jnp.log(total)

    def project(start):
        rows = pl.ds(start, share)
        for block in range(fsdp):
            at = pl.ds(block * columns, columns)
            r.sum_own[rows, at] = mm(r.mixture[rows, :], r.output[block]).astype(LOW)

    branch_sum = LineSum(r.sum_own, r.sum_slots, r.sum_sems)
    spread = LineSpread(r.input_two, r.spread_sems)
    r.squares[...] = jnp.zeros_like(r.squares)

    def home(half, k):
        branch = branch_sum.total(half, k) + vector(2)
        middle = r.stream[line.at(half, k), :].astype(WIDE) + branch
        r.middle[pl.ds(k * step_rows, step_rows), :] = middle
        unit, scaled = norm_of(middle)
        r.input_two[line.at(half, k), :] = (unit * vector(3) + vector(4)).astype(LOW)
        spread.begin(half, k)
        slot = place * tokens + half * line.half + k * step_rows
        slots = slot + lax.broadcasted_iota(jnp.int32, (step_rows, width), 0)
        keep = jnp.where(slots < length, 1.0, 0.0)
        r.squares[...] += jnp.sum(keep * branch * branch, 0, keepdims=True)

    big = [(gathers.up, k) for k in range(gathers.up.cut)]
    big += [(gathers.down, k) for k in range(gathers.down.cut)]
    events = []
    for index, (one, k) in enumerate(big):
        events.append(functools.partial(one.cross, k))
        if index > 0:
            before, last = big[index - 1]
            events.append(functools.partial(before.pass_on, last))
    events.append(functools.partial(big[-1][0].pass_on, big[-1][1]))

    def move_on(count):
        for event in events[:count]:
            event()
        del events[:count]

    flow = Flow(branch_sum, spread, home, LAG)
    groups = line.half // share
    for group in range(groups):
        for half in range(2):
            start = half * line.half + group * share
            attend(start)
            if group == 0 and half == 0:
                gathers.output.ready()
            project(start)
        flow.launch(per_share * group, per_share * group + per_share)
        if group < groups - 1:
            flow.advance(1)
            move_on(1)
    while flow.now < flow.steps:
        flow.advance(1)
        if flow.now % 2 == 0:
            move_on(1)
    move_on(len(events))
    keeps = [
        pltpu.make_async_copy(source, target, r.load_sem.at[1 + n])
        for n, (source, target) in enumerate(
            ((r.query, r.query_all), (r.pair, r.pair_all), (r.output, r.output_all))
        )
    ]
    for copy in keeps:
        copy.start()
    for one in (gathers.up, gathers.down):
        one.ready()
    for copy in keeps:
        copy.wait()
    for other in range(1, ctx):
        pair_copy(other).wait_send()
    for one in vars(gathers).values():
        one.drain()
    branch_sum.drain()
    spread.drain()


def front(values, tokens):
    fsdp, ctx = lax.axis_size(FSDP), lax.axis_size(CTX)
    stream = values.stream
    width = stream.shape[1]
    columns = width // fsdp
    inner = values.up.shape[1]
    query_width = values.query.shape[1]
    pair_width = 2 * HD
    dma = pltpu.SemaphoreType.DMA
    wide_row = max(width, inner)
    return call_kernel(
        front_body,
        1,
        dict(stream_hbm=stream),
        dict(
            packed=values.packed,
            query_shard=values.query,
            pair_shard=values.pair,
            output_shard=values.output,
            up_shard=values.up,
            down_shard=values.down,
        ),
        dict(lengths=values.lengths),
        dict(
            up_all=((width, inner), LOW),
            down_all=((fsdp, inner, columns), LOW),
            query_all=((width, query_width), LOW),
            pair_all=((width, pair_width), LOW),
            output_all=((fsdp, query_width, columns), LOW),
        ),
        dict(
            vectors=((8, wide_row), WIDE),
            input_one=((tokens, width), LOW),
            input_two=((tokens, width), LOW),
            queries=((tokens, query_width), LOW),
            pairs=((tokens * ctx, pair_width), LOW),
            mixture=((tokens, query_width), LOW),
            log_total=((tokens, query_width // HD), WIDE),
            middle=((tokens // 2, width), WIDE),
            squares=((1, width), WIDE),
        ),
        dict(
            stream=pltpu.VMEM((tokens, width), LOW),
            smalls=pltpu.VMEM((fsdp,) + values.packed.shape, WIDE),
            query=pltpu.VMEM((width, query_width), LOW),
            pair=pltpu.VMEM((width, pair_width), LOW),
            output=pltpu.VMEM((fsdp, query_width, columns), LOW),
            sum_own=pltpu.VMEM((tokens, width), LOW),
            sum_slots=pltpu.VMEM((tokens, width), LOW),
            sum_sems=line_sems(tokens),
            spread_sems=line_sems(tokens),
            query_sems=Gather.sems(2),
            pair_sems=Gather.sems(2),
            output_sems=Gather.sems(1),
            up_sems=Gather.sems(2),
            down_sems=Gather.sems(2),
            load_sem=dma((4,)),
            small_sem=dma((2, fsdp - 1)),
            exchange_sem=dma((2, ctx - 1)),
        ),
    )


def back_body(r):
    me, place, zone = lax.axis_index(FSDP), lax.axis_index(CTX), lax.axis_index(TP)
    fsdp, ctx, tp = lax.axis_size(FSDP), lax.axis_size(CTX), lax.axis_size(TP)
    tokens, width = r.input_two_hbm.shape
    inner = r.up_hbm.shape[1]
    columns = width // fsdp
    share = tokens // tp
    query_width = r.queries_hbm.shape[1]
    heads = query_width // HD
    length = r.lengths[0]
    line = Line(tokens)
    step_rows, chunks = line.rows, line.chunks
    step = columns
    blocks = inner // step

    ready = greet(all_peers())

    def up_load(q):
        at = pl.ds(q, step)
        return pltpu.make_async_copy(r.up_hbm.at[:, at], r.up.at[:, at], r.weight_sem.at[0, q // step])

    def down_load(q):
        at = pl.ds(q, step)
        return pltpu.make_async_copy(
            r.down_hbm.at[:, at], r.down.at[:, at], r.weight_sem.at[1, q // step]
        )

    at_end = jnp.where(zone == tp - 1, tokens // 2, 0)
    pairs_of = dict(
        input_two=(r.input_two_hbm, r.input_two),
        cotangent=(r.cotangent_hbm, r.grad_feed),
        output=(r.output_hbm, r.output),
        queries=(r.queries_hbm, r.queries),
        pairs=(r.pairs_hbm, r.pairs),
        mixture=(r.mixture_hbm, r.mixture),
        query=(r.query_hbm, r.query),
        pair=(r.pair_hbm, r.pair),
        middle=(r.middle_hbm, r.middle),
        stream=(r.stream_hbm.at[pl.ds(pl.multiple_of(at_end, tokens // 2), tokens // 2)], r.stream),
    )
    loads = {}
    for index, (name, (source, target)) in enumerate(pairs_of.items()):
        loads[name] = pltpu.make_async_copy(source, target, r.load_sem.at[index])
    loads = types.SimpleNamespace(**loads)
    loads.input_two.start()
    loads.cotangent.start()
    for q in range(blocks):
        up_load(q * step).start()
        down_load(q * step).start()
    for name, copy in vars(loads).items():
        if copy is not loads.input_two and copy is not loads.cotangent:
            copy.start()
    for rows in (r.early, r.late, r.own):
        rows[...] = jnp.zeros_like(rows)
    r.late[pl.ds(3, 1), pl.ds(0, width)] = r.squares[...]
    counted = jnp.clip(length - place * tokens, 0, tokens).astype(WIDE)
    r.late[pl.ds(7, 1), :] = jnp.full((1, r.late.shape[1]), jnp.where(zone == 0, counted, 0.0))
    loads.cotangent.wait()

    @tiles(tokens, step_rows)
    def _(row):
        rows = pl.ds(row, step_rows)
        slots = place * tokens + row + lax.broadcasted_iota(jnp.int32, (step_rows, width), 0)
        keep = jnp.where(slots < length, 1.0, 0.0)
        r.grad_feed[rows, :] = (keep * r.grad_feed[rows, :].astype(WIDE)).astype(LOW)

    loads.input_two.wait()

    def vector(n):
        return r.vectors[pl.ds(n, 1), pl.ds(0, width)]

    def note(rows, row, values):
        rows[pl.ds(row, 1), pl.ds(0, width)] += jnp.sum(values, 0, keepdims=True)

    @tiles(inner, step)
    def _(q):
        up_load(q).wait()
        down_load(q).wait()
        at = pl.ds(q, step)
        r.work_one[...] = mm(r.input_two[...], r.up[:, at])
        total = mm_nt(r.grad_feed[:, pl.ds(0, columns)], r.down[0, at, :])
        for block in range(1, fsdp):
            total += mm_nt(r.grad_feed[:, pl.ds(block * columns, columns)], r.down[block, at, :])
        r.work_two[...] = total
        bias = r.vectors[pl.ds(6, 1), at]

        @tiles(tokens, 32)
        def _(row):
            here = pl.ds(row, 32)
            v = r.work_one[here, :] + bias
            square = v * v
            reach = math.sqrt(2.0 / math.pi)
            t = jnp.tanh(reach * v * (1.0 + 0.044715 * square))
            gate = 0.5 * (1.0 + t)
            slope = gate + 0.5 * v * (1.0 - t * t) * reach * (1.0 + 3 * 0.044715 * square)
            r.hidden[here, at] = (v * gate).astype(LOW)
            grad = (r.work_two[here, :] * slope).astype(LOW)
            r.grad_pre[here, at] = grad
            r.own[pl.ds(0, 1), at] += jnp.sum(grad.astype(WIDE), 0, keepdims=True)

    ready()
    sum_two = LineSum(r.sum_own, r.sum_slots, r.two_sems)
    sum_feed = LineSum(r.feed_own, r.feed_slots, r.feed_sems)
    sum_one = LineSum(r.sum_own, r.sum_slots, r.one_sems)
    spread_branch = LineSpread(r.grad_branch, r.branch_sems)
    spread_result = LineSpread(r.result, r.result_sems)
    spread_stream = LineSpread(r.stream_grad, r.stream_sems)

    @tiles(width, step)
    def _(col):
        at = pl.ds(col, step)
        r.sum_own[:, at] = mm_nt(r.grad_pre[...], r.up[at, :]).astype(LOW)

    for half in range(2):
        sum_two.launch(half)

    def turn(n):
        target = me
        for bit in (1, 2):
            if n & bit:
                target = flip(target, bit)
        return pl.ds(pl.multiple_of(target * columns, columns), columns)

    up_chunks, down_chunks = r.up_sems[1].shape[1], r.down_sems[1].shape[1]
    up_rows, down_rows = columns // up_chunks, inner // down_chunks

    def whole_piece(held, kept, size):
        if held is not None:
            return lambda n, k: held.at[n]
        return lambda n, k: kept.at[:, pl.ds(n * size, size)]

    def stage_part(rows, size):
        return [r.stage_down.at[n, pl.ds(0, rows), pl.ds(0, size)] for n in range(3)]

    sums = types.SimpleNamespace(
        up=PieceSum(
            lambda n, k: r.up.at[pl.ds(n * columns + k * up_rows, up_rows)],
            r.up_near,
            r.up_far,
            r.up_last,
            [r.stage_up.at[n] for n in range(3)],
            r.up_sems,
            up_chunks,
        ),
        down=PieceSum(
            lambda n, k: r.down.at[n, pl.ds(k * down_rows, down_rows)],
            r.down_near,
            r.down_far,
            r.down_last,
            [r.stage_down.at[n] for n in range(3)],
            r.down_sems,
            down_chunks,
        ),
        output=PieceSum(
            whole_piece(getattr(r, "output_piece", None), r.grad_pre, columns),
            r.output_near,
            r.output_far,
            r.output_last,
            stage_part(query_width, columns),
            r.output_sems,
            1,
        ),
        query=PieceSum(
            whole_piece(getattr(r, "query_piece", None), r.hidden, query_width),
            r.query_near,
            r.query_far,
            r.query_last,
            stage_part(columns, query_width),
            r.query_sems,
            1,
        ),
        pair=PieceSum(
            lambda n, k: r.pair_piece.at[n],
            r.pair_near,
            r.pair_far,
            r.pair_last,
            stage_part(columns, 2 * HD),
            r.pair_sems,
            1,
        ),
    )

    def up_terms(n):
        left = r.input_two[:, turn(n)]

        @tiles(inner, step)
        def _(q):
            part = mm_tn(left, r.grad_pre[:, pl.ds(q, step)])
            r.up[pl.ds(n * columns, columns), pl.ds(q, step)] = part.astype(LOW)

    def down_terms(n):
        right = r.grad_feed[:, turn(n)]

        @tiles(inner, step)
        def _(q):
            r.down[n, pl.ds(q, step), :] = mm_tn(r.hidden[:, pl.ds(q, step)], right).astype(LOW)

    def feed_terms(block):
        at = pl.ds(block * columns, columns)
        r.feed_own[:, at] = mm(r.hidden[...], r.down[block]).astype(LOW)

    def home_two(half, k):
        rows = line.at(half, k)
        unit, scaled = norm_of(r.middle[pl.ds(k * step_rows, step_rows), :])
        upstream = sum_two.total(half, k)
        note(r.early, 0, upstream * unit)
        note(r.early, 1, upstream)
        own = r.grad_feed[rows, :].astype(WIDE)
        note(r.early, 3, own)
        grad = own + norm_backward(upstream, unit, scaled, vector(3))
        r.grad_middle[pl.ds(k * step_rows, step_rows), :] = grad
        rounded = grad.astype(LOW)
        note(r.early, 2, rounded.astype(WIDE))
        r.grad_branch[rows, :] = rounded
        spread_branch.begin(half, k)

    tasks, late, held_first, held_second = [], [], [], []

    def flush_first():
        for one, k in held_first:
            one.add_first(k)
            late.append((one, k))
        del held_first[:]

    def first(one, k):
        flush_first()
        one.fetch_first(k)
        held_first.append((one, k))

    def flush_second():
        for one, k in held_second:
            one.add_second(k)
        del held_second[:]

    def fetch_second():
        flush_second()
        for one, k in late[:1]:
            one.fetch_second(k)
            held_second.append((one, k))
        del late[:1]

    def terms_and_start(work, n, one, which):
        work(n)
        one.start(which)

    def begin(one, terms):
        plan(terms_and_start, terms, 1, one, 0)
        plan(terms_and_start, terms, 3, one, 1)
        plan(terms, 2)
        plan(terms, 0)

    def plan(work, *given):
        tasks.append(functools.partial(work, *given))

    def work_on(count):
        for task in tasks[:count]:
            task()
        del tasks[:count]

    begin(sums.up, up_terms)
    for k in range(up_chunks):
        plan(first, sums.up, k)
    plan(flush_first)
    for block in range(fsdp):
        plan(feed_terms, block)
    begin(sums.down, down_terms)
    for k in range(down_chunks):
        plan(first, sums.down, k)
    plan(flush_first)

    loads.middle.wait()
    work_on(2)
    for copy in (loads.output, loads.queries, loads.pairs, loads.mixture):
        copy.wait()
    r.grad_pairs[...] = jnp.zeros_like(r.grad_pairs)

    def home_feed(half, k):
        rows = line.at(half, k)
        feed = sum_feed.total(half, k) + vector(5)
        total = r.middle[pl.ds(k * step_rows, step_rows), :] + feed
        slot = place * tokens + half * line.half + k * step_rows
        slots = slot + lax.broadcasted_iota(jnp.int32, (step_rows, width), 0)
        keep = jnp.where(slots < length, 1.0, 0.0)
        note(r.late, 2, keep * total * total)
        note(r.late, 4, keep * feed * feed)
        r.feed_own[rows, :] = (keep * total).astype(LOW)
        spread_result.begin(half, k, r.feed_own)

    def attend_share(start):
        rows = pl.ds(start, share)
        total = mm_nt(r.grad_branch[rows, pl.ds(0, columns)], r.output[0])
        for block in range(1, fsdp):
            total += mm_nt(r.grad_branch[rows, pl.ds(block * columns, columns)], r.output[block])
        r.grad_mixture[...] = total.astype(LOW)
        keys = r.pairs[:, pl.ds(0, HD)]
        values = r.pairs[:, pl.ds(HD, HD)]
        shape = (share, keys.shape[0])
        query_at = place * tokens + start + lax.broadcasted_iota(jnp.int32, shape, 0)
        key_at = lax.broadcasted_iota(jnp.int32, shape, 1)
        allowed = (key_at <= query_at) & (key_at < length)
        factor = 1.0 / math.sqrt(HD)
        for head in range(heads):
            at = pl.ds(head * HD, HD)
            query = r.queries[rows, at]
            grad_mix = r.grad_mixture[:, at]
            scores = jnp.where(allowed, mm_nt(query, keys) * factor, NEGATIVE)
            soft = jnp.exp(scores - r.log_total[rows, pl.ds(head, 1)])
            grad_soft = mm_nt(grad_mix, values)
            dot_rows = jnp.sum(soft * grad_soft, -1, keepdims=True)
            grad_scores = (soft * (grad_soft - dot_rows) * factor).astype(LOW)
            r.grad_queries[rows, at] = mm(grad_scores, keys).astype(LOW)
            r.grad_pairs[:, pl.ds(0, HD)] += mm_tn(grad_scores, query)
            r.grad_pairs[:, pl.ds(HD, HD)] += mm_tn(soft.astype(LOW), grad_mix)

    every = (TP, FSDP, CTX)
    sum_early = RowSum(r.early, r.early_came, r.row_sems.at[0], every)
    sum_late = RowSum(r.late, r.late_came, r.row_sems.at[1], every)
    sum_rows = RowSum(r.own, r.own_came, r.row_sems.at[2], (FSDP, CTX))
    flow_two = Flow(sum_two, spread_branch, home_two, LAG)
    flow_feed = Flow(sum_feed, spread_result, home_feed, LAG)
    starts = [half * line.half + group * share for group in range(tp // 2) for half in range(2)]
    per_share = share // step_rows
    for n in range(flow_two.steps):
        flow_two.advance(1)
        if n == flow_two.steps - 4:
            flow_feed.launch()
        work_on(1)
        if n % 3 == 1:
            flush_second()
        if n >= 6 and n % 3 == 0:
            fetch_second()
        group = tp // 2 - (len(starts) + 1) // 2
        if starts and n >= flow_two.ready((group + 1) * per_share - 1):
            attend_share(starts.pop(0))
    work_on(len(tasks))
    for start in starts:
        attend_share(start)
        flow_feed.advance(1)
    sum_early.start()
    loads.query.wait()
    loads.pair.wait()

    def pair_out(other):
        target = lax.rem(place + other, ctx)
        rows = pl.ds(pl.multiple_of(target * tokens, tokens), tokens)
        r.pair_sent[other - 1] = r.grad_pairs[rows, :].astype(LOW)
        return send(
            r.pair_sent.at[other - 1],
            r.pair_came.at[other - 1],
            r.pair_ctx_sem.at[0, other - 1],
            r.pair_ctx_sem.at[1, other - 1],
            CTX,
            target,
        )

    ctx_copies = [pair_out(other) for other in range(1, ctx)]
    for copy in ctx_copies:
        copy.start()
    sum_two.drain()

    def output_terms(n):
        terms = mm_tn(r.mixture[...], r.grad_branch[:, turn(n)])
        sums.output.piece(n, 0)[...] = terms.astype(LOW)

    def query_terms(n):
        terms = mm_tn(r.input_two[:, turn(n)], r.grad_queries[...])
        sums.query.piece(n, 0)[...] = terms.astype(LOW)

    def pair_terms(n):
        terms = mm_tn(r.input_two[:, turn(n)], r.pair_all[...].reshape(tokens, 2 * HD))
        r.pair_piece[n] = terms.astype(LOW)

    loads_one = pltpu.make_async_copy(r.input_one_hbm, r.input_two, r.load_sem.at[0])
    loads_one.start()
    begin(sums.output, output_terms)
    work_on(2)
    flow_feed.advance(1)
    for copy in ctx_copies:
        copy.wait()
    own_rows = pl.ds(pl.multiple_of(place * tokens, tokens), tokens)
    own_pairs = r.grad_pairs[own_rows, :]
    for other in range(1, ctx):
        own_pairs += r.pair_came[other - 1].astype(WIDE)
    r.pair_own[...] = own_pairs.astype(LOW).reshape(r.pair_own.shape)

    @tiles(width, step)
    def _(col):
        at = pl.ds(col, step)
        part = mm_nt(r.grad_queries[...], r.query[at, :])
        part += mm_nt(r.pair_own[...].reshape(tokens, 2 * HD), r.pair[at, :])
        r.sum_own[:, at] = part.astype(LOW)

    def pair_line(other):
        target = lax.rem(zone + other, tp)
        return send(
            r.pair_own.at[target],
            r.pair_terms.at[other - 1],
            r.pair_line_sem.at[0, other - 1],
            r.pair_line_sem.at[1, other - 1],
            TP,
            target,
        )

    def pair_spread(other):
        return send(
            r.pair_all.at[zone],
            r.pair_all.at[zone],
            r.pair_line_sem.at[2, other - 1],
            r.pair_line_sem.at[3, other - 1],
            TP,
            lax.rem(zone + other, tp),
        )

    def pair_begin():
        for other in range(1, tp):
            pair_line(other).start()
        r.own[pl.ds(1, 1), pl.ds(0, query_width)] = jnp.sum(
            r.grad_queries[...].astype(WIDE), 0, keepdims=True
        )

    def pair_shares():
        total = r.pair_own[zone].astype(WIDE)
        for other in range(1, tp):
            pair_line(other).wait_recv()
            total += r.pair_terms[other - 1].astype(WIDE)
        r.pair_all[zone] = total.astype(LOW)
        for other in range(1, tp):
            pair_spread(other).start()

    def pair_gathered():
        for other in range(1, tp):
            pair_spread(other).wait_recv()
        values = r.pair_all[...].reshape(tokens, 2 * HD)[:, HD:]
        r.own[pl.ds(2, 1), pl.ds(0, HD)] = jnp.sum(values.astype(WIDE), 0, keepdims=True)

    def home_one(half, k):
        rows = line.at(half, k)
        here = pl.ds(k * step_rows, step_rows)
        unit, scaled = norm_of(r.stream[here, :].astype(WIDE))
        upstream = sum_one.total(half, k)
        note(r.late, 0, upstream * unit)
        note(r.late, 1, upstream)
        grad = r.grad_middle[here, :] + norm_backward(upstream, unit, scaled, vector(0))
        r.sum_own[rows, :] = grad.astype(LOW)
        spread_stream.begin(half, k, r.sum_own)

    flow_one = Flow(sum_one, spread_stream, home_one, LAG)
    flow_one.launch()
    pair_begin()
    plan(loads_one.wait)
    begin(sums.query, query_terms)
    plan(pair_shares)
    plan(first, sums.output, 0)
    plan(first, sums.query, 0)
    plan(flush_first)
    plan(pair_gathered)
    begin(sums.pair, pair_terms)
    plan(first, sums.pair, 0)
    plan(flush_first)
    plan(sum_rows.start)
    loads.stream.wait()
    late_on = False
    for n in range(flow_one.steps):
        flow_one.advance(1)
        flow_feed.advance(1)
        work_on(1)
        if n % 3 == 1:
            fetch_second()
        if n % 3 == 2:
            flush_second()
        if n % 2 == 1:
            sum_early.move()
        sum_rows.move()
        if late_on:
            sum_late.move()
        elif flow_one.all_home() and flow_feed.all_home():
            sum_late.start()
            late_on = True
    work_on(len(tasks))
    flow_feed.advance(flow_feed.steps)
    if not late_on:
        sum_late.start()
    sum_early.finish()
    while late:
        fetch_second()
        flush_second()
        sum_rows.move()
        sum_late.move()
    flush_second()
    sum_rows.finish()
    sum_late.finish()
    mine = pl.ds(pl.multiple_of(me * columns, columns), columns)
    r.small[pl.ds(0, 4), :] = r.early[pl.ds(0, 4), mine]
    r.small[pl.ds(4, 2), :] = r.late[pl.ds(0, 2), mine]
    squares = jnp.sum(r.late[pl.ds(2, 3), pl.ds(0, width)], 1, keepdims=True)
    roots = jnp.sqrt(squares / (r.late[pl.ds(7, 1), pl.ds(0, 1)] * width))
    r.small[pl.ds(8, 3), :] = jnp.broadcast_to(roots, (3, columns))

    for half in range(2):

        @pl.when(line.is_home(half))
        def _():
            rows = pl.ds(half * line.half, line.half)
            copies = [
                pltpu.make_async_copy(r.feed_own.at[rows], r.result.at[rows], r.keep_sem.at[0]),
                pltpu.make_async_copy(r.sum_own.at[rows], r.stream_grad.at[rows], r.keep_sem.at[1]),
            ]
            for copy in copies:
                copy.start()
            for copy in copies:
                copy.wait()

    for one in (sum_feed, sum_one, spread_branch, spread_result, spread_stream):
        one.drain()
    for other in range(1, tp):
        pair_line(other).wait_send()
        pair_spread(other).wait_send()
    for one in vars(sums).values():
        one.finish()


def back(values, front_given):
    fsdp, ctx, tp = lax.axis_size(FSDP), lax.axis_size(CTX), lax.axis_size(TP)
    g = types.SimpleNamespace(**front_given)
    tokens, width = g.input_two.shape
    inner = g.up_all.shape[1]
    columns = width // fsdp
    share = tokens // tp
    query_width = g.queries.shape[1]
    pair_width = 2 * HD
    key_count = g.pairs.shape[0]
    dma = pltpu.SemaphoreType.DMA
    wide_row = max(width, inner)
    hops, tp_hops = len(bits_of(FSDP)) + len(bits_of(CTX)), len(bits_of(TP))
    far_outs = dict(
        result=((tokens, width), LOW),
        stream_grad=((tokens, width), LOW),
        up_last=((ctx, columns, inner), LOW),
        up_near=((2, columns, inner), LOW),
        up_far=((columns, inner), LOW),
        down_last=((ctx, inner, columns), LOW),
        down_near=((2, inner, columns), LOW),
        down_far=((inner, columns), LOW),
        output_last=((ctx, query_width, columns), LOW),
        output_near=((2, query_width, columns), LOW),
        output_far=((query_width, columns), LOW),
        query_last=((ctx, columns, query_width), LOW),
        query_near=((2, columns, query_width), LOW),
        query_far=((columns, query_width), LOW),
        pair_last=((ctx, columns, pair_width), LOW),
        pair_near=((2, columns, pair_width), LOW),
        pair_far=((columns, pair_width), LOW),
    )
    scratch = dict(
        up=pltpu.VMEM((width, inner), LOW),
        down=pltpu.VMEM((fsdp, inner, columns), LOW),
        input_two=pltpu.VMEM((tokens, width), LOW),
        grad_feed=pltpu.VMEM((tokens, width), LOW),
        hidden=pltpu.VMEM((tokens, inner), LOW),
        grad_pre=pltpu.VMEM((tokens, inner), LOW),
        work_one=pltpu.VMEM((tokens, columns), WIDE),
        work_two=pltpu.VMEM((tokens, columns), WIDE),
        sum_own=pltpu.VMEM((tokens, width), LOW),
        sum_slots=pltpu.VMEM((tokens, width), LOW),
        feed_own=pltpu.VMEM((tokens, width), LOW),
        feed_slots=pltpu.VMEM((tokens, width), LOW),
        grad_branch=pltpu.VMEM((tokens, width), LOW),
        middle=pltpu.VMEM((tokens // 2, width), WIDE),
        grad_middle=pltpu.VMEM((tokens // 2, width), WIDE),
        stream=pltpu.VMEM((tokens // 2, width), LOW),
        output=pltpu.VMEM((fsdp, query_width, columns), LOW),
        query=pltpu.VMEM((width, query_width), LOW),
        pair=pltpu.VMEM((width, pair_width), LOW),
        queries=pltpu.VMEM((tokens, query_width), LOW),
        pairs=pltpu.VMEM((key_count, pair_width), LOW),
        mixture=pltpu.VMEM((tokens, query_width), LOW),
        grad_mixture=pltpu.VMEM((share, query_width), LOW),
        grad_queries=pltpu.VMEM((tokens, query_width), LOW),
        grad_pairs=pltpu.VMEM((key_count, pair_width), WIDE),
        pair_sent=pltpu.VMEM((ctx - 1, tokens, pair_width), LOW),
        pair_came=pltpu.VMEM((ctx - 1, tokens, pair_width), LOW),
        pair_own=pltpu.VMEM((tp, share, pair_width), LOW),
        pair_terms=pltpu.VMEM((tp - 1, share, pair_width), LOW),
        pair_all=pltpu.VMEM((tp, share, pair_width), LOW),
        pair_piece=pltpu.VMEM((fsdp, columns, pair_width), LOW),
        stage_up=pltpu.VMEM((3, columns // 4, inner), LOW),
        stage_down=pltpu.VMEM((3, inner // 4, columns), LOW),
        weight_sem=dma((2, inner // columns)),
        load_sem=dma((10,)),
        early=pltpu.VMEM((8, wide_row), WIDE),
        late=pltpu.VMEM((8, wide_row), WIDE),
        early_came=pltpu.VMEM((hops + tp_hops, 8, wide_row), WIDE),
        late_came=pltpu.VMEM((hops + tp_hops, 8, wide_row), WIDE),
        own_came=pltpu.VMEM((hops, 8, wide_row), WIDE),
        row_sems=dma((3, 2, hops + tp_hops)),
        keep_sem=dma((2,)),
        pair_ctx_sem=dma((2, ctx - 1)),
        pair_line_sem=dma((4, tp - 1)),
        two_sems=line_sems(tokens),
        feed_sems=line_sems(tokens),
        one_sems=line_sems(tokens),
        branch_sems=line_sems(tokens),
        result_sems=line_sems(tokens),
        stream_sems=line_sems(tokens),
        up_sems=PieceSum.sems(4),
        down_sems=PieceSum.sems(4),
        output_sems=PieceSum.sems(1),
        query_sems=PieceSum.sems(1),
        pair_sems=PieceSum.sems(1),
    )
    if tokens != query_width or inner < width:
        scratch.update(output_piece=pltpu.VMEM((fsdp, query_width, columns), LOW))
    if tokens != columns or inner < fsdp * query_width:
        scratch.update(query_piece=pltpu.VMEM((fsdp, columns, query_width), LOW))
    return call_kernel(
        back_body,
        2,
        dict(
            input_two_hbm=g.input_two,
            cotangent_hbm=values.cotangent,
            up_hbm=g.up_all,
            down_hbm=g.down_all,
            output_hbm=g.output_all,
            queries_hbm=g.queries,
            pairs_hbm=g.pairs,
            mixture_hbm=g.mixture,
            query_hbm=g.query_all,
            pair_hbm=g.pair_all,
            middle_hbm=g.middle,
            stream_hbm=values.stream,
            input_one_hbm=g.input_one,
        ),
        dict(vectors=g.vectors, log_total=g.log_total, squares=g.squares),
        dict(lengths=values.lengths),
        far_outs,
        dict(small=((16, columns), WIDE), own=((8, wide_row), WIDE)),
        scratch,
    )


def body(
    stream,
    cotangent,
    lengths,
    first_gain,
    first_shift,
    query_weight,
    query_bias,
    pair_weight,
    value_bias,
    output_weight,
    output_bias,
    second_gain,
    second_shift,
    up_weight,
    up_bias,
    down_weight,
    down_bias,
):
    fsdp = lax.axis_size(FSDP)
    me = lax.axis_index(FSDP)
    seq_count, group_len, width = stream.shape
    tokens = seq_count * group_len
    columns, inner = first_gain.shape[0], up_weight.shape[1]

    def placed(bias):
        spots = jnp.arange(fsdp)[None, :, None] == me
        return jnp.where(spots, bias.reshape(-1, 1, bias.shape[-1]).astype(WIDE), 0.0).reshape(-1)

    def row(values):
        return jnp.pad(values.astype(WIDE), (0, columns - values.shape[0]))[None]

    vectors = (first_gain, first_shift, output_bias, second_gain, second_shift, down_bias)
    packed = jnp.concatenate(
        [row(vector) for vector in vectors]
        + [row(placed(query_bias)), row(placed(value_bias.reshape(1, -1)))]
        + [placed(up_bias).reshape(-1, columns)]
    )
    packed = jnp.pad(packed, ((0, -packed.shape[0] % 8), (0, 0)))
    values = types.SimpleNamespace(
        stream=stream.reshape(tokens, width),
        cotangent=cotangent.reshape(tokens, width),
        lengths=lengths,
        packed=packed,
        query=query_weight,
        pair=pair_weight,
        output=output_weight,
        up=up_weight,
        down=down_weight,
    )
    given = front(values, tokens)
    ended = types.SimpleNamespace(**back(values, given))
    small, own = ended.small, ended.own
    query_width = query_weight.shape[1]

    def finished(last):
        return jnp.sum(last.astype(WIDE), 0)

    up_bias_all = own[0, :inner].reshape(up_bias.shape[0], fsdp, -1)
    query_bias_all = own[1, :query_width].reshape(query_bias.shape[0], fsdp, -1)
    value_size = value_bias.shape[0]
    return (
        ended.result.reshape(stream.shape),
        ended.stream_grad.reshape(stream.shape),
        small[4],
        small[5],
        finished(ended.query_last),
        lax.dynamic_index_in_dim(query_bias_all, me, 1, False),
        finished(ended.pair_last),
        lax.dynamic_slice_in_dim(own[2], me * value_size, value_size, 0),
        finished(ended.output_last),
        small[2],
        small[0],
        small[1],
        finished(ended.up_last),
        lax.dynamic_index_in_dim(up_bias_all, me, 1, False),
        finished(ended.down_last),
        small[3],
        small[8:11, 0],
    )


def solution(mesh):
    in_specs = (
        P(FSDP, CTX, None),
        P(FSDP, CTX, None),
        P(FSDP),
        P(FSDP),
        P(FSDP),
        P(FSDP, TP),
        P(TP, FSDP),
        P(FSDP, None),
        P(FSDP),
        P(TP, FSDP),
        P(FSDP),
        P(FSDP),
        P(FSDP),
        P(FSDP, TP),
        P(TP, FSDP),
        P(TP, FSDP),
        P(FSDP),
    )
    out_specs = (
        P(FSDP, CTX, None),
        P(FSDP, CTX, None),
        P(FSDP),
        P(FSDP),
        P(FSDP, TP),
        P(TP, FSDP),
        P(FSDP, None),
        P(FSDP),
        P(TP, FSDP),
        P(FSDP),
        P(FSDP),
        P(FSDP),
        P(FSDP, TP),
        P(TP, FSDP),
        P(TP, FSDP),
        P(FSDP),
        P(),
    )
    return jax.shard_map(body, mesh=mesh, in_specs=in_specs, out_specs=out_specs, check_vma=False)
```

```python
import functools
import math
import types

import jax
import jax.numpy as jnp
from jax import lax
from jax.experimental import pallas as pl
from jax.experimental.pallas import tpu as pltpu
from jax.sharding import PartitionSpec as P

HD = 128
EPSILON = 1e-05
NEGATIVE = -1e30
FSDP, CTX, TP = "fsdp", "ctx", "tp"
LOW, WIDE = jnp.bfloat16, jnp.float32
MESH = pl.DeviceIdType.MESH
VMEM_BYTES = 60 << 20
SKEW, LAG = 2, 2


def flip(place, bit):
    return place + bit - 2 * bit * lax.rem(lax.div(place, bit), 2)


def bits_of(axis):
    count, bit, found = lax.axis_size(axis), 1, []
    while bit < count:
        found.append(bit)
        bit *= 2
    return found


def mm(left, right):
    return jnp.dot(left, right, preferred_element_type=WIDE)


def mm_nt(left, right):
    return lax.dot_general(left, right, (((1,), (1,)), ((), ())), preferred_element_type=WIDE)


def mm_tn(left, right):
    return lax.dot_general(left, right, (((0,), (0,)), ((), ())), preferred_element_type=WIDE)


def tiles(count, step):
    def run(work):
        def once(index, carry):
            work(pl.multiple_of(index * step, step))
            return carry

        lax.fori_loop(0, count // step, once, 0)

    return run


def norm_of(values):
    center = values - jnp.mean(values, -1, keepdims=True)
    scaled = lax.rsqrt(jnp.mean(center * center, -1, keepdims=True) + EPSILON)
    return center * scaled, scaled


def norm_backward(upstream, unit_rows, scaled, norm_gain):
    gained = upstream * norm_gain
    return scaled * (
        gained
        - jnp.mean(gained, -1, keepdims=True)
        - unit_rows * jnp.mean(gained * unit_rows, -1, keepdims=True)
    )


def send(source, target, outgo, income, axis, place):
    return pltpu.make_async_remote_copy(
        src_ref=source,
        dst_ref=target,
        send_sem=outgo,
        recv_sem=income,
        device_id={axis: place},
        device_id_type=MESH,
    )


def all_peers():
    me, place, zone = lax.axis_index(FSDP), lax.axis_index(CTX), lax.axis_index(TP)
    ctx, tp = lax.axis_size(CTX), lax.axis_size(TP)
    peers = [(FSDP, flip(me, 1)), (FSDP, flip(me, 2)), (FSDP, flip(flip(me, 1), 2))]
    peers += [(CTX, lax.rem(place + k, ctx)) for k in range(1, ctx)]
    peers += [(TP, lax.rem(zone + k, tp)) for k in range(1, tp)]
    return peers


def greet(peers):
    barrier = pltpu.get_barrier_semaphore()
    for axis, place in peers:
        pl.semaphore_signal(barrier, inc=1, device_id={axis: place}, device_id_type=MESH)
    return lambda: pl.semaphore_wait(barrier, len(peers))


def split_rows(tokens):
    rows = 32 if tokens % 512 == 0 else 16
    return rows, tokens // 2 // rows


class Line:
    def __init__(self, tokens):
        self.place, self.count = lax.axis_index(TP), lax.axis_size(TP)
        self.rows, self.chunks = split_rows(tokens)
        self.half = tokens // 2

    def at(self, half, k):
        start = half * self.half + k * self.rows
        return pl.ds(start if isinstance(start, int) else pl.multiple_of(start, self.rows), self.rows)

    def is_home(self, half):
        return self.place == (0 if half == 0 else self.count - 1)

    def is_far(self, half):
        return self.place == (self.count - 1 if half == 0 else 0)

    def toward(self, half):
        move = self.count - 1 if half == 0 else 1
        return lax.rem(self.place + move, self.count)

    def away(self, half):
        return self.toward(1 - half)


class LineSum(Line):
    def __init__(self, own, slots, sems):
        super().__init__(own.shape[0])
        self.own, self.slots = own, slots
        self.outgo, self.income = sems

    def copy(self, half, k):
        rows = self.at(half, k)
        return send(
            self.own.at[rows],
            self.slots.at[rows],
            self.outgo.at[half, k],
            self.income.at[half, k],
            TP,
            self.toward(half),
        )

    def launch(self, half, first=0, last=None):
        @pl.when(self.is_far(half))
        def _():
            for k in range(first, self.chunks if last is None else last):
                self.copy(half, k).start()

    def total(self, half, k):
        rows = self.at(half, k)
        return self.own[rows, :].astype(WIDE) + self.slots[rows, :].astype(WIDE)

    def pass_on(self, half, k):
        self.copy(half, k).wait_recv()
        self.own[self.at(half, k), :] = self.total(half, k).astype(LOW)
        self.copy(half, k).start()

    def drain(self):
        for half in range(2):

            @pl.when(jnp.logical_not(self.is_home(half)))
            def _():
                for k in range(self.chunks):
                    self.copy(half, k).wait_send()


class LineSpread(Line):
    def __init__(self, held, sems):
        super().__init__(held.shape[0])
        self.held = held
        self.outgo, self.income = sems

    def copy(self, half, k, source=None):
        rows = self.at(half, k)
        return send(
            self.held.at[rows] if source is None else source.at[rows],
            self.held.at[rows],
            self.outgo.at[half, k],
            self.income.at[half, k],
            TP,
            self.away(half),
        )

    def begin(self, half, k, source=None):
        self.copy(half, k, source).start()

    def serve(self, half, k):
        self.copy(half, k).wait_recv()

        @pl.when(jnp.logical_not(self.is_far(half)))
        def _():
            self.copy(half, k).start()

    def drain(self):
        for half in range(2):

            @pl.when(jnp.logical_not(self.is_far(half)))
            def _():
                for k in range(self.chunks):
                    self.copy(half, k).wait_send()


class Flow(Line):
    def __init__(self, line_sum, spread, home, lag):
        super().__init__(line_sum.own.shape[0])
        self.sum, self.spread, self.home, self.lag = line_sum, spread, home, lag
        self.now = 0
        self.to_home = SKEW * (self.count - 2)
        self.steps = self.chunks + lag + 2 * self.to_home

    def launch(self, first=0, last=None):
        for half in range(2):
            self.sum.launch(half, first, last)

    def inside(self, k):
        return (k >= 0) & (k < self.chunks)

    def advance(self, count=1):
        for n in range(self.now, min(self.now + count, self.steps)):
            self.step(n)
        self.now = min(self.now + count, self.steps)

    def step(self, n):
        last = self.count - 1
        at_home = n - self.to_home
        for half in range(2):
            hops = last - self.place if half == 0 else self.place
            k = n - SKEW * (hops - 1)

            @pl.when((hops >= 1) & (hops < last) & self.inside(k))
            def _():
                self.sum.pass_on(half, k)

            if 0 <= at_home < self.chunks:

                @pl.when(self.is_home(half))
                def _():
                    self.sum.copy(half, at_home).wait_recv()
                    self.home(half, at_home)

        for half in range(2):
            hops = self.place if half == 0 else last - self.place
            k = at_home - self.lag - SKEW * (hops - 1)

            @pl.when((hops >= 1) & self.inside(k))
            def _():
                self.spread.serve(half, k)

    def all_home(self):
        return self.now >= self.chunks + self.to_home

    def ready(self, chunk):
        return chunk + self.lag + 2 * self.to_home


class Gather:
    def __init__(self, shard, held, sems, cut):
        self.shard, self.held = shard, held
        self.me, self.place = lax.axis_index(FSDP), lax.axis_index(CTX)
        self.ctx = lax.axis_size(CTX)
        self.cut = cut
        self.rows = shard.shape[0] // self.ctx // cut
        self.near_sem, self.far_sem, self.side_sem, self.pass_sem, self.local = sems

    def part(self, place, k):
        return pl.ds(pl.multiple_of((place * self.cut + k) * self.rows, self.rows), self.rows)

    def keep(self):
        every = pl.ds(0, self.shard.shape[0])
        return pltpu.make_async_copy(self.shard, self.held(self.me, every), self.local.at[0])

    def near(self):
        every = pl.ds(0, self.shard.shape[0])
        return send(
            self.shard,
            self.held(self.me, every),
            self.near_sem.at[0],
            self.near_sem.at[1],
            FSDP,
            flip(self.me, 1),
        )

    def far(self, k):
        part = self.part(self.place, k)
        return send(
            self.shard.at[part],
            self.held(self.me, part),
            self.far_sem.at[0, k],
            self.far_sem.at[1, k],
            FSDP,
            flip(self.me, 2),
        )

    def side(self, other, k):
        held = self.held(flip(self.me, 2), self.part(self.place, k))
        return send(
            held,
            held,
            self.side_sem.at[0, other - 1, k],
            self.side_sem.at[1, other - 1, k],
            CTX,
            lax.rem(self.place + other, self.ctx),
        )

    def over(self, other, k):
        place = lax.rem(self.place + self.ctx - other, self.ctx)
        held = self.held(flip(self.me, 2), self.part(place, k))
        return send(
            held,
            held,
            self.pass_sem.at[0, other, k],
            self.pass_sem.at[1, other, k],
            FSDP,
            flip(self.me, 1),
        )

    def start(self):
        for k in range(self.cut):
            self.far(k).start()
        self.near().start()
        self.keep().start()

    def cross(self, k):
        self.far(k).wait_recv()
        for other in range(1, self.ctx):
            self.side(other, k).start()
        self.over(0, k).start()

    def pass_on(self, k):
        for other in range(1, self.ctx):
            self.side(other, k).wait_recv()
            self.over(other, k).start()

    def ready(self):
        self.keep().wait()
        self.near().wait_recv()
        for k in range(self.cut):
            for other in range(self.ctx):
                self.over(other, k).wait_recv()

    def drain(self):
        self.near().wait_send()
        for k in range(self.cut):
            self.far(k).wait_send()
            for other in range(self.ctx):
                self.over(other, k).wait_send()
                if other > 0:
                    self.side(other, k).wait_send()

    @staticmethod
    def sems(cut):
        ctx = lax.axis_size(CTX)
        shapes = ((2,), (2, cut), (2, ctx - 1, cut), (2, ctx, cut), (1,))
        return tuple(pltpu.SemaphoreType.DMA(shape) for shape in shapes)


class PieceSum:
    def __init__(self, piece, near, far, last, stages, sems, chunks):
        self.piece, self.near, self.far, self.last = piece, near, far, last
        self.stages, self.chunks = stages, chunks
        self.rows = far.shape[0] // chunks
        self.near_sem, self.far_sem, self.last_sem, self.local = sems
        self.me, self.place = lax.axis_index(FSDP), lax.axis_index(CTX)
        self.ctx = lax.axis_size(CTX)

    def part(self, k):
        return pl.ds(k * self.rows, self.rows)

    def near_copy(self, which, k):
        return send(
            self.piece(2 * which + 1, k),
            self.near.at[which, self.part(k)],
            self.near_sem.at[0, which, k],
            self.near_sem.at[1, which, k],
            FSDP,
            flip(self.me, 1),
        )

    def far_copy(self, k):
        return send(
            self.piece(2, k),
            self.far.at[self.part(k)],
            self.far_sem.at[0, k],
            self.far_sem.at[1, k],
            FSDP,
            flip(self.me, 2),
        )

    def last_copy(self, other, k):
        return send(
            self.piece(0, k),
            self.last.at[self.place, self.part(k)],
            self.last_sem.at[0, other - 1, k],
            self.last_sem.at[1, other - 1, k],
            CTX,
            lax.rem(self.place + other, self.ctx),
        )

    def own_copy(self, k):
        return pltpu.make_async_copy(
            self.piece(0, k), self.last.at[self.place, self.part(k)], self.local.at[3 + k]
        )

    def start(self, which):
        for k in range(self.chunks):
            self.near_copy(which, k).start()

    def load(self, source, index):
        return pltpu.make_async_copy(source, self.stages[index], self.local.at[index])

    def add(self, r, k, index):
        step = 32 if self.rows % 32 == 0 else 16
        piece, stage = self.piece(r, k), self.stages[index]

        @tiles(self.rows, step)
        def _(at):
            here = pl.ds(at, step)
            total = piece[here].astype(WIDE) + stage[here].astype(WIDE)
            piece[here] = total.astype(LOW)

    def fetch_first(self, k):
        for which in range(2):
            self.near_copy(which, k).wait_recv()
        for which in range(2):
            self.load(self.near.at[which, self.part(k)], which).start()

    def add_first(self, k):
        self.load(self.near.at[1, self.part(k)], 1).wait()
        self.add(2, k, 1)
        self.far_copy(k).start()
        self.load(self.near.at[0, self.part(k)], 0).wait()
        self.add(0, k, 0)

    def fetch_second(self, k):
        self.far_copy(k).wait_recv()
        self.load(self.far.at[self.part(k)], 2).start()

    def add_second(self, k):
        self.load(self.far.at[self.part(k)], 2).wait()
        self.add(0, k, 2)
        for other in range(1, self.ctx):
            self.last_copy(other, k).start()
        self.own_copy(k).start()

    def finish(self):
        for k in range(self.chunks):
            for other in range(1, self.ctx):
                self.last_copy(other, k).wait_recv()
                self.last_copy(other, k).wait_send()
            self.own_copy(k).wait()
            self.far_copy(k).wait_send()
            for which in range(2):
                self.near_copy(which, k).wait_send()

    @staticmethod
    def sems(chunks):
        ctx = lax.axis_size(CTX)
        shapes = ((2, 2, chunks), (2, chunks), (2, ctx - 1, chunks), (3 + chunks,))
        return tuple(pltpu.SemaphoreType.DMA(shape) for shape in shapes)


class RowSum:
    def __init__(self, rows, came, sems, axes):
        self.rows, self.came, self.sems = rows, came, sems
        self.hops = [(axis, bit) for axis in axes for bit in bits_of(axis)]
        self.now = len(self.hops)

    def copy(self, n):
        axis, bit = self.hops[n]
        return send(
            self.rows,
            self.came.at[n],
            self.sems.at[0, n],
            self.sems.at[1, n],
            axis,
            flip(lax.axis_index(axis), bit),
        )

    def start(self):
        self.now = 0
        self.copy(0).start()

    def move(self):
        if self.now == len(self.hops):
            return False
        self.copy(self.now).wait()
        self.rows[...] += self.came[self.now]
        self.now += 1
        if self.now < len(self.hops):
            self.copy(self.now).start()
        return True

    def finish(self):
        while self.move():
            pass


def line_sems(tokens):
    rows, chunks = split_rows(tokens)
    return tuple(pltpu.SemaphoreType.DMA((2, chunks)) for _ in range(2))


def call_kernel(body, ident, far, near, scalars, far_outs, near_outs, scratch):
    groups = (far, near, scalars)
    spaces = (pl.ANY, pltpu.VMEM, pltpu.SMEM)
    arrays, in_specs = [], []
    for group, space in zip(groups, spaces):
        arrays += list(group.values())
        in_specs += [pl.BlockSpec(memory_space=space)] * len(group)
    outs = dict(far_outs, **near_outs)
    out_specs = [pl.BlockSpec(memory_space=pl.ANY)] * len(far_outs)
    out_specs += [pl.BlockSpec(memory_space=pltpu.VMEM)] * len(near_outs)
    shapes, tree = jax.tree.flatten(scratch)
    ins = [name for group in groups for name in group]

    def kernel(*refs):
        held = dict(zip(ins + list(outs), refs))
        held.update(jax.tree.unflatten(tree, refs[len(ins) + len(outs) :]))
        body(types.SimpleNamespace(**held))

    given = pl.pallas_call(
        kernel,
        out_shape=[jax.ShapeDtypeStruct(shape, kind) for shape, kind in outs.values()],
        in_specs=in_specs,
        out_specs=out_specs,
        scratch_shapes=shapes,
        compiler_params=pltpu.CompilerParams(
            collective_id=ident, has_side_effects=True, vmem_limit_bytes=VMEM_BYTES
        ),
    )(*arrays)
    return dict(zip(outs, given))


def front_part(r):
    me, place, zone = lax.axis_index(FSDP), lax.axis_index(CTX), lax.axis_index(TP)
    fsdp, ctx, tp = lax.axis_size(FSDP), lax.axis_size(CTX), lax.axis_size(TP)
    tokens, width = r.stream_hbm.shape
    columns = width // fsdp
    query_width = r.query.shape[1]
    heads = query_width // HD
    inner = r.up.shape[1]
    length = r.lengths[0]
    line = Line(tokens)
    step_rows, chunks = line.rows, line.chunks

    ready = greet(all_peers())
    stream_load = pltpu.make_async_copy(r.stream_hbm, r.feed_own, r.load_sem.at[0])
    stream_load.start()
    cotangent_load = pltpu.make_async_copy(r.cotangent_hbm, r.grad_feed, r.load_sem.at[1])
    cotangent_load.start()

    def block_rows(held):
        size = held.shape[0] // fsdp

        def view(block, rows):
            start = pl.multiple_of(block * size + rows.start, 16)
            return held.at[pl.ds(start, rows.size)]

        return view

    gathers = types.SimpleNamespace(
        query=Gather(r.query_shard, block_rows(r.query), r.query_gather, r.query_gather[1].shape[1]),
        pair=Gather(r.pair_shard, block_rows(r.pair), r.pair_gather, r.pair_gather[1].shape[1]),
        output=Gather(r.output_shard, lambda b, rows: r.output.at[b, rows], r.output_gather, r.output_gather[1].shape[1]),
        up=Gather(r.up_shard, block_rows(r.up), r.up_gather, r.up_gather[1].shape[1]),
        down=Gather(
            r.down_shard, lambda b, rows: r.down.at[b, rows], r.down_gather, r.down_gather[1].shape[1]
        ),
    )

    def small_copy(k):
        target = flip(me, k) if k < 3 else flip(flip(me, 1), 2)
        return send(
            r.smalls.at[0], r.smalls.at[k], r.small_sem.at[0, k - 1], r.small_sem.at[1, k - 1],
            FSDP, target,
        )

    r.smalls[0] = r.packed[...]
    ready()
    for k in range(1, fsdp):
        small_copy(k).start()
    gathers.pair.start()
    gathers.query.start()
    for k in range(1, fsdp):
        small_copy(k).wait()
    query_add = jnp.zeros((1, query_width), WIDE)
    value_add = jnp.zeros((1, HD), WIDE)
    for k in range(fsdp):
        block = me if k == 0 else flip(me, k) if k < 3 else flip(flip(me, 1), 2)
        at = pl.ds(pl.multiple_of(block * columns, columns), columns)
        r.vectors[pl.ds(0, 6), at] = r.smalls[k, pl.ds(0, 6), :]
        query_add += r.smalls[k, pl.ds(6, 1), pl.ds(0, query_width)]
        value_add += r.smalls[k, pl.ds(7, 1), pl.ds(0, HD)]
    for q in range(inner // columns):
        total = jnp.zeros((1, columns), WIDE)
        for k in range(fsdp):
            total += r.smalls[k, pl.ds(8 + q, 1), :]
        r.vectors[pl.ds(6, 1), pl.ds(q * columns, columns)] = total
    r.vectors[pl.ds(7, 1), :] = jnp.zeros((1, r.vectors.shape[1]), WIDE)

    def vector(n):
        return r.vectors[pl.ds(n, 1), pl.ds(0, width)]

    stream_load.wait()
    norm_step = min(32, tokens)

    @tiles(tokens, norm_step)
    def _(row):
        rows = pl.ds(row, norm_step)
        unit, scaled = norm_of(r.feed_own[rows, :].astype(WIDE))
        r.grad_branch[rows, :] = (unit * vector(0) + vector(1)).astype(LOW)

    early = (gathers.pair, gathers.query)
    for k in range(2):
        for one in early:
            one.cross(k)
    for k in range(2):
        for one in early:
            one.pass_on(k)
    for one in (gathers.output, gathers.up, gathers.down):
        one.start()
    gathers.pair.ready()
    own_rows = pl.ds(pl.multiple_of(place * tokens, tokens), tokens)
    key_half = mm(r.grad_branch[...], r.pair[...])
    r.pairs[own_rows, pl.ds(0, HD)] = key_half[:, :HD].astype(LOW)
    r.pairs[own_rows, pl.ds(HD, HD)] = (key_half[:, HD:] + value_add).astype(LOW)

    def pair_copy(other):
        return send(
            r.pairs.at[own_rows],
            r.pairs.at[own_rows],
            r.exchange_sem.at[0, other - 1],
            r.exchange_sem.at[1, other - 1],
            CTX,
            lax.rem(place + other, ctx),
        )

    for other in range(1, ctx):
        pair_copy(other).start()
    gathers.query.ready()
    r.queries[...] = (mm(r.grad_branch[...], r.query[...]) + query_add).astype(LOW)
    input_save = pltpu.make_async_copy(r.grad_branch, r.input_one_hbm, r.load_sem.at[2])
    input_save.start()
    gathers.output.cross(0)
    cotangent_load.wait()

    @tiles(tokens, step_rows)
    def _(row):
        rows = pl.ds(row, step_rows)
        slots = place * tokens + row + lax.broadcasted_iota(jnp.int32, (step_rows, width), 0)
        keep = jnp.where(slots < length, 1.0, 0.0)
        r.grad_feed[rows, :] = (keep * r.grad_feed[rows, :].astype(WIDE)).astype(LOW)

    for other in range(1, ctx):
        pair_copy(other).wait_recv()
    gathers.output.pass_on(0)

    share = min(HD, line.half)
    per_share = share // step_rows
    factor = 1.0 / math.sqrt(HD)

    def attend(start):
        rows = pl.ds(start, share)
        keys = r.pairs[:, pl.ds(0, HD)]
        values = r.pairs[:, pl.ds(HD, HD)]
        shape = (share, keys.shape[0])
        query_at = place * tokens + start + lax.broadcasted_iota(jnp.int32, shape, 0)
        key_at = lax.broadcasted_iota(jnp.int32, shape, 1)
        allowed = (key_at <= query_at) & (key_at < length)
        for head in range(heads):
            at = pl.ds(head * HD, HD)
            scores = jnp.where(allowed, mm_nt(r.queries[rows, at], keys) * factor, NEGATIVE)
            peak = jnp.max(scores, -1, keepdims=True)
            soft = jnp.exp(scores - peak)
            total = jnp.sum(soft, -1, keepdims=True)
            r.mixture[rows, at] = mm((soft / total).astype(LOW), values).astype(LOW)
            r.log_total[rows, pl.ds(head, 1)] = peak + jnp.log(total)

    def project(start):
        rows = pl.ds(start, share)
        for block in range(fsdp):
            at = pl.ds(block * columns, columns)
            r.sum_own[rows, at] = mm(r.mixture[rows, :], r.output[block]).astype(LOW)

    branch_sum = LineSum(r.sum_own, r.sum_slots, r.front_sems)
    spread = LineSpread(r.input_two, r.spread_sems)
    r.squares[...] = jnp.zeros_like(r.squares)

    def home(half, k):
        branch = branch_sum.total(half, k) + vector(2)
        middle = r.feed_own[line.at(half, k), :].astype(WIDE) + branch
        r.middle[pl.ds(k * step_rows, step_rows), :] = middle
        unit, scaled = norm_of(middle)
        r.input_two[line.at(half, k), :] = (unit * vector(3) + vector(4)).astype(LOW)
        spread.begin(half, k)
        slot = place * tokens + half * line.half + k * step_rows
        slots = slot + lax.broadcasted_iota(jnp.int32, (step_rows, width), 0)
        keep = jnp.where(slots < length, 1.0, 0.0)
        r.squares[...] += jnp.sum(keep * branch * branch, 0, keepdims=True)

    big = [(gathers.up, k) for k in range(gathers.up.cut)]
    big += [(gathers.down, k) for k in range(gathers.down.cut)]
    events = []
    for index, (one, k) in enumerate(big):
        events.append(functools.partial(one.cross, k))
        if index > 0:
            before, last = big[index - 1]
            events.append(functools.partial(before.pass_on, last))
    events.append(functools.partial(big[-1][0].pass_on, big[-1][1]))

    def move_on(count):
        for event in events[:count]:
            event()
        del events[:count]

    flow = Flow(branch_sum, spread, home, LAG)
    groups = line.half // share
    for group in range(groups):
        for half in range(2):
            start = half * line.half + group * share
            attend(start)
            if group == 0 and half == 0:
                gathers.output.ready()
            project(start)
        flow.launch(per_share * group, per_share * group + per_share)
        if group < groups - 1:
            flow.advance(1)
            move_on(1)
    while flow.now < flow.steps:
        flow.advance(1)
        if flow.now % 2 == 0:
            move_on(1)
    move_on(len(events))
    input_save.wait()
    branch_sum.drain()

    def end():
        for other in range(1, ctx):
            pair_copy(other).wait_send()
        for one in vars(gathers).values():
            one.drain()
        spread.drain()

    return gathers, end


def layer_body(r):
    gathers, front_end = front_part(r)
    back_part(r, gathers, front_end)


def back_part(r, gathers, front_end):
    me, place, zone = lax.axis_index(FSDP), lax.axis_index(CTX), lax.axis_index(TP)
    fsdp, ctx, tp = lax.axis_size(FSDP), lax.axis_size(CTX), lax.axis_size(TP)
    tokens, width = r.input_two.shape
    inner = r.up.shape[1]
    columns = width // fsdp
    share = tokens // tp
    query_width = r.queries.shape[1]
    heads = query_width // HD
    length = r.lengths[0]
    line = Line(tokens)
    step_rows, chunks = line.rows, line.chunks
    step = columns
    blocks = inner // step

    at_end = jnp.where(zone == tp - 1, tokens // 2, 0)
    stream_part = r.stream_hbm.at[pl.ds(pl.multiple_of(at_end, tokens // 2), tokens // 2)]
    stream_load = pltpu.make_async_copy(stream_part, r.stream, r.load_sem.at[0])
    stream_load.start()
    for rows in (r.early, r.late, r.own):
        rows[...] = jnp.zeros_like(rows)
    r.late[pl.ds(3, 1), pl.ds(0, width)] = r.squares[...]
    counted = jnp.clip(length - place * tokens, 0, tokens).astype(WIDE)
    r.late[pl.ds(7, 1), :] = jnp.full((1, r.late.shape[1]), jnp.where(zone == 0, counted, 0.0))
    def vector(n):
        return r.vectors[pl.ds(n, 1), pl.ds(0, width)]

    def note(rows, row, values):
        rows[pl.ds(row, 1), pl.ds(0, width)] += jnp.sum(values, 0, keepdims=True)

    gathers.up.ready()
    gathers.down.ready()

    @tiles(inner, step)
    def _(q):
        at = pl.ds(q, step)
        r.work_one[...] = mm(r.input_two[...], r.up[:, at])
        total = mm_nt(r.grad_feed[:, pl.ds(0, columns)], r.down[0, at, :])
        for block in range(1, fsdp):
            total += mm_nt(r.grad_feed[:, pl.ds(block * columns, columns)], r.down[block, at, :])
        r.work_two[...] = total
        bias = r.vectors[pl.ds(6, 1), at]

        @tiles(tokens, 32)
        def _(row):
            here = pl.ds(row, 32)
            v = r.work_one[here, :] + bias
            square = v * v
            reach = math.sqrt(2.0 / math.pi)
            t = jnp.tanh(reach * v * (1.0 + 0.044715 * square))
            gate = 0.5 * (1.0 + t)
            slope = gate + 0.5 * v * (1.0 - t * t) * reach * (1.0 + 3 * 0.044715 * square)
            r.hidden[here, at] = (v * gate).astype(LOW)
            grad = (r.work_two[here, :] * slope).astype(LOW)
            r.grad_pre[here, at] = grad
            r.own[pl.ds(0, 1), at] += jnp.sum(grad.astype(WIDE), 0, keepdims=True)

    front_end()
    sum_two = LineSum(r.sum_own, r.sum_slots, r.two_sems)
    sum_feed = LineSum(r.feed_own, r.feed_slots, r.feed_sems)
    sum_one = LineSum(r.sum_own, r.sum_slots, r.one_sems)
    spread_branch = LineSpread(r.grad_branch, r.branch_sems)
    spread_result = LineSpread(r.result, r.result_sems)
    spread_stream = LineSpread(r.stream_grad, r.stream_sems)

    @tiles(width, step)
    def _(col):
        at = pl.ds(col, step)
        r.sum_own[:, at] = mm_nt(r.grad_pre[...], r.up[at, :]).astype(LOW)

    for half in range(2):
        sum_two.launch(half)

    def turn(n):
        target = me
        for bit in (1, 2):
            if n & bit:
                target = flip(target, bit)
        return pl.ds(pl.multiple_of(target * columns, columns), columns)

    up_chunks, down_chunks = r.up_sems[1].shape[1], r.down_sems[1].shape[1]
    up_rows, down_rows = columns // up_chunks, inner // down_chunks

    def whole_piece(held, kept, size):
        if held is not None:
            return lambda n, k: held.at[n]
        return lambda n, k: kept.at[:, pl.ds(n * size, size)]

    def stage_part(rows, size):
        return [r.stage_down.at[n, pl.ds(0, rows), pl.ds(0, size)] for n in range(3)]

    sums = types.SimpleNamespace(
        up=PieceSum(
            lambda n, k: r.up.at[pl.ds(n * columns + k * up_rows, up_rows)],
            r.up_near,
            r.up_far,
            r.up_last,
            [r.stage_up.at[n] for n in range(3)],
            r.up_sems,
            up_chunks,
        ),
        down=PieceSum(
            lambda n, k: r.down.at[n, pl.ds(k * down_rows, down_rows)],
            r.down_near,
            r.down_far,
            r.down_last,
            [r.stage_down.at[n] for n in range(3)],
            r.down_sems,
            down_chunks,
        ),
        output=PieceSum(
            whole_piece(getattr(r, "output_piece", None), r.grad_pre, columns),
            r.output_near,
            r.output_far,
            r.output_last,
            stage_part(query_width, columns),
            r.output_sems,
            1,
        ),
        query=PieceSum(
            whole_piece(getattr(r, "query_piece", None), r.hidden, query_width),
            r.query_near,
            r.query_far,
            r.query_last,
            stage_part(columns, query_width),
            r.query_sems,
            1,
        ),
        pair=PieceSum(
            lambda n, k: r.pair_piece.at[n],
            r.pair_near,
            r.pair_far,
            r.pair_last,
            stage_part(columns, 2 * HD),
            r.pair_sems,
            1,
        ),
    )

    def up_terms(n):
        left = r.input_two[:, turn(n)]

        @tiles(inner, step)
        def _(q):
            part = mm_tn(left, r.grad_pre[:, pl.ds(q, step)])
            r.up[pl.ds(n * columns, columns), pl.ds(q, step)] = part.astype(LOW)

    def down_terms(n):
        right = r.grad_feed[:, turn(n)]

        @tiles(inner, step)
        def _(q):
            r.down[n, pl.ds(q, step), :] = mm_tn(r.hidden[:, pl.ds(q, step)], right).astype(LOW)

    def feed_terms(block):
        at = pl.ds(block * columns, columns)
        r.feed_own[:, at] = mm(r.hidden[...], r.down[block]).astype(LOW)

    def home_two(half, k):
        rows = line.at(half, k)
        unit, scaled = norm_of(r.middle[pl.ds(k * step_rows, step_rows), :])
        upstream = sum_two.total(half, k)
        note(r.early, 0, upstream * unit)
        note(r.early, 1, upstream)
        own = r.grad_feed[rows, :].astype(WIDE)
        note(r.early, 3, own)
        grad = own + norm_backward(upstream, unit, scaled, vector(3))
        r.grad_middle[pl.ds(k * step_rows, step_rows), :] = grad
        rounded = grad.astype(LOW)
        note(r.early, 2, rounded.astype(WIDE))
        r.grad_branch[rows, :] = rounded
        spread_branch.begin(half, k)

    tasks, late, held_first, held_second = [], [], [], []

    def flush_first():
        for one, k in held_first:
            one.add_first(k)
            late.append((one, k))
        del held_first[:]

    def first(one, k):
        flush_first()
        one.fetch_first(k)
        held_first.append((one, k))

    def flush_second():
        for one, k in held_second:
            one.add_second(k)
        del held_second[:]

    def fetch_second():
        flush_second()
        for one, k in late[:1]:
            one.fetch_second(k)
            held_second.append((one, k))
        del late[:1]

    def terms_and_start(work, n, one, which):
        work(n)
        one.start(which)

    def begin(one, terms):
        plan(terms_and_start, terms, 1, one, 0)
        plan(terms_and_start, terms, 3, one, 1)
        plan(terms, 2)
        plan(terms, 0)

    def plan(work, *given):
        tasks.append(functools.partial(work, *given))

    def work_on(count):
        for task in tasks[:count]:
            task()
        del tasks[:count]

    begin(sums.up, up_terms)
    for k in range(up_chunks):
        plan(first, sums.up, k)
    plan(flush_first)
    for block in range(fsdp):
        plan(feed_terms, block)
    begin(sums.down, down_terms)
    for k in range(down_chunks):
        plan(first, sums.down, k)
    plan(flush_first)

    work_on(2)
    r.grad_pairs[...] = jnp.zeros_like(r.grad_pairs)

    def home_feed(half, k):
        rows = line.at(half, k)
        feed = sum_feed.total(half, k) + vector(5)
        total = r.middle[pl.ds(k * step_rows, step_rows), :] + feed
        slot = place * tokens + half * line.half + k * step_rows
        slots = slot + lax.broadcasted_iota(jnp.int32, (step_rows, width), 0)
        keep = jnp.where(slots < length, 1.0, 0.0)
        note(r.late, 2, keep * total * total)
        note(r.late, 4, keep * feed * feed)
        r.feed_own[rows, :] = (keep * total).astype(LOW)
        spread_result.begin(half, k, r.feed_own)

    def attend_share(start):
        rows = pl.ds(start, share)
        total = mm_nt(r.grad_branch[rows, pl.ds(0, columns)], r.output[0])
        for block in range(1, fsdp):
            total += mm_nt(r.grad_branch[rows, pl.ds(block * columns, columns)], r.output[block])
        r.grad_mixture[...] = total.astype(LOW)
        keys = r.pairs[:, pl.ds(0, HD)]
        values = r.pairs[:, pl.ds(HD, HD)]
        shape = (share, keys.shape[0])
        query_at = place * tokens + start + lax.broadcasted_iota(jnp.int32, shape, 0)
        key_at = lax.broadcasted_iota(jnp.int32, shape, 1)
        allowed = (key_at <= query_at) & (key_at < length)
        factor = 1.0 / math.sqrt(HD)
        for head in range(heads):
            at = pl.ds(head * HD, HD)
            query = r.queries[rows, at]
            grad_mix = r.grad_mixture[:, at]
            scores = jnp.where(allowed, mm_nt(query, keys) * factor, NEGATIVE)
            soft = jnp.exp(scores - r.log_total[rows, pl.ds(head, 1)])
            grad_soft = mm_nt(grad_mix, values)
            dot_rows = jnp.sum(soft * grad_soft, -1, keepdims=True)
            grad_scores = (soft * (grad_soft - dot_rows) * factor).astype(LOW)
            r.grad_queries[rows, at] = mm(grad_scores, keys).astype(LOW)
            r.grad_pairs[:, pl.ds(0, HD)] += mm_tn(grad_scores, query)
            r.grad_pairs[:, pl.ds(HD, HD)] += mm_tn(soft.astype(LOW), grad_mix)

    every = (TP, FSDP, CTX)
    sum_early = RowSum(r.early, r.early_came, r.row_sems.at[0], every)
    sum_late = RowSum(r.late, r.late_came, r.row_sems.at[1], every)
    sum_rows = RowSum(r.own, r.own_came, r.row_sems.at[2], (FSDP, CTX))
    flow_two = Flow(sum_two, spread_branch, home_two, LAG)
    flow_feed = Flow(sum_feed, spread_result, home_feed, LAG)
    starts = [half * line.half + group * share for group in range(tp // 2) for half in range(2)]
    per_share = share // step_rows
    for n in range(flow_two.steps):
        flow_two.advance(1)
        if n == flow_two.steps - 4:
            flow_feed.launch()
        work_on(1)
        if n % 3 == 1:
            flush_second()
        if n >= 6 and n % 3 == 0:
            fetch_second()
        group = tp // 2 - (len(starts) + 1) // 2
        if starts and n >= flow_two.ready((group + 1) * per_share - 1):
            attend_share(starts.pop(0))
    work_on(len(tasks))
    for start in starts:
        attend_share(start)
        flow_feed.advance(1)
    sum_early.start()

    def pair_out(other):
        target = lax.rem(place + other, ctx)
        rows = pl.ds(pl.multiple_of(target * tokens, tokens), tokens)
        r.pair_sent[other - 1] = r.grad_pairs[rows, :].astype(LOW)
        return send(
            r.pair_sent.at[other - 1],
            r.pair_came.at[other - 1],
            r.pair_ctx_sem.at[0, other - 1],
            r.pair_ctx_sem.at[1, other - 1],
            CTX,
            target,
        )

    ctx_copies = [pair_out(other) for other in range(1, ctx)]
    for copy in ctx_copies:
        copy.start()
    sum_two.drain()

    def output_terms(n):
        terms = mm_tn(r.mixture[...], r.grad_branch[:, turn(n)])
        sums.output.piece(n, 0)[...] = terms.astype(LOW)

    def query_terms(n):
        terms = mm_tn(r.input_two[:, turn(n)], r.grad_queries[...])
        sums.query.piece(n, 0)[...] = terms.astype(LOW)

    def pair_terms(n):
        terms = mm_tn(r.input_two[:, turn(n)], r.pair_all[...].reshape(tokens, 2 * HD))
        r.pair_piece[n] = terms.astype(LOW)

    loads_one = pltpu.make_async_copy(r.input_one_hbm, r.input_two, r.load_sem.at[1])
    loads_one.start()
    begin(sums.output, output_terms)
    work_on(2)
    flow_feed.advance(1)
    for copy in ctx_copies:
        copy.wait()
    own_rows = pl.ds(pl.multiple_of(place * tokens, tokens), tokens)
    own_pairs = r.grad_pairs[own_rows, :]
    for other in range(1, ctx):
        own_pairs += r.pair_came[other - 1].astype(WIDE)
    r.pair_own[...] = own_pairs.astype(LOW).reshape(r.pair_own.shape)

    @tiles(width, step)
    def _(col):
        at = pl.ds(col, step)
        part = mm_nt(r.grad_queries[...], r.query[at, :])
        part += mm_nt(r.pair_own[...].reshape(tokens, 2 * HD), r.pair[at, :])
        r.sum_own[:, at] = part.astype(LOW)

    def pair_line(other):
        target = lax.rem(zone + other, tp)
        return send(
            r.pair_own.at[target],
            r.pair_terms.at[other - 1],
            r.pair_line_sem.at[0, other - 1],
            r.pair_line_sem.at[1, other - 1],
            TP,
            target,
        )

    def pair_spread(other):
        return send(
            r.pair_all.at[zone],
            r.pair_all.at[zone],
            r.pair_line_sem.at[2, other - 1],
            r.pair_line_sem.at[3, other - 1],
            TP,
            lax.rem(zone + other, tp),
        )

    def pair_begin():
        for other in range(1, tp):
            pair_line(other).start()
        r.own[pl.ds(1, 1), pl.ds(0, query_width)] = jnp.sum(
            r.grad_queries[...].astype(WIDE), 0, keepdims=True
        )

    def pair_shares():
        total = r.pair_own[zone].astype(WIDE)
        for other in range(1, tp):
            pair_line(other).wait_recv()
            total += r.pair_terms[other - 1].astype(WIDE)
        r.pair_all[zone] = total.astype(LOW)
        for other in range(1, tp):
            pair_spread(other).start()

    def pair_gathered():
        for other in range(1, tp):
            pair_spread(other).wait_recv()
        values = r.pair_all[...].reshape(tokens, 2 * HD)[:, HD:]
        r.own[pl.ds(2, 1), pl.ds(0, HD)] = jnp.sum(values.astype(WIDE), 0, keepdims=True)

    def home_one(half, k):
        rows = line.at(half, k)
        here = pl.ds(k * step_rows, step_rows)
        unit, scaled = norm_of(r.stream[here, :].astype(WIDE))
        upstream = sum_one.total(half, k)
        note(r.late, 0, upstream * unit)
        note(r.late, 1, upstream)
        grad = r.grad_middle[here, :] + norm_backward(upstream, unit, scaled, vector(0))
        r.sum_own[rows, :] = grad.astype(LOW)
        spread_stream.begin(half, k, r.sum_own)

    flow_one = Flow(sum_one, spread_stream, home_one, LAG)
    flow_one.launch()
    pair_begin()
    plan(loads_one.wait)
    begin(sums.query, query_terms)
    plan(pair_shares)
    plan(first, sums.output, 0)
    plan(first, sums.query, 0)
    plan(flush_first)
    plan(pair_gathered)
    begin(sums.pair, pair_terms)
    plan(first, sums.pair, 0)
    plan(flush_first)
    plan(sum_rows.start)
    stream_load.wait()
    late_on = False
    for n in range(flow_one.steps):
        flow_one.advance(1)
        flow_feed.advance(1)
        work_on(1)
        if n % 3 == 1:
            fetch_second()
        if n % 3 == 2:
            flush_second()
        if n % 2 == 1:
            sum_early.move()
        sum_rows.move()
        if late_on:
            sum_late.move()
        elif flow_one.all_home() and flow_feed.all_home():
            sum_late.start()
            late_on = True
    work_on(len(tasks))
    flow_feed.advance(flow_feed.steps)
    if not late_on:
        sum_late.start()
    sum_early.finish()
    while late:
        fetch_second()
        flush_second()
        sum_rows.move()
        sum_late.move()
    flush_second()
    sum_rows.finish()
    sum_late.finish()
    mine = pl.ds(pl.multiple_of(me * columns, columns), columns)
    r.small[pl.ds(0, 4), :] = r.early[pl.ds(0, 4), mine]
    r.small[pl.ds(4, 2), :] = r.late[pl.ds(0, 2), mine]
    squares = jnp.sum(r.late[pl.ds(2, 3), pl.ds(0, width)], 1, keepdims=True)
    roots = jnp.sqrt(squares / (r.late[pl.ds(7, 1), pl.ds(0, 1)] * width))
    r.small[pl.ds(8, 3), :] = jnp.broadcast_to(roots, (3, columns))

    for half in range(2):

        @pl.when(line.is_home(half))
        def _():
            rows = pl.ds(half * line.half, line.half)
            copies = [
                pltpu.make_async_copy(r.feed_own.at[rows], r.result.at[rows], r.keep_sem.at[0]),
                pltpu.make_async_copy(r.sum_own.at[rows], r.stream_grad.at[rows], r.keep_sem.at[1]),
            ]
            for copy in copies:
                copy.start()
            for copy in copies:
                copy.wait()

    for one in (sum_feed, sum_one, spread_branch, spread_result, spread_stream):
        one.drain()
    for other in range(1, tp):
        pair_line(other).wait_send()
        pair_spread(other).wait_send()
    for one in vars(sums).values():
        one.finish()


def layer(values):
    fsdp, ctx, tp = lax.axis_size(FSDP), lax.axis_size(CTX), lax.axis_size(TP)
    tokens, width = values.stream.shape
    inner = values.up.shape[1]
    columns = width // fsdp
    share = tokens // tp
    query_width = values.query.shape[1]
    pair_width = 2 * HD
    key_count = ctx * tokens
    dma = pltpu.SemaphoreType.DMA
    wide_row = max(width, inner)
    hops, tp_hops = len(bits_of(FSDP)) + len(bits_of(CTX)), len(bits_of(TP))
    far_outs = dict(
        input_one_hbm=((tokens, width), LOW),
        result=((tokens, width), LOW),
        stream_grad=((tokens, width), LOW),
        up_last=((ctx, columns, inner), LOW),
        up_near=((2, columns, inner), LOW),
        up_far=((columns, inner), LOW),
        down_last=((ctx, inner, columns), LOW),
        down_near=((2, inner, columns), LOW),
        down_far=((inner, columns), LOW),
        output_last=((ctx, query_width, columns), LOW),
        output_near=((2, query_width, columns), LOW),
        output_far=((query_width, columns), LOW),
        query_last=((ctx, columns, query_width), LOW),
        query_near=((2, columns, query_width), LOW),
        query_far=((columns, query_width), LOW),
        pair_last=((ctx, columns, pair_width), LOW),
        pair_near=((2, columns, pair_width), LOW),
        pair_far=((columns, pair_width), LOW),
    )
    scratch = dict(
        up=pltpu.VMEM((width, inner), LOW),
        down=pltpu.VMEM((fsdp, inner, columns), LOW),
        input_two=pltpu.VMEM((tokens, width), LOW),
        grad_feed=pltpu.VMEM((tokens, width), LOW),
        hidden=pltpu.VMEM((tokens, inner), LOW),
        grad_pre=pltpu.VMEM((tokens, inner), LOW),
        work_one=pltpu.VMEM((tokens, columns), WIDE),
        work_two=pltpu.VMEM((tokens, columns), WIDE),
        sum_own=pltpu.VMEM((tokens, width), LOW),
        sum_slots=pltpu.VMEM((tokens, width), LOW),
        feed_own=pltpu.VMEM((tokens, width), LOW),
        feed_slots=pltpu.VMEM((tokens, width), LOW),
        grad_branch=pltpu.VMEM((tokens, width), LOW),
        middle=pltpu.VMEM((tokens // 2, width), WIDE),
        grad_middle=pltpu.VMEM((tokens // 2, width), WIDE),
        stream=pltpu.VMEM((tokens // 2, width), LOW),
        output=pltpu.VMEM((fsdp, query_width, columns), LOW),
        query=pltpu.VMEM((width, query_width), LOW),
        pair=pltpu.VMEM((width, pair_width), LOW),
        queries=pltpu.VMEM((tokens, query_width), LOW),
        pairs=pltpu.VMEM((key_count, pair_width), LOW),
        mixture=pltpu.VMEM((tokens, query_width), LOW),
        grad_mixture=pltpu.VMEM((share, query_width), LOW),
        grad_queries=pltpu.VMEM((tokens, query_width), LOW),
        grad_pairs=pltpu.VMEM((key_count, pair_width), WIDE),
        pair_sent=pltpu.VMEM((ctx - 1, tokens, pair_width), LOW),
        pair_came=pltpu.VMEM((ctx - 1, tokens, pair_width), LOW),
        pair_own=pltpu.VMEM((tp, share, pair_width), LOW),
        pair_terms=pltpu.VMEM((tp - 1, share, pair_width), LOW),
        pair_all=pltpu.VMEM((tp, share, pair_width), LOW),
        pair_piece=pltpu.VMEM((fsdp, columns, pair_width), LOW),
        stage_up=pltpu.VMEM((3, columns // 4, inner), LOW),
        stage_down=pltpu.VMEM((3, inner // 4, columns), LOW),
        smalls=pltpu.VMEM((fsdp,) + values.packed.shape, WIDE),
        vectors=pltpu.VMEM((8, wide_row), WIDE),
        squares=pltpu.VMEM((1, width), WIDE),
        log_total=pltpu.VMEM((tokens, query_width // HD), WIDE),
        front_sems=line_sems(tokens),
        spread_sems=line_sems(tokens),
        query_gather=Gather.sems(2),
        pair_gather=Gather.sems(2),
        output_gather=Gather.sems(1),
        up_gather=Gather.sems(2),
        down_gather=Gather.sems(2),
        small_sem=dma((2, fsdp - 1)),
        exchange_sem=dma((2, ctx - 1)),
        load_sem=dma((3,)),
        early=pltpu.VMEM((8, wide_row), WIDE),
        late=pltpu.VMEM((8, wide_row), WIDE),
        early_came=pltpu.VMEM((hops + tp_hops, 8, wide_row), WIDE),
        late_came=pltpu.VMEM((hops + tp_hops, 8, wide_row), WIDE),
        own_came=pltpu.VMEM((hops, 8, wide_row), WIDE),
        row_sems=dma((3, 2, hops + tp_hops)),
        keep_sem=dma((2,)),
        pair_ctx_sem=dma((2, ctx - 1)),
        pair_line_sem=dma((4, tp - 1)),
        two_sems=line_sems(tokens),
        feed_sems=line_sems(tokens),
        one_sems=line_sems(tokens),
        branch_sems=line_sems(tokens),
        result_sems=line_sems(tokens),
        stream_sems=line_sems(tokens),
        up_sems=PieceSum.sems(4),
        down_sems=PieceSum.sems(4),
        output_sems=PieceSum.sems(1),
        query_sems=PieceSum.sems(1),
        pair_sems=PieceSum.sems(1),
    )
    if tokens != query_width or inner < width:
        scratch.update(output_piece=pltpu.VMEM((fsdp, query_width, columns), LOW))
    if tokens != columns or inner < fsdp * query_width:
        scratch.update(query_piece=pltpu.VMEM((fsdp, columns, query_width), LOW))
    return call_kernel(
        layer_body,
        1,
        dict(
            stream_hbm=values.stream,
            cotangent_hbm=values.cotangent,
            query_shard=values.query,
            pair_shard=values.pair,
            output_shard=values.output,
            up_shard=values.up,
            down_shard=values.down,
        ),
        dict(packed=values.packed),
        dict(lengths=values.lengths),
        far_outs,
        dict(small=((16, columns), WIDE), own=((8, wide_row), WIDE)),
        scratch,
    )


def body(
    stream,
    cotangent,
    lengths,
    first_gain,
    first_shift,
    query_weight,
    query_bias,
    pair_weight,
    value_bias,
    output_weight,
    output_bias,
    second_gain,
    second_shift,
    up_weight,
    up_bias,
    down_weight,
    down_bias,
):
    fsdp = lax.axis_size(FSDP)
    me = lax.axis_index(FSDP)
    seq_count, group_len, width = stream.shape
    tokens = seq_count * group_len
    columns, inner = first_gain.shape[0], up_weight.shape[1]

    def placed(bias):
        spots = jnp.arange(fsdp)[None, :, None] == me
        return jnp.where(spots, bias.reshape(-1, 1, bias.shape[-1]).astype(WIDE), 0.0).reshape(-1)

    def row(values):
        return jnp.pad(values.astype(WIDE), (0, columns - values.shape[0]))[None]

    vectors = (first_gain, first_shift, output_bias, second_gain, second_shift, down_bias)
    packed = jnp.concatenate(
        [row(vector) for vector in vectors]
        + [row(placed(query_bias)), row(placed(value_bias.reshape(1, -1)))]
        + [placed(up_bias).reshape(-1, columns)]
    )
    packed = jnp.pad(packed, ((0, -packed.shape[0] % 8), (0, 0)))
    values = types.SimpleNamespace(
        stream=stream.reshape(tokens, width),
        cotangent=cotangent.reshape(tokens, width),
        lengths=lengths,
        packed=packed,
        query=query_weight,
        pair=pair_weight,
        output=output_weight,
        up=up_weight,
        down=down_weight,
    )
    ended = types.SimpleNamespace(**layer(values))
    small, own = ended.small, ended.own
    query_width = query_weight.shape[1]

    def finished(last):
        return jnp.sum(last.astype(WIDE), 0)

    up_bias_all = own[0, :inner].reshape(up_bias.shape[0], fsdp, -1)
    query_bias_all = own[1, :query_width].reshape(query_bias.shape[0], fsdp, -1)
    value_size = value_bias.shape[0]
    return (
        ended.result.reshape(stream.shape),
        ended.stream_grad.reshape(stream.shape),
        small[4],
        small[5],
        finished(ended.query_last),
        lax.dynamic_index_in_dim(query_bias_all, me, 1, False),
        finished(ended.pair_last),
        lax.dynamic_slice_in_dim(own[2], me * value_size, value_size, 0),
        finished(ended.output_last),
        small[2],
        small[0],
        small[1],
        finished(ended.up_last),
        lax.dynamic_index_in_dim(up_bias_all, me, 1, False),
        finished(ended.down_last),
        small[3],
        small[8:11, 0],
    )


def solution(mesh):
    in_specs = (
        P(FSDP, CTX, None),
        P(FSDP, CTX, None),
        P(FSDP),
        P(FSDP),
        P(FSDP),
        P(FSDP, TP),
        P(TP, FSDP),
        P(FSDP, None),
        P(FSDP),
        P(TP, FSDP),
        P(FSDP),
        P(FSDP),
        P(FSDP),
        P(FSDP, TP),
        P(TP, FSDP),
        P(TP, FSDP),
        P(FSDP),
    )
    out_specs = (
        P(FSDP, CTX, None),
        P(FSDP, CTX, None),
        P(FSDP),
        P(FSDP),
        P(FSDP, TP),
        P(TP, FSDP),
        P(FSDP, None),
        P(FSDP),
        P(TP, FSDP),
        P(FSDP),
        P(FSDP),
        P(FSDP),
        P(FSDP, TP),
        P(TP, FSDP),
        P(TP, FSDP),
        P(FSDP),
        P(),
    )
    return jax.shard_map(body, mesh=mesh, in_specs=in_specs, out_specs=out_specs, check_vma=False)
```

```python
import functools
import math
import types

import jax
import jax.numpy as jnp
from jax import lax
from jax.experimental import pallas as pl
from jax.experimental.pallas import tpu as pltpu
from jax.sharding import PartitionSpec as P

HD = 128
EPSILON = 1e-05
NEGATIVE = -1e30
FSDP, CTX, TP = "fsdp", "ctx", "tp"
LOW, WIDE = jnp.bfloat16, jnp.float32
MESH = pl.DeviceIdType.MESH
VMEM_BYTES = 60 << 20
SKEW, LAG = 2, 2


def flip(place, bit):
    return place + bit - 2 * bit * lax.rem(lax.div(place, bit), 2)


def bits_of(axis):
    count, bit, found = lax.axis_size(axis), 1, []
    while bit < count:
        found.append(bit)
        bit *= 2
    return found


def mm(left, right):
    return jnp.dot(left, right, preferred_element_type=WIDE)


def mm_nt(left, right):
    return lax.dot_general(left, right, (((1,), (1,)), ((), ())), preferred_element_type=WIDE)


def mm_tn(left, right):
    return lax.dot_general(left, right, (((0,), (0,)), ((), ())), preferred_element_type=WIDE)


def tiles(count, step):
    def run(work):
        def once(index, carry):
            work(pl.multiple_of(index * step, step))
            return carry

        lax.fori_loop(0, count // step, once, 0)

    return run


def norm_of(values):
    center = values - jnp.mean(values, -1, keepdims=True)
    scaled = lax.rsqrt(jnp.mean(center * center, -1, keepdims=True) + EPSILON)
    return center * scaled, scaled


def norm_backward(upstream, unit_rows, scaled, norm_gain):
    gained = upstream * norm_gain
    return scaled * (
        gained
        - jnp.mean(gained, -1, keepdims=True)
        - unit_rows * jnp.mean(gained * unit_rows, -1, keepdims=True)
    )


def send(source, target, outgo, income, axis, place):
    return pltpu.make_async_remote_copy(
        src_ref=source,
        dst_ref=target,
        send_sem=outgo,
        recv_sem=income,
        device_id={axis: place},
        device_id_type=MESH,
    )


def all_peers():
    me, place, zone = lax.axis_index(FSDP), lax.axis_index(CTX), lax.axis_index(TP)
    ctx, tp = lax.axis_size(CTX), lax.axis_size(TP)
    peers = [(FSDP, flip(me, 1)), (FSDP, flip(me, 2)), (FSDP, flip(flip(me, 1), 2))]
    peers += [(CTX, lax.rem(place + k, ctx)) for k in range(1, ctx)]
    peers += [(TP, lax.rem(zone + k, tp)) for k in range(1, tp)]
    return peers


def greet(peers):
    barrier = pltpu.get_barrier_semaphore()
    for axis, place in peers:
        pl.semaphore_signal(barrier, inc=1, device_id={axis: place}, device_id_type=MESH)
    return lambda: pl.semaphore_wait(barrier, len(peers))


def split_rows(tokens):
    rows = 32 if tokens % 512 == 0 else 16
    return rows, tokens // 2 // rows


class Line:
    def __init__(self, tokens):
        self.place, self.count = lax.axis_index(TP), lax.axis_size(TP)
        self.rows, self.chunks = split_rows(tokens)
        self.half = tokens // 2

    def at(self, half, k):
        start = half * self.half + k * self.rows
        return pl.ds(start if isinstance(start, int) else pl.multiple_of(start, self.rows), self.rows)

    def is_home(self, half):
        return self.place == (0 if half == 0 else self.count - 1)

    def is_far(self, half):
        return self.place == (self.count - 1 if half == 0 else 0)

    def toward(self, half):
        move = self.count - 1 if half == 0 else 1
        return lax.rem(self.place + move, self.count)

    def away(self, half):
        return self.toward(1 - half)


class LineSum(Line):
    def __init__(self, own, slots, sems):
        super().__init__(own.shape[0])
        self.own, self.slots = own, slots
        self.outgo, self.income = sems

    def copy(self, half, k):
        rows = self.at(half, k)
        return send(
            self.own.at[rows],
            self.slots.at[rows],
            self.outgo.at[half, k],
            self.income.at[half, k],
            TP,
            self.toward(half),
        )

    def launch(self, half, first=0, last=None):
        @pl.when(self.is_far(half))
        def _():
            for k in range(first, self.chunks if last is None else last):
                self.copy(half, k).start()

    def total(self, half, k):
        rows = self.at(half, k)
        return self.own[rows, :].astype(WIDE) + self.slots[rows, :].astype(WIDE)

    def pass_on(self, half, k):
        self.copy(half, k).wait_recv()
        self.own[self.at(half, k), :] = self.total(half, k).astype(LOW)
        self.copy(half, k).start()

    def drain(self):
        for half in range(2):

            @pl.when(jnp.logical_not(self.is_home(half)))
            def _():
                for k in range(self.chunks):
                    self.copy(half, k).wait_send()


class LineSpread(Line):
    def __init__(self, held, sems):
        super().__init__(held.shape[0])
        self.held = held
        self.outgo, self.income = sems

    def copy(self, half, k, source=None):
        rows = self.at(half, k)
        return send(
            self.held.at[rows] if source is None else source.at[rows],
            self.held.at[rows],
            self.outgo.at[half, k],
            self.income.at[half, k],
            TP,
            self.away(half),
        )

    def begin(self, half, k, source=None):
        self.copy(half, k, source).start()

    def serve(self, half, k):
        self.copy(half, k).wait_recv()

        @pl.when(jnp.logical_not(self.is_far(half)))
        def _():
            self.copy(half, k).start()

    def drain(self):
        for half in range(2):

            @pl.when(jnp.logical_not(self.is_far(half)))
            def _():
                for k in range(self.chunks):
                    self.copy(half, k).wait_send()


class Flow(Line):
    def __init__(self, line_sum, spread, home, lag):
        super().__init__(line_sum.own.shape[0])
        self.sum, self.spread, self.home, self.lag = line_sum, spread, home, lag
        self.now = 0
        self.to_home = SKEW * (self.count - 2)
        self.steps = self.chunks + lag + 2 * self.to_home

    def launch(self, first=0, last=None):
        for half in range(2):
            self.sum.launch(half, first, last)

    def inside(self, k):
        return (k >= 0) & (k < self.chunks)

    def advance(self, count=1):
        for n in range(self.now, min(self.now + count, self.steps)):
            self.step(n)
        self.now = min(self.now + count, self.steps)

    def step(self, n):
        last = self.count - 1
        at_home = n - self.to_home
        for half in range(2):
            hops = last - self.place if half == 0 else self.place
            k = n - SKEW * (hops - 1)

            @pl.when((hops >= 1) & (hops < last) & self.inside(k))
            def _():
                self.sum.pass_on(half, k)

            if 0 <= at_home < self.chunks:

                @pl.when(self.is_home(half))
                def _():
                    self.sum.copy(half, at_home).wait_recv()
                    self.home(half, at_home)

        for half in range(2):
            hops = self.place if half == 0 else last - self.place
            k = at_home - self.lag - SKEW * (hops - 1)

            @pl.when((hops >= 1) & self.inside(k))
            def _():
                self.spread.serve(half, k)

    def all_home(self):
        return self.now >= self.chunks + self.to_home

    def ready(self, chunk):
        return chunk + self.lag + 2 * self.to_home


class Gather:
    def __init__(self, shard, held, sems, cut):
        self.shard, self.held = shard, held
        self.me, self.place = lax.axis_index(FSDP), lax.axis_index(CTX)
        self.ctx = lax.axis_size(CTX)
        self.cut = cut
        self.rows = shard.shape[0] // self.ctx // cut
        self.near_sem, self.far_sem, self.side_sem, self.pass_sem, self.local = sems

    def part(self, place, k):
        return pl.ds(pl.multiple_of((place * self.cut + k) * self.rows, self.rows), self.rows)

    def keep(self):
        every = pl.ds(0, self.shard.shape[0])
        return pltpu.make_async_copy(self.shard, self.held(self.me, every), self.local.at[0])

    def near(self):
        every = pl.ds(0, self.shard.shape[0])
        return send(
            self.shard,
            self.held(self.me, every),
            self.near_sem.at[0],
            self.near_sem.at[1],
            FSDP,
            flip(self.me, 1),
        )

    def far(self, k):
        part = self.part(self.place, k)
        return send(
            self.shard.at[part],
            self.held(self.me, part),
            self.far_sem.at[0, k],
            self.far_sem.at[1, k],
            FSDP,
            flip(self.me, 2),
        )

    def side(self, other, k):
        held = self.held(flip(self.me, 2), self.part(self.place, k))
        return send(
            held,
            held,
            self.side_sem.at[0, other - 1, k],
            self.side_sem.at[1, other - 1, k],
            CTX,
            lax.rem(self.place + other, self.ctx),
        )

    def over(self, other, k):
        place = lax.rem(self.place + self.ctx - other, self.ctx)
        held = self.held(flip(self.me, 2), self.part(place, k))
        return send(
            held,
            held,
            self.pass_sem.at[0, other, k],
            self.pass_sem.at[1, other, k],
            FSDP,
            flip(self.me, 1),
        )

    def start(self):
        for k in range(self.cut):
            self.far(k).start()
        self.near().start()
        self.keep().start()

    def cross(self, k):
        self.far(k).wait_recv()
        for other in range(1, self.ctx):
            self.side(other, k).start()
        self.over(0, k).start()

    def pass_on(self, k):
        for other in range(1, self.ctx):
            self.side(other, k).wait_recv()
            self.over(other, k).start()

    def ready(self):
        self.keep().wait()
        self.near().wait_recv()
        for k in range(self.cut):
            for other in range(self.ctx):
                self.over(other, k).wait_recv()

    def drain(self):
        self.near().wait_send()
        for k in range(self.cut):
            self.far(k).wait_send()
            for other in range(self.ctx):
                self.over(other, k).wait_send()
                if other > 0:
                    self.side(other, k).wait_send()

    @staticmethod
    def sems(cut):
        ctx = lax.axis_size(CTX)
        shapes = ((2,), (2, cut), (2, ctx - 1, cut), (2, ctx, cut), (1,))
        return tuple(pltpu.SemaphoreType.DMA(shape) for shape in shapes)


class PieceSum:
    def __init__(self, piece, near, far, last, stages, sems, chunks):
        self.piece, self.near, self.far, self.last = piece, near, far, last
        self.stages, self.chunks = stages, chunks
        self.rows = far.shape[0] // chunks
        self.near_sem, self.far_sem, self.last_sem, self.local = sems
        self.me, self.place = lax.axis_index(FSDP), lax.axis_index(CTX)
        self.ctx = lax.axis_size(CTX)

    def part(self, k):
        return pl.ds(k * self.rows, self.rows)

    def near_copy(self, which, k):
        return send(
            self.piece(2 * which + 1, k),
            self.near.at[which, self.part(k)],
            self.near_sem.at[0, which, k],
            self.near_sem.at[1, which, k],
            FSDP,
            flip(self.me, 1),
        )

    def far_copy(self, k):
        return send(
            self.piece(2, k),
            self.far.at[self.part(k)],
            self.far_sem.at[0, k],
            self.far_sem.at[1, k],
            FSDP,
            flip(self.me, 2),
        )

    def last_copy(self, other, k):
        return send(
            self.piece(0, k),
            self.last.at[self.place, self.part(k)],
            self.last_sem.at[0, other - 1, k],
            self.last_sem.at[1, other - 1, k],
            CTX,
            lax.rem(self.place + other, self.ctx),
        )

    def own_copy(self, k):
        return pltpu.make_async_copy(
            self.piece(0, k), self.last.at[self.place, self.part(k)], self.local.at[3 + k]
        )

    def start(self, which):
        for k in range(self.chunks):
            self.near_copy(which, k).start()

    def load(self, source, index):
        return pltpu.make_async_copy(source, self.stages[index], self.local.at[index])

    def add(self, r, k, index):
        step = 32 if self.rows % 32 == 0 else 16
        piece, stage = self.piece(r, k), self.stages[index]

        @tiles(self.rows, step)
        def _(at):
            here = pl.ds(at, step)
            total = piece[here].astype(WIDE) + stage[here].astype(WIDE)
            piece[here] = total.astype(LOW)

    def fetch_first(self, k):
        for which in range(2):
            self.near_copy(which, k).wait_recv()
        for which in range(2):
            self.load(self.near.at[which, self.part(k)], which).start()

    def add_first(self, k):
        self.load(self.near.at[1, self.part(k)], 1).wait()
        self.add(2, k, 1)
        self.far_copy(k).start()
        self.load(self.near.at[0, self.part(k)], 0).wait()
        self.add(0, k, 0)

    def fetch_second(self, k):
        self.far_copy(k).wait_recv()
        self.load(self.far.at[self.part(k)], 2).start()

    def add_second(self, k):
        self.load(self.far.at[self.part(k)], 2).wait()
        self.add(0, k, 2)
        for other in range(1, self.ctx):
            self.last_copy(other, k).start()
        self.own_copy(k).start()

    def finish(self):
        for k in range(self.chunks):
            for other in range(1, self.ctx):
                self.last_copy(other, k).wait_recv()
                self.last_copy(other, k).wait_send()
            self.own_copy(k).wait()
            self.far_copy(k).wait_send()
            for which in range(2):
                self.near_copy(which, k).wait_send()

    @staticmethod
    def sems(chunks):
        ctx = lax.axis_size(CTX)
        shapes = ((2, 2, chunks), (2, chunks), (2, ctx - 1, chunks), (3 + chunks,))
        return tuple(pltpu.SemaphoreType.DMA(shape) for shape in shapes)


class RowSum:
    def __init__(self, rows, came, sems, axes):
        self.rows, self.came, self.sems = rows, came, sems
        self.hops = [(axis, bit) for axis in axes for bit in bits_of(axis)]
        self.now = len(self.hops)

    def copy(self, n):
        axis, bit = self.hops[n]
        return send(
            self.rows,
            self.came.at[n],
            self.sems.at[0, n],
            self.sems.at[1, n],
            axis,
            flip(lax.axis_index(axis), bit),
        )

    def start(self):
        self.now = 0
        self.copy(0).start()

    def move(self):
        if self.now == len(self.hops):
            return False
        self.copy(self.now).wait()
        self.rows[...] += self.came[self.now]
        self.now += 1
        if self.now < len(self.hops):
            self.copy(self.now).start()
        return True

    def finish(self):
        while self.move():
            pass


def line_sems(tokens):
    rows, chunks = split_rows(tokens)
    return tuple(pltpu.SemaphoreType.DMA((2, chunks)) for _ in range(2))


def call_kernel(body, ident, far, near, scalars, far_outs, near_outs, scratch):
    groups = (far, near, scalars)
    spaces = (pl.ANY, pltpu.VMEM, pltpu.SMEM)
    arrays, in_specs = [], []
    for group, space in zip(groups, spaces):
        arrays += list(group.values())
        in_specs += [pl.BlockSpec(memory_space=space)] * len(group)
    outs = dict(far_outs, **near_outs)
    out_specs = [pl.BlockSpec(memory_space=pl.ANY)] * len(far_outs)
    out_specs += [pl.BlockSpec(memory_space=pltpu.VMEM)] * len(near_outs)
    shapes, tree = jax.tree.flatten(scratch)
    ins = [name for group in groups for name in group]

    def kernel(*refs):
        held = dict(zip(ins + list(outs), refs))
        held.update(jax.tree.unflatten(tree, refs[len(ins) + len(outs) :]))
        body(types.SimpleNamespace(**held))

    given = pl.pallas_call(
        kernel,
        out_shape=[jax.ShapeDtypeStruct(shape, kind) for shape, kind in outs.values()],
        in_specs=in_specs,
        out_specs=out_specs,
        scratch_shapes=shapes,
        compiler_params=pltpu.CompilerParams(
            collective_id=ident, has_side_effects=True, vmem_limit_bytes=VMEM_BYTES
        ),
    )(*arrays)
    return dict(zip(outs, given))


def front_part(r):
    me, place, zone = lax.axis_index(FSDP), lax.axis_index(CTX), lax.axis_index(TP)
    fsdp, ctx, tp = lax.axis_size(FSDP), lax.axis_size(CTX), lax.axis_size(TP)
    tokens, width = r.stream_hbm.shape
    columns = width // fsdp
    query_width = r.query.shape[1]
    heads = query_width // HD
    inner = r.up.shape[1]
    length = r.lengths[0]
    line = Line(tokens)
    step_rows, chunks = line.rows, line.chunks

    ready = greet(all_peers())
    stream_load = pltpu.make_async_copy(r.stream_hbm, r.feed_own, r.load_sem.at[0])
    stream_load.start()
    cotangent_load = pltpu.make_async_copy(r.cotangent_hbm, r.grad_feed, r.load_sem.at[1])
    cotangent_load.start()

    def block_rows(held):
        size = held.shape[0] // fsdp

        def view(block, rows):
            start = pl.multiple_of(block * size + rows.start, 16)
            return held.at[pl.ds(start, rows.size)]

        return view

    gathers = types.SimpleNamespace(
        query=Gather(r.query_shard, block_rows(r.query), r.query_gather, r.query_gather[1].shape[1]),
        pair=Gather(r.pair_shard, block_rows(r.pair), r.pair_gather, r.pair_gather[1].shape[1]),
        output=Gather(r.output_shard, lambda b, rows: r.output.at[b, rows], r.output_gather, r.output_gather[1].shape[1]),
        up=Gather(r.up_shard, block_rows(r.up), r.up_gather, r.up_gather[1].shape[1]),
        down=Gather(
            r.down_shard, lambda b, rows: r.down.at[b, rows], r.down_gather, r.down_gather[1].shape[1]
        ),
    )

    def small_copy(k):
        target = flip(me, k) if k < 3 else flip(flip(me, 1), 2)
        return send(
            r.smalls.at[0], r.smalls.at[k], r.small_sem.at[0, k - 1], r.small_sem.at[1, k - 1],
            FSDP, target,
        )

    r.smalls[0] = r.packed[...]
    ready()
    for k in range(1, fsdp):
        small_copy(k).start()
    gathers.pair.start()
    gathers.query.start()
    for k in range(1, fsdp):
        small_copy(k).wait()
    query_add = jnp.zeros((1, query_width), WIDE)
    value_add = jnp.zeros((1, HD), WIDE)
    for k in range(fsdp):
        block = me if k == 0 else flip(me, k) if k < 3 else flip(flip(me, 1), 2)
        at = pl.ds(pl.multiple_of(block * columns, columns), columns)
        r.vectors[pl.ds(0, 6), at] = r.smalls[k, pl.ds(0, 6), :]
        query_add += r.smalls[k, pl.ds(6, 1), pl.ds(0, query_width)]
        value_add += r.smalls[k, pl.ds(7, 1), pl.ds(0, HD)]
    for q in range(inner // columns):
        total = jnp.zeros((1, columns), WIDE)
        for k in range(fsdp):
            total += r.smalls[k, pl.ds(8 + q, 1), :]
        r.vectors[pl.ds(6, 1), pl.ds(q * columns, columns)] = total
    r.vectors[pl.ds(7, 1), :] = jnp.zeros((1, r.vectors.shape[1]), WIDE)

    def vector(n):
        return r.vectors[pl.ds(n, 1), pl.ds(0, width)]

    stream_load.wait()
    norm_step = min(32, tokens)

    @tiles(tokens, norm_step)
    def _(row):
        rows = pl.ds(row, norm_step)
        unit, scaled = norm_of(r.feed_own[rows, :].astype(WIDE))
        r.grad_branch[rows, :] = (unit * vector(0) + vector(1)).astype(LOW)

    early = (gathers.pair, gathers.query)
    for k in range(2):
        for one in early:
            one.cross(k)
    for k in range(2):
        for one in early:
            one.pass_on(k)
    for one in (gathers.output, gathers.down, gathers.up):
        one.start()
    gathers.pair.ready()
    own_rows = pl.ds(pl.multiple_of(place * tokens, tokens), tokens)
    key_half = mm(r.grad_branch[...], r.pair[...])
    r.pairs[own_rows, pl.ds(0, HD)] = key_half[:, :HD].astype(LOW)
    r.pairs[own_rows, pl.ds(HD, HD)] = (key_half[:, HD:] + value_add).astype(LOW)

    def pair_copy(other):
        return send(
            r.pairs.at[own_rows],
            r.pairs.at[own_rows],
            r.exchange_sem.at[0, other - 1],
            r.exchange_sem.at[1, other - 1],
            CTX,
            lax.rem(place + other, ctx),
        )

    for other in range(1, ctx):
        pair_copy(other).start()
    gathers.query.ready()
    r.queries[...] = (mm(r.grad_branch[...], r.query[...]) + query_add).astype(LOW)
    input_save = pltpu.make_async_copy(r.grad_branch, r.input_one_hbm, r.load_sem.at[2])
    input_save.start()
    gathers.output.cross(0)
    cotangent_load.wait()

    @tiles(tokens, step_rows)
    def _(row):
        rows = pl.ds(row, step_rows)
        slots = place * tokens + row + lax.broadcasted_iota(jnp.int32, (step_rows, width), 0)
        keep = jnp.where(slots < length, 1.0, 0.0)
        r.grad_feed[rows, :] = (keep * r.grad_feed[rows, :].astype(WIDE)).astype(LOW)

    for other in range(1, ctx):
        pair_copy(other).wait_recv()
    gathers.output.pass_on(0)

    share = min(HD, line.half)
    per_share = share // step_rows
    factor = 1.0 / math.sqrt(HD)

    def attend(start):
        rows = pl.ds(start, share)
        keys = r.pairs[:, pl.ds(0, HD)]
        values = r.pairs[:, pl.ds(HD, HD)]
        shape = (share, keys.shape[0])
        query_at = place * tokens + start + lax.broadcasted_iota(jnp.int32, shape, 0)
        key_at = lax.broadcasted_iota(jnp.int32, shape, 1)
        allowed = (key_at <= query_at) & (key_at < length)
        for head in range(heads):
            at = pl.ds(head * HD, HD)
            scores = jnp.where(allowed, mm_nt(r.queries[rows, at], keys) * factor, NEGATIVE)
            peak = jnp.max(scores, -1, keepdims=True)
            soft = jnp.exp(scores - peak)
            total = jnp.sum(soft, -1, keepdims=True)
            r.mixture[rows, at] = mm((soft / total).astype(LOW), values).astype(LOW)
            r.log_total[rows, pl.ds(head, 1)] = peak + jnp.log(total)

    def project(start):
        rows = pl.ds(start, share)
        for block in range(fsdp):
            at = pl.ds(block * columns, columns)
            r.sum_own[rows, at] = mm(r.mixture[rows, :], r.output[block]).astype(LOW)

    branch_sum = LineSum(r.sum_own, r.sum_slots, r.front_sems)
    spread = LineSpread(r.input_two, r.spread_sems)
    r.squares[...] = jnp.zeros_like(r.squares)

    def home(half, k):
        branch = branch_sum.total(half, k) + vector(2)
        middle = r.feed_own[line.at(half, k), :].astype(WIDE) + branch
        r.middle[pl.ds(k * step_rows, step_rows), :] = middle
        unit, scaled = norm_of(middle)
        r.input_two[line.at(half, k), :] = (unit * vector(3) + vector(4)).astype(LOW)
        spread.begin(half, k)
        slot = place * tokens + half * line.half + k * step_rows
        slots = slot + lax.broadcasted_iota(jnp.int32, (step_rows, width), 0)
        keep = jnp.where(slots < length, 1.0, 0.0)
        r.squares[...] += jnp.sum(keep * branch * branch, 0, keepdims=True)

    big = [(gathers.down, k) for k in range(gathers.down.cut)]
    big += [(gathers.up, k) for k in range(gathers.up.cut)]
    events = []
    for index, (one, k) in enumerate(big):
        events.append(functools.partial(one.cross, k))
        if index > 0:
            before, last = big[index - 1]
            events.append(functools.partial(before.pass_on, last))
    events.append(functools.partial(big[-1][0].pass_on, big[-1][1]))

    def move_on(count):
        for event in events[:count]:
            event()
        del events[:count]

    flow = Flow(branch_sum, spread, home, LAG)
    groups = line.half // share
    for group in range(groups):
        for half in range(2):
            start = half * line.half + group * share
            attend(start)
            if group == 0 and half == 0:
                gathers.output.ready()
            project(start)
        flow.launch(per_share * group, per_share * group + per_share)
        if group < groups - 1:
            flow.advance(1)
            move_on(1)
    def hidden_terms(q):
        at = pl.ds(q * columns, columns)
        total = mm_nt(r.grad_feed[:, pl.ds(0, columns)], r.down[0, at, :])
        for block in range(1, fsdp):
            total += mm_nt(r.grad_feed[:, pl.ds(block * columns, columns)], r.down[block, at, :])
        r.grad_pre[:, at] = total.astype(LOW)

    left = list(range(inner // columns))
    while flow.now < flow.steps:
        flow.advance(1)
        if flow.now % 2 == 0:
            move_on(1)
        if left and flow.now >= flow.steps - len(left):
            if left[0] == 0:
                gathers.down.ready()
            hidden_terms(left.pop(0))
    for q in left:
        hidden_terms(q)
    move_on(len(events))
    input_save.wait()
    branch_sum.drain()

    def end():
        for other in range(1, ctx):
            pair_copy(other).wait_send()
        for one in vars(gathers).values():
            one.drain()
        spread.drain()

    return gathers, end


def layer_body(r):
    gathers, front_end = front_part(r)
    back_part(r, gathers, front_end)


def back_part(r, gathers, front_end):
    me, place, zone = lax.axis_index(FSDP), lax.axis_index(CTX), lax.axis_index(TP)
    fsdp, ctx, tp = lax.axis_size(FSDP), lax.axis_size(CTX), lax.axis_size(TP)
    tokens, width = r.input_two.shape
    inner = r.up.shape[1]
    columns = width // fsdp
    share = tokens // tp
    query_width = r.queries.shape[1]
    heads = query_width // HD
    length = r.lengths[0]
    line = Line(tokens)
    step_rows, chunks = line.rows, line.chunks
    step = columns
    blocks = inner // step

    at_end = jnp.where(zone == tp - 1, tokens // 2, 0)
    stream_part = r.stream_hbm.at[pl.ds(pl.multiple_of(at_end, tokens // 2), tokens // 2)]
    stream_load = pltpu.make_async_copy(stream_part, r.stream, r.load_sem.at[0])
    stream_load.start()
    for rows in (r.early, r.late, r.own):
        rows[...] = jnp.zeros_like(rows)
    r.late[pl.ds(3, 1), pl.ds(0, width)] = r.squares[...]
    counted = jnp.clip(length - place * tokens, 0, tokens).astype(WIDE)
    r.late[pl.ds(7, 1), :] = jnp.full((1, r.late.shape[1]), jnp.where(zone == 0, counted, 0.0))
    def vector(n):
        return r.vectors[pl.ds(n, 1), pl.ds(0, width)]

    def note(rows, row, values):
        rows[pl.ds(row, 1), pl.ds(0, width)] += jnp.sum(values, 0, keepdims=True)

    gathers.up.ready()

    @tiles(inner, step)
    def _(q):
        at = pl.ds(q, step)
        r.work_one[...] = mm(r.input_two[...], r.up[:, at])
        bias = r.vectors[pl.ds(6, 1), at]

        @tiles(tokens, 32)
        def _(row):
            here = pl.ds(row, 32)
            v = r.work_one[here, :] + bias
            square = v * v
            reach = math.sqrt(2.0 / math.pi)
            t = jnp.tanh(reach * v * (1.0 + 0.044715 * square))
            gate = 0.5 * (1.0 + t)
            slope = gate + 0.5 * v * (1.0 - t * t) * reach * (1.0 + 3 * 0.044715 * square)
            r.hidden[here, at] = (v * gate).astype(LOW)
            grad = (r.grad_pre[here, at].astype(WIDE) * slope).astype(LOW)
            r.grad_pre[here, at] = grad
            r.own[pl.ds(0, 1), at] += jnp.sum(grad.astype(WIDE), 0, keepdims=True)

    front_end()
    sum_two = LineSum(r.sum_own, r.sum_slots, r.two_sems)
    sum_feed = LineSum(r.feed_own, r.feed_slots, r.feed_sems)
    sum_one = LineSum(r.sum_own, r.sum_slots, r.one_sems)
    spread_branch = LineSpread(r.grad_branch, r.branch_sems)
    spread_result = LineSpread(r.result, r.result_sems)
    spread_stream = LineSpread(r.stream_grad, r.stream_sems)

    @tiles(width, step)
    def _(col):
        at = pl.ds(col, step)
        r.sum_own[:, at] = mm_nt(r.grad_pre[...], r.up[at, :]).astype(LOW)

    for half in range(2):
        sum_two.launch(half)

    def turn(n):
        target = me
        for bit in (1, 2):
            if n & bit:
                target = flip(target, bit)
        return pl.ds(pl.multiple_of(target * columns, columns), columns)

    up_chunks, down_chunks = r.up_sems[1].shape[1], r.down_sems[1].shape[1]
    up_rows, down_rows = columns // up_chunks, inner // down_chunks

    def whole_piece(held, kept, size):
        if held is not None:
            return lambda n, k: held.at[n]
        return lambda n, k: kept.at[:, pl.ds(n * size, size)]

    def stage_part(rows, size):
        return [r.stage_down.at[n, pl.ds(0, rows), pl.ds(0, size)] for n in range(3)]

    sums = types.SimpleNamespace(
        up=PieceSum(
            lambda n, k: r.up.at[pl.ds(n * columns + k * up_rows, up_rows)],
            r.up_near,
            r.up_far,
            r.up_last,
            [r.stage_up.at[n] for n in range(3)],
            r.up_sems,
            up_chunks,
        ),
        down=PieceSum(
            lambda n, k: r.down.at[n, pl.ds(k * down_rows, down_rows)],
            r.down_near,
            r.down_far,
            r.down_last,
            [r.stage_down.at[n] for n in range(3)],
            r.down_sems,
            down_chunks,
        ),
        output=PieceSum(
            whole_piece(getattr(r, "output_piece", None), r.grad_pre, columns),
            r.output_near,
            r.output_far,
            r.output_last,
            stage_part(query_width, columns),
            r.output_sems,
            1,
        ),
        query=PieceSum(
            whole_piece(getattr(r, "query_piece", None), r.hidden, query_width),
            r.query_near,
            r.query_far,
            r.query_last,
            stage_part(columns, query_width),
            r.query_sems,
            1,
        ),
        pair=PieceSum(
            lambda n, k: r.pair_piece.at[n],
            r.pair_near,
            r.pair_far,
            r.pair_last,
            stage_part(columns, 2 * HD),
            r.pair_sems,
            1,
        ),
    )

    def up_terms(n):
        left = r.input_two[:, turn(n)]

        @tiles(inner, step)
        def _(q):
            part = mm_tn(left, r.grad_pre[:, pl.ds(q, step)])
            r.up[pl.ds(n * columns, columns), pl.ds(q, step)] = part.astype(LOW)

    def down_terms(n):
        right = r.grad_feed[:, turn(n)]

        @tiles(inner, step)
        def _(q):
            r.down[n, pl.ds(q, step), :] = mm_tn(r.hidden[:, pl.ds(q, step)], right).astype(LOW)

    def feed_terms(block):
        at = pl.ds(block * columns, columns)
        r.feed_own[:, at] = mm(r.hidden[...], r.down[block]).astype(LOW)

    def home_two(half, k):
        rows = line.at(half, k)
        unit, scaled = norm_of(r.middle[pl.ds(k * step_rows, step_rows), :])
        upstream = sum_two.total(half, k)
        note(r.early, 0, upstream * unit)
        note(r.early, 1, upstream)
        own = r.grad_feed[rows, :].astype(WIDE)
        note(r.early, 3, own)
        grad = own + norm_backward(upstream, unit, scaled, vector(3))
        r.grad_middle[pl.ds(k * step_rows, step_rows), :] = grad
        rounded = grad.astype(LOW)
        note(r.early, 2, rounded.astype(WIDE))
        r.grad_branch[rows, :] = rounded
        spread_branch.begin(half, k)

    tasks, late, held_first, held_second = [], [], [], []

    def flush_first():
        for one, k in held_first:
            one.add_first(k)
            late.append((one, k))
        del held_first[:]

    def first(one, k):
        flush_first()
        one.fetch_first(k)
        held_first.append((one, k))

    def flush_second():
        for one, k in held_second:
            one.add_second(k)
        del held_second[:]

    def fetch_second():
        flush_second()
        for one, k in late[:1]:
            one.fetch_second(k)
            held_second.append((one, k))
        del late[:1]

    def terms_and_start(work, n, one, which):
        work(n)
        one.start(which)

    def begin(one, terms):
        plan(terms_and_start, terms, 1, one, 0)
        plan(terms_and_start, terms, 3, one, 1)
        plan(terms, 2)
        plan(terms, 0)

    def plan(work, *given):
        tasks.append(functools.partial(work, *given))

    def work_on(count):
        for task in tasks[:count]:
            task()
        del tasks[:count]

    begin(sums.up, up_terms)
    for k in range(up_chunks):
        plan(first, sums.up, k)
    plan(flush_first)
    for block in range(fsdp):
        plan(feed_terms, block)
    begin(sums.down, down_terms)
    for k in range(down_chunks):
        plan(first, sums.down, k)
    plan(flush_first)

    work_on(2)
    r.grad_pairs[...] = jnp.zeros_like(r.grad_pairs)

    def home_feed(half, k):
        rows = line.at(half, k)
        feed = sum_feed.total(half, k) + vector(5)
        total = r.middle[pl.ds(k * step_rows, step_rows), :] + feed
        slot = place * tokens + half * line.half + k * step_rows
        slots = slot + lax.broadcasted_iota(jnp.int32, (step_rows, width), 0)
        keep = jnp.where(slots < length, 1.0, 0.0)
        note(r.late, 2, keep * total * total)
        note(r.late, 4, keep * feed * feed)
        r.feed_own[rows, :] = (keep * total).astype(LOW)
        spread_result.begin(half, k, r.feed_own)

    def attend_share(start):
        rows = pl.ds(start, share)
        total = mm_nt(r.grad_branch[rows, pl.ds(0, columns)], r.output[0])
        for block in range(1, fsdp):
            total += mm_nt(r.grad_branch[rows, pl.ds(block * columns, columns)], r.output[block])
        r.grad_mixture[...] = total.astype(LOW)
        keys = r.pairs[:, pl.ds(0, HD)]
        values = r.pairs[:, pl.ds(HD, HD)]
        shape = (share, keys.shape[0])
        query_at = place * tokens + start + lax.broadcasted_iota(jnp.int32, shape, 0)
        key_at = lax.broadcasted_iota(jnp.int32, shape, 1)
        allowed = (key_at <= query_at) & (key_at < length)
        factor = 1.0 / math.sqrt(HD)
        for head in range(heads):
            at = pl.ds(head * HD, HD)
            query = r.queries[rows, at]
            grad_mix = r.grad_mixture[:, at]
            scores = jnp.where(allowed, mm_nt(query, keys) * factor, NEGATIVE)
            soft = jnp.exp(scores - r.log_total[rows, pl.ds(head, 1)])
            grad_soft = mm_nt(grad_mix, values)
            dot_rows = jnp.sum(soft * grad_soft, -1, keepdims=True)
            grad_scores = (soft * (grad_soft - dot_rows) * factor).astype(LOW)
            r.grad_queries[rows, at] = mm(grad_scores, keys).astype(LOW)
            r.grad_pairs[:, pl.ds(0, HD)] += mm_tn(grad_scores, query)
            r.grad_pairs[:, pl.ds(HD, HD)] += mm_tn(soft.astype(LOW), grad_mix)

    every = (TP, FSDP, CTX)
    sum_early = RowSum(r.early, r.early_came, r.row_sems.at[0], every)
    sum_late = RowSum(r.late, r.late_came, r.row_sems.at[1], every)
    sum_rows = RowSum(r.own, r.own_came, r.row_sems.at[2], (FSDP, CTX))
    flow_two = Flow(sum_two, spread_branch, home_two, LAG)
    flow_feed = Flow(sum_feed, spread_result, home_feed, LAG)
    starts = [half * line.half + group * share for group in range(tp // 2) for half in range(2)]
    per_share = share // step_rows
    for n in range(flow_two.steps):
        flow_two.advance(1)
        if n == flow_two.steps - 4:
            flow_feed.launch()
        work_on(1)
        if n % 3 == 1:
            flush_second()
        if n >= 6 and n % 3 == 0:
            fetch_second()
        group = tp // 2 - (len(starts) + 1) // 2
        if starts and n >= flow_two.ready((group + 1) * per_share - 1):
            attend_share(starts.pop(0))
    work_on(len(tasks))
    for start in starts:
        attend_share(start)
        flow_feed.advance(1)
        fetch_second()
    sum_early.start()

    def pair_out(other):
        target = lax.rem(place + other, ctx)
        rows = pl.ds(pl.multiple_of(target * tokens, tokens), tokens)
        r.pair_sent[other - 1] = r.grad_pairs[rows, :].astype(LOW)
        return send(
            r.pair_sent.at[other - 1],
            r.pair_came.at[other - 1],
            r.pair_ctx_sem.at[0, other - 1],
            r.pair_ctx_sem.at[1, other - 1],
            CTX,
            target,
        )

    ctx_copies = [pair_out(other) for other in range(1, ctx)]
    for copy in ctx_copies:
        copy.start()
    sum_two.drain()

    def output_terms(n):
        terms = mm_tn(r.mixture[...], r.grad_branch[:, turn(n)])
        sums.output.piece(n, 0)[...] = terms.astype(LOW)

    def query_terms(n):
        terms = mm_tn(r.input_two[:, turn(n)], r.grad_queries[...])
        sums.query.piece(n, 0)[...] = terms.astype(LOW)

    def pair_terms(n):
        terms = mm_tn(r.input_two[:, turn(n)], r.pair_all[...].reshape(tokens, 2 * HD))
        r.pair_piece[n] = terms.astype(LOW)

    loads_one = pltpu.make_async_copy(r.input_one_hbm, r.input_two, r.load_sem.at[1])
    loads_one.start()
    begin(sums.output, output_terms)
    work_on(2)
    flow_feed.advance(1)
    flush_second()
    for copy in ctx_copies:
        copy.wait()
    own_rows = pl.ds(pl.multiple_of(place * tokens, tokens), tokens)
    own_pairs = r.grad_pairs[own_rows, :]
    for other in range(1, ctx):
        own_pairs += r.pair_came[other - 1].astype(WIDE)
    r.pair_own[...] = own_pairs.astype(LOW).reshape(r.pair_own.shape)

    @tiles(width, step)
    def _(col):
        at = pl.ds(col, step)
        part = mm_nt(r.grad_queries[...], r.query[at, :])
        part += mm_nt(r.pair_own[...].reshape(tokens, 2 * HD), r.pair[at, :])
        r.sum_own[:, at] = part.astype(LOW)

    def pair_line(other):
        target = lax.rem(zone + other, tp)
        return send(
            r.pair_own.at[target],
            r.pair_terms.at[other - 1],
            r.pair_line_sem.at[0, other - 1],
            r.pair_line_sem.at[1, other - 1],
            TP,
            target,
        )

    def pair_spread(other):
        return send(
            r.pair_all.at[zone],
            r.pair_all.at[zone],
            r.pair_line_sem.at[2, other - 1],
            r.pair_line_sem.at[3, other - 1],
            TP,
            lax.rem(zone + other, tp),
        )

    def pair_begin():
        for other in range(1, tp):
            pair_line(other).start()
        r.own[pl.ds(1, 1), pl.ds(0, query_width)] = jnp.sum(
            r.grad_queries[...].astype(WIDE), 0, keepdims=True
        )

    def pair_shares():
        total = r.pair_own[zone].astype(WIDE)
        for other in range(1, tp):
            pair_line(other).wait_recv()
            total += r.pair_terms[other - 1].astype(WIDE)
        r.pair_all[zone] = total.astype(LOW)
        for other in range(1, tp):
            pair_spread(other).start()

    def pair_gathered():
        for other in range(1, tp):
            pair_spread(other).wait_recv()
        values = r.pair_all[...].reshape(tokens, 2 * HD)[:, HD:]
        r.own[pl.ds(2, 1), pl.ds(0, HD)] = jnp.sum(values.astype(WIDE), 0, keepdims=True)

    def home_one(half, k):
        rows = line.at(half, k)
        here = pl.ds(k * step_rows, step_rows)
        unit, scaled = norm_of(r.stream[here, :].astype(WIDE))
        upstream = sum_one.total(half, k)
        note(r.late, 0, upstream * unit)
        note(r.late, 1, upstream)
        grad = r.grad_middle[here, :] + norm_backward(upstream, unit, scaled, vector(0))
        r.sum_own[rows, :] = grad.astype(LOW)
        spread_stream.begin(half, k, r.sum_own)

    flow_one = Flow(sum_one, spread_stream, home_one, LAG)
    flow_one.launch()
    pair_begin()
    plan(first, sums.output, 0)
    plan(flush_first)
    plan(loads_one.wait)
    begin(sums.query, query_terms)
    plan(pair_shares)
    plan(first, sums.query, 0)
    plan(flush_first)
    plan(pair_gathered)
    begin(sums.pair, pair_terms)
    plan(first, sums.pair, 0)
    plan(flush_first)
    plan(sum_rows.start)
    stream_load.wait()
    late_on = False
    for n in range(flow_one.steps):
        flow_one.advance(1)
        flow_feed.advance(1)
        work_on(2)
        if n % 2 == 0:
            fetch_second()
        if n % 2 == 1:
            flush_second()
        if n % 2 == 1:
            sum_early.move()
        sum_rows.move()
        if late_on:
            sum_late.move()
        elif flow_one.all_home() and flow_feed.all_home():
            sum_late.start()
            late_on = True
    work_on(len(tasks))
    flow_feed.advance(flow_feed.steps)
    if not late_on:
        sum_late.start()
    sum_early.finish()
    while late:
        fetch_second()
        flush_second()
        sum_rows.move()
        sum_late.move()
    flush_second()
    sum_rows.finish()
    sum_late.finish()
    mine = pl.ds(pl.multiple_of(me * columns, columns), columns)
    r.small[pl.ds(0, 4), :] = r.early[pl.ds(0, 4), mine]
    r.small[pl.ds(4, 2), :] = r.late[pl.ds(0, 2), mine]
    squares = jnp.sum(r.late[pl.ds(2, 3), pl.ds(0, width)], 1, keepdims=True)
    roots = jnp.sqrt(squares / (r.late[pl.ds(7, 1), pl.ds(0, 1)] * width))
    r.small[pl.ds(8, 3), :] = jnp.broadcast_to(roots, (3, columns))

    for half in range(2):

        @pl.when(line.is_home(half))
        def _():
            rows = pl.ds(half * line.half, line.half)
            copies = [
                pltpu.make_async_copy(r.feed_own.at[rows], r.result.at[rows], r.keep_sem.at[0]),
                pltpu.make_async_copy(r.sum_own.at[rows], r.stream_grad.at[rows], r.keep_sem.at[1]),
            ]
            for copy in copies:
                copy.start()
            for copy in copies:
                copy.wait()

    for one in (sum_feed, sum_one, spread_branch, spread_result, spread_stream):
        one.drain()
    for other in range(1, tp):
        pair_line(other).wait_send()
        pair_spread(other).wait_send()
    for one in vars(sums).values():
        one.finish()


def layer(values):
    fsdp, ctx, tp = lax.axis_size(FSDP), lax.axis_size(CTX), lax.axis_size(TP)
    tokens, width = values.stream.shape
    inner = values.up.shape[1]
    columns = width // fsdp
    share = tokens // tp
    query_width = values.query.shape[1]
    pair_width = 2 * HD
    key_count = ctx * tokens
    dma = pltpu.SemaphoreType.DMA
    wide_row = max(width, inner)
    hops, tp_hops = len(bits_of(FSDP)) + len(bits_of(CTX)), len(bits_of(TP))
    far_outs = dict(
        input_one_hbm=((tokens, width), LOW),
        result=((tokens, width), LOW),
        stream_grad=((tokens, width), LOW),
        up_last=((ctx, columns, inner), LOW),
        up_near=((2, columns, inner), LOW),
        up_far=((columns, inner), LOW),
        down_last=((ctx, inner, columns), LOW),
        down_near=((2, inner, columns), LOW),
        down_far=((inner, columns), LOW),
        output_last=((ctx, query_width, columns), LOW),
        output_near=((2, query_width, columns), LOW),
        output_far=((query_width, columns), LOW),
        query_last=((ctx, columns, query_width), LOW),
        query_near=((2, columns, query_width), LOW),
        query_far=((columns, query_width), LOW),
        pair_last=((ctx, columns, pair_width), LOW),
        pair_near=((2, columns, pair_width), LOW),
        pair_far=((columns, pair_width), LOW),
    )
    scratch = dict(
        up=pltpu.VMEM((width, inner), LOW),
        down=pltpu.VMEM((fsdp, inner, columns), LOW),
        input_two=pltpu.VMEM((tokens, width), LOW),
        grad_feed=pltpu.VMEM((tokens, width), LOW),
        hidden=pltpu.VMEM((tokens, inner), LOW),
        grad_pre=pltpu.VMEM((tokens, inner), LOW),
        work_one=pltpu.VMEM((tokens, columns), WIDE),
        sum_own=pltpu.VMEM((tokens, width), LOW),
        sum_slots=pltpu.VMEM((tokens, width), LOW),
        feed_own=pltpu.VMEM((tokens, width), LOW),
        feed_slots=pltpu.VMEM((tokens, width), LOW),
        grad_branch=pltpu.VMEM((tokens, width), LOW),
        middle=pltpu.VMEM((tokens // 2, width), WIDE),
        grad_middle=pltpu.VMEM((tokens // 2, width), WIDE),
        stream=pltpu.VMEM((tokens // 2, width), LOW),
        output=pltpu.VMEM((fsdp, query_width, columns), LOW),
        query=pltpu.VMEM((width, query_width), LOW),
        pair=pltpu.VMEM((width, pair_width), LOW),
        queries=pltpu.VMEM((tokens, query_width), LOW),
        pairs=pltpu.VMEM((key_count, pair_width), LOW),
        mixture=pltpu.VMEM((tokens, query_width), LOW),
        grad_mixture=pltpu.VMEM((share, query_width), LOW),
        grad_queries=pltpu.VMEM((tokens, query_width), LOW),
        grad_pairs=pltpu.VMEM((key_count, pair_width), WIDE),
        pair_sent=pltpu.VMEM((ctx - 1, tokens, pair_width), LOW),
        pair_came=pltpu.VMEM((ctx - 1, tokens, pair_width), LOW),
        pair_own=pltpu.VMEM((tp, share, pair_width), LOW),
        pair_terms=pltpu.VMEM((tp - 1, share, pair_width), LOW),
        pair_all=pltpu.VMEM((tp, share, pair_width), LOW),
        pair_piece=pltpu.VMEM((fsdp, columns, pair_width), LOW),
        stage_up=pltpu.VMEM((3, columns // 4, inner), LOW),
        stage_down=pltpu.VMEM((3, inner // 4, columns), LOW),
        smalls=pltpu.VMEM((fsdp,) + values.packed.shape, WIDE),
        vectors=pltpu.VMEM((8, wide_row), WIDE),
        squares=pltpu.VMEM((1, width), WIDE),
        log_total=pltpu.VMEM((tokens, query_width // HD), WIDE),
        front_sems=line_sems(tokens),
        spread_sems=line_sems(tokens),
        query_gather=Gather.sems(2),
        pair_gather=Gather.sems(2),
        output_gather=Gather.sems(1),
        up_gather=Gather.sems(2),
        down_gather=Gather.sems(2),
        small_sem=dma((2, fsdp - 1)),
        exchange_sem=dma((2, ctx - 1)),
        load_sem=dma((3,)),
        early=pltpu.VMEM((8, wide_row), WIDE),
        late=pltpu.VMEM((8, wide_row), WIDE),
        early_came=pltpu.VMEM((hops + tp_hops, 8, wide_row), WIDE),
        late_came=pltpu.VMEM((hops + tp_hops, 8, wide_row), WIDE),
        own_came=pltpu.VMEM((hops, 8, wide_row), WIDE),
        row_sems=dma((3, 2, hops + tp_hops)),
        keep_sem=dma((2,)),
        pair_ctx_sem=dma((2, ctx - 1)),
        pair_line_sem=dma((4, tp - 1)),
        two_sems=line_sems(tokens),
        feed_sems=line_sems(tokens),
        one_sems=line_sems(tokens),
        branch_sems=line_sems(tokens),
        result_sems=line_sems(tokens),
        stream_sems=line_sems(tokens),
        up_sems=PieceSum.sems(4),
        down_sems=PieceSum.sems(4),
        output_sems=PieceSum.sems(1),
        query_sems=PieceSum.sems(1),
        pair_sems=PieceSum.sems(1),
    )
    if tokens != query_width or inner < width:
        scratch.update(output_piece=pltpu.VMEM((fsdp, query_width, columns), LOW))
    if tokens != columns or inner < fsdp * query_width:
        scratch.update(query_piece=pltpu.VMEM((fsdp, columns, query_width), LOW))
    return call_kernel(
        layer_body,
        1,
        dict(
            stream_hbm=values.stream,
            cotangent_hbm=values.cotangent,
            query_shard=values.query,
            pair_shard=values.pair,
            output_shard=values.output,
            up_shard=values.up,
            down_shard=values.down,
        ),
        dict(packed=values.packed),
        dict(lengths=values.lengths),
        far_outs,
        dict(small=((16, columns), WIDE), own=((8, wide_row), WIDE)),
        scratch,
    )


def body(
    stream,
    cotangent,
    lengths,
    first_gain,
    first_shift,
    query_weight,
    query_bias,
    pair_weight,
    value_bias,
    output_weight,
    output_bias,
    second_gain,
    second_shift,
    up_weight,
    up_bias,
    down_weight,
    down_bias,
):
    fsdp = lax.axis_size(FSDP)
    me = lax.axis_index(FSDP)
    seq_count, group_len, width = stream.shape
    tokens = seq_count * group_len
    columns, inner = first_gain.shape[0], up_weight.shape[1]

    def placed(bias):
        spots = jnp.arange(fsdp)[None, :, None] == me
        return jnp.where(spots, bias.reshape(-1, 1, bias.shape[-1]).astype(WIDE), 0.0).reshape(-1)

    def row(values):
        return jnp.pad(values.astype(WIDE), (0, columns - values.shape[0]))[None]

    vectors = (first_gain, first_shift, output_bias, second_gain, second_shift, down_bias)
    packed = jnp.concatenate(
        [row(vector) for vector in vectors]
        + [row(placed(query_bias)), row(placed(value_bias.reshape(1, -1)))]
        + [placed(up_bias).reshape(-1, columns)]
    )
    packed = jnp.pad(packed, ((0, -packed.shape[0] % 8), (0, 0)))
    values = types.SimpleNamespace(
        stream=stream.reshape(tokens, width),
        cotangent=cotangent.reshape(tokens, width),
        lengths=lengths,
        packed=packed,
        query=query_weight,
        pair=pair_weight,
        output=output_weight,
        up=up_weight,
        down=down_weight,
    )
    ended = types.SimpleNamespace(**layer(values))
    small, own = ended.small, ended.own
    query_width = query_weight.shape[1]

    def finished(last):
        return jnp.sum(last.astype(WIDE), 0)

    up_bias_all = own[0, :inner].reshape(up_bias.shape[0], fsdp, -1)
    query_bias_all = own[1, :query_width].reshape(query_bias.shape[0], fsdp, -1)
    value_size = value_bias.shape[0]
    return (
        ended.result.reshape(stream.shape),
        ended.stream_grad.reshape(stream.shape),
        small[4],
        small[5],
        finished(ended.query_last),
        lax.dynamic_index_in_dim(query_bias_all, me, 1, False),
        finished(ended.pair_last),
        lax.dynamic_slice_in_dim(own[2], me * value_size, value_size, 0),
        finished(ended.output_last),
        small[2],
        small[0],
        small[1],
        finished(ended.up_last),
        lax.dynamic_index_in_dim(up_bias_all, me, 1, False),
        finished(ended.down_last),
        small[3],
        small[8:11, 0],
    )


def solution(mesh):
    in_specs = (
        P(FSDP, CTX, None),
        P(FSDP, CTX, None),
        P(FSDP),
        P(FSDP),
        P(FSDP),
        P(FSDP, TP),
        P(TP, FSDP),
        P(FSDP, None),
        P(FSDP),
        P(TP, FSDP),
        P(FSDP),
        P(FSDP),
        P(FSDP),
        P(FSDP, TP),
        P(TP, FSDP),
        P(TP, FSDP),
        P(FSDP),
    )
    out_specs = (
        P(FSDP, CTX, None),
        P(FSDP, CTX, None),
        P(FSDP),
        P(FSDP),
        P(FSDP, TP),
        P(TP, FSDP),
        P(FSDP, None),
        P(FSDP),
        P(TP, FSDP),
        P(FSDP),
        P(FSDP),
        P(FSDP),
        P(FSDP, TP),
        P(TP, FSDP),
        P(TP, FSDP),
        P(FSDP),
        P(),
    )
    return jax.shard_map(body, mesh=mesh, in_specs=in_specs, out_specs=out_specs, check_vma=False)
```

```python
import functools
import math
import types

import jax
import jax.numpy as jnp
from jax import lax
from jax.experimental import pallas as pl
from jax.experimental.pallas import tpu as pltpu
from jax.sharding import PartitionSpec as P

HD = 128
EPSILON = 1e-05
NEGATIVE = -1e30
FSDP, CTX, TP = "fsdp", "ctx", "tp"
LOW, WIDE = jnp.bfloat16, jnp.float32
MESH = pl.DeviceIdType.MESH
VMEM_BYTES = 60 << 20
SKEW, LAG = 2, 2


def flip(place, bit):
    return place + bit - 2 * bit * lax.rem(lax.div(place, bit), 2)


def bits_of(axis):
    count, bit, found = lax.axis_size(axis), 1, []
    while bit < count:
        found.append(bit)
        bit *= 2
    return found


def mm(left, right):
    return jnp.dot(left, right, preferred_element_type=WIDE)


def mm_nt(left, right):
    return lax.dot_general(left, right, (((1,), (1,)), ((), ())), preferred_element_type=WIDE)


def mm_tn(left, right):
    return lax.dot_general(left, right, (((0,), (0,)), ((), ())), preferred_element_type=WIDE)


def tiles(count, step):
    def run(work):
        def once(index, carry):
            work(pl.multiple_of(index * step, step))
            return carry

        lax.fori_loop(0, count // step, once, 0)

    return run


def norm_of(values):
    center = values - jnp.mean(values, -1, keepdims=True)
    scaled = lax.rsqrt(jnp.mean(center * center, -1, keepdims=True) + EPSILON)
    return center * scaled, scaled


def norm_backward(upstream, unit_rows, scaled, norm_gain):
    gained = upstream * norm_gain
    return scaled * (
        gained
        - jnp.mean(gained, -1, keepdims=True)
        - unit_rows * jnp.mean(gained * unit_rows, -1, keepdims=True)
    )


def send(source, target, outgo, income, axis, place):
    return pltpu.make_async_remote_copy(
        src_ref=source,
        dst_ref=target,
        send_sem=outgo,
        recv_sem=income,
        device_id={axis: place},
        device_id_type=MESH,
    )


def all_peers():
    me, place, zone = lax.axis_index(FSDP), lax.axis_index(CTX), lax.axis_index(TP)
    ctx, tp = lax.axis_size(CTX), lax.axis_size(TP)
    peers = [(FSDP, flip(me, 1)), (FSDP, flip(me, 2)), (FSDP, flip(flip(me, 1), 2))]
    peers += [(CTX, lax.rem(place + k, ctx)) for k in range(1, ctx)]
    peers += [(TP, lax.rem(zone + k, tp)) for k in range(1, tp)]
    return peers


def greet(peers):
    barrier = pltpu.get_barrier_semaphore()
    for axis, place in peers:
        pl.semaphore_signal(barrier, inc=1, device_id={axis: place}, device_id_type=MESH)
    return lambda: pl.semaphore_wait(barrier, len(peers))


def split_rows(tokens):
    rows = 32 if tokens % 512 == 0 else 16
    return rows, tokens // 2 // rows


class Line:
    def __init__(self, tokens):
        self.place, self.count = lax.axis_index(TP), lax.axis_size(TP)
        self.rows, self.chunks = split_rows(tokens)
        self.half = tokens // 2

    def at(self, half, k):
        start = half * self.half + k * self.rows
        return pl.ds(start if isinstance(start, int) else pl.multiple_of(start, self.rows), self.rows)

    def is_home(self, half):
        return self.place == (0 if half == 0 else self.count - 1)

    def is_far(self, half):
        return self.place == (self.count - 1 if half == 0 else 0)

    def toward(self, half):
        move = self.count - 1 if half == 0 else 1
        return lax.rem(self.place + move, self.count)

    def away(self, half):
        return self.toward(1 - half)


class LineSum(Line):
    def __init__(self, own, slots, sems):
        super().__init__(own.shape[0])
        self.own, self.slots = own, slots
        self.outgo, self.income = sems

    def copy(self, half, k):
        rows = self.at(half, k)
        return send(
            self.own.at[rows],
            self.slots.at[rows],
            self.outgo.at[half, k],
            self.income.at[half, k],
            TP,
            self.toward(half),
        )

    def launch(self, half, first=0, last=None):
        @pl.when(self.is_far(half))
        def _():
            for k in range(first, self.chunks if last is None else last):
                self.copy(half, k).start()

    def total(self, half, k):
        rows = self.at(half, k)
        return self.own[rows, :].astype(WIDE) + self.slots[rows, :].astype(WIDE)

    def pass_on(self, half, k):
        self.copy(half, k).wait_recv()
        self.own[self.at(half, k), :] = self.total(half, k).astype(LOW)
        self.copy(half, k).start()

    def drain(self):
        for half in range(2):

            @pl.when(jnp.logical_not(self.is_home(half)))
            def _():
                for k in range(self.chunks):
                    self.copy(half, k).wait_send()


class LineSpread(Line):
    def __init__(self, held, sems):
        super().__init__(held.shape[0])
        self.held = held
        self.outgo, self.income = sems

    def copy(self, half, k, source=None):
        rows = self.at(half, k)
        return send(
            self.held.at[rows] if source is None else source.at[rows],
            self.held.at[rows],
            self.outgo.at[half, k],
            self.income.at[half, k],
            TP,
            self.away(half),
        )

    def begin(self, half, k, source=None):
        self.copy(half, k, source).start()

    def serve(self, half, k):
        self.copy(half, k).wait_recv()

        @pl.when(jnp.logical_not(self.is_far(half)))
        def _():
            self.copy(half, k).start()

    def drain(self):
        for half in range(2):

            @pl.when(jnp.logical_not(self.is_far(half)))
            def _():
                for k in range(self.chunks):
                    self.copy(half, k).wait_send()


class Flow(Line):
    def __init__(self, line_sum, spread, home, lag):
        super().__init__(line_sum.own.shape[0])
        self.sum, self.spread, self.home, self.lag = line_sum, spread, home, lag
        self.now = 0
        self.to_home = SKEW * (self.count - 2)
        self.steps = self.chunks + lag + 2 * self.to_home

    def launch(self, first=0, last=None):
        for half in range(2):
            self.sum.launch(half, first, last)

    def inside(self, k):
        return (k >= 0) & (k < self.chunks)

    def advance(self, count=1):
        for n in range(self.now, min(self.now + count, self.steps)):
            self.step(n)
        self.now = min(self.now + count, self.steps)

    def step(self, n):
        last = self.count - 1
        at_home = n - self.to_home
        for half in range(2):
            hops = last - self.place if half == 0 else self.place
            k = n - SKEW * (hops - 1)

            @pl.when((hops >= 1) & (hops < last) & self.inside(k))
            def _():
                self.sum.pass_on(half, k)

            if 0 <= at_home < self.chunks:

                @pl.when(self.is_home(half))
                def _():
                    self.sum.copy(half, at_home).wait_recv()
                    self.home(half, at_home)

        for half in range(2):
            hops = self.place if half == 0 else last - self.place
            k = at_home - self.lag - SKEW * (hops - 1)

            @pl.when((hops >= 1) & self.inside(k))
            def _():
                self.spread.serve(half, k)

    def all_home(self):
        return self.now >= self.chunks + self.to_home

    def ready(self, chunk):
        return chunk + self.lag + 2 * self.to_home


class Gather:
    def __init__(self, shard, held, sems, cut):
        self.shard, self.held = shard, held
        self.me, self.place = lax.axis_index(FSDP), lax.axis_index(CTX)
        self.ctx = lax.axis_size(CTX)
        self.cut = cut
        self.rows = shard.shape[0] // self.ctx // cut
        self.near_sem, self.far_sem, self.side_sem, self.pass_sem, self.local = sems

    def part(self, place, k):
        return pl.ds(pl.multiple_of((place * self.cut + k) * self.rows, self.rows), self.rows)

    def keep(self):
        every = pl.ds(0, self.shard.shape[0])
        return pltpu.make_async_copy(self.shard, self.held(self.me, every), self.local.at[0])

    def near(self):
        every = pl.ds(0, self.shard.shape[0])
        return send(
            self.shard,
            self.held(self.me, every),
            self.near_sem.at[0],
            self.near_sem.at[1],
            FSDP,
            flip(self.me, 1),
        )

    def far(self, k):
        part = self.part(self.place, k)
        return send(
            self.shard.at[part],
            self.held(self.me, part),
            self.far_sem.at[0, k],
            self.far_sem.at[1, k],
            FSDP,
            flip(self.me, 2),
        )

    def side(self, other, k):
        held = self.held(flip(self.me, 2), self.part(self.place, k))
        return send(
            held,
            held,
            self.side_sem.at[0, other - 1, k],
            self.side_sem.at[1, other - 1, k],
            CTX,
            lax.rem(self.place + other, self.ctx),
        )

    def over(self, other, k):
        place = lax.rem(self.place + self.ctx - other, self.ctx)
        held = self.held(flip(self.me, 2), self.part(place, k))
        return send(
            held,
            held,
            self.pass_sem.at[0, other, k],
            self.pass_sem.at[1, other, k],
            FSDP,
            flip(self.me, 1),
        )

    def start(self):
        for k in range(self.cut):
            self.far(k).start()
        self.near().start()
        self.keep().start()

    def cross(self, k):
        self.far(k).wait_recv()
        for other in range(1, self.ctx):
            self.side(other, k).start()
        self.over(0, k).start()

    def pass_on(self, k):
        for other in range(1, self.ctx):
            self.side(other, k).wait_recv()
            self.over(other, k).start()

    def ready(self):
        self.keep().wait()
        self.near().wait_recv()
        for k in range(self.cut):
            for other in range(self.ctx):
                self.over(other, k).wait_recv()

    def drain(self):
        self.near().wait_send()
        for k in range(self.cut):
            self.far(k).wait_send()
            for other in range(self.ctx):
                self.over(other, k).wait_send()
                if other > 0:
                    self.side(other, k).wait_send()

    @staticmethod
    def sems(cut):
        ctx = lax.axis_size(CTX)
        shapes = ((2,), (2, cut), (2, ctx - 1, cut), (2, ctx, cut), (1,))
        return tuple(pltpu.SemaphoreType.DMA(shape) for shape in shapes)


class PieceSum:
    def __init__(self, piece, near, far, last, stages, sems, chunks):
        self.piece, self.near, self.far, self.last = piece, near, far, last
        self.stages, self.chunks = stages, chunks
        self.rows = far.shape[0] // chunks
        self.near_sem, self.far_sem, self.last_sem, self.local = sems
        self.me, self.place = lax.axis_index(FSDP), lax.axis_index(CTX)
        self.ctx = lax.axis_size(CTX)

    def part(self, k):
        return pl.ds(k * self.rows, self.rows)

    def near_copy(self, which, k):
        return send(
            self.piece(2 * which + 1, k),
            self.near.at[which, self.part(k)],
            self.near_sem.at[0, which, k],
            self.near_sem.at[1, which, k],
            FSDP,
            flip(self.me, 1),
        )

    def far_copy(self, k):
        return send(
            self.piece(2, k),
            self.far.at[self.part(k)],
            self.far_sem.at[0, k],
            self.far_sem.at[1, k],
            FSDP,
            flip(self.me, 2),
        )

    def last_copy(self, other, k):
        return send(
            self.piece(0, k),
            self.last.at[self.place, self.part(k)],
            self.last_sem.at[0, other - 1, k],
            self.last_sem.at[1, other - 1, k],
            CTX,
            lax.rem(self.place + other, self.ctx),
        )

    def own_copy(self, k):
        return pltpu.make_async_copy(
            self.piece(0, k), self.last.at[self.place, self.part(k)], self.local.at[3 + k]
        )

    def start(self, which):
        for k in range(self.chunks):
            self.near_copy(which, k).start()

    def load(self, source, index):
        return pltpu.make_async_copy(source, self.stages[index], self.local.at[index])

    def add(self, r, k, index):
        step = 32 if self.rows % 32 == 0 else 16
        piece, stage = self.piece(r, k), self.stages[index]

        @tiles(self.rows, step)
        def _(at):
            here = pl.ds(at, step)
            total = piece[here].astype(WIDE) + stage[here].astype(WIDE)
            piece[here] = total.astype(LOW)

    def fetch_first(self, k):
        for which in range(2):
            self.near_copy(which, k).wait_recv()
        for which in range(2):
            self.load(self.near.at[which, self.part(k)], which).start()

    def add_first(self, k):
        self.load(self.near.at[1, self.part(k)], 1).wait()
        self.add(2, k, 1)
        self.far_copy(k).start()
        self.load(self.near.at[0, self.part(k)], 0).wait()
        self.add(0, k, 0)

    def fetch_second(self, k):
        self.far_copy(k).wait_recv()
        self.load(self.far.at[self.part(k)], 2).start()

    def add_second(self, k):
        self.load(self.far.at[self.part(k)], 2).wait()
        self.add(0, k, 2)
        for other in range(1, self.ctx):
            self.last_copy(other, k).start()
        self.own_copy(k).start()

    def finish(self):
        for k in range(self.chunks):
            for other in range(1, self.ctx):
                self.last_copy(other, k).wait_recv()
                self.last_copy(other, k).wait_send()
            self.own_copy(k).wait()
            self.far_copy(k).wait_send()
            for which in range(2):
                self.near_copy(which, k).wait_send()

    @staticmethod
    def sems(chunks):
        ctx = lax.axis_size(CTX)
        shapes = ((2, 2, chunks), (2, chunks), (2, ctx - 1, chunks), (3 + chunks,))
        return tuple(pltpu.SemaphoreType.DMA(shape) for shape in shapes)


class RowSum:
    def __init__(self, rows, came, sems, axes):
        self.rows, self.came, self.sems = rows, came, sems
        self.hops = [(axis, bit) for axis in axes for bit in bits_of(axis)]
        self.now = len(self.hops)

    def copy(self, n):
        axis, bit = self.hops[n]
        return send(
            self.rows,
            self.came.at[n],
            self.sems.at[0, n],
            self.sems.at[1, n],
            axis,
            flip(lax.axis_index(axis), bit),
        )

    def start(self):
        self.now = 0
        self.copy(0).start()

    def move(self):
        if self.now == len(self.hops):
            return False
        self.copy(self.now).wait()
        self.rows[...] += self.came[self.now]
        self.now += 1
        if self.now < len(self.hops):
            self.copy(self.now).start()
        return True

    def finish(self):
        while self.move():
            pass


def line_sems(tokens):
    rows, chunks = split_rows(tokens)
    return tuple(pltpu.SemaphoreType.DMA((2, chunks)) for _ in range(2))


def call_kernel(body, ident, far, near, scalars, far_outs, near_outs, scratch):
    groups = (far, near, scalars)
    spaces = (pl.ANY, pltpu.VMEM, pltpu.SMEM)
    arrays, in_specs = [], []
    for group, space in zip(groups, spaces):
        arrays += list(group.values())
        in_specs += [pl.BlockSpec(memory_space=space)] * len(group)
    outs = dict(far_outs, **near_outs)
    out_specs = [pl.BlockSpec(memory_space=pl.ANY)] * len(far_outs)
    out_specs += [pl.BlockSpec(memory_space=pltpu.VMEM)] * len(near_outs)
    shapes, tree = jax.tree.flatten(scratch)
    ins = [name for group in groups for name in group]

    def kernel(*refs):
        held = dict(zip(ins + list(outs), refs))
        held.update(jax.tree.unflatten(tree, refs[len(ins) + len(outs) :]))
        body(types.SimpleNamespace(**held))

    given = pl.pallas_call(
        kernel,
        out_shape=[jax.ShapeDtypeStruct(shape, kind) for shape, kind in outs.values()],
        in_specs=in_specs,
        out_specs=out_specs,
        scratch_shapes=shapes,
        compiler_params=pltpu.CompilerParams(
            collective_id=ident, has_side_effects=True, vmem_limit_bytes=VMEM_BYTES
        ),
    )(*arrays)
    return dict(zip(outs, given))


def front_part(r):
    me, place, zone = lax.axis_index(FSDP), lax.axis_index(CTX), lax.axis_index(TP)
    fsdp, ctx, tp = lax.axis_size(FSDP), lax.axis_size(CTX), lax.axis_size(TP)
    tokens, width = r.stream_hbm.shape
    columns = width // fsdp
    query_width = r.query.shape[1]
    heads = query_width // HD
    inner = r.up.shape[1]
    length = r.lengths[0]
    line = Line(tokens)
    step_rows, chunks = line.rows, line.chunks

    ready = greet(all_peers())
    stream_load = pltpu.make_async_copy(r.stream_hbm, r.feed_own, r.load_sem.at[0])
    stream_load.start()
    cotangent_load = pltpu.make_async_copy(r.cotangent_hbm, r.grad_feed, r.load_sem.at[1])
    cotangent_load.start()

    def block_rows(held):
        size = held.shape[0] // fsdp

        def view(block, rows):
            start = pl.multiple_of(block * size + rows.start, 16)
            return held.at[pl.ds(start, rows.size)]

        return view

    gathers = types.SimpleNamespace(
        query=Gather(r.query_shard, block_rows(r.query), r.query_gather, r.query_gather[1].shape[1]),
        pair=Gather(r.pair_shard, block_rows(r.pair), r.pair_gather, r.pair_gather[1].shape[1]),
        output=Gather(r.output_shard, lambda b, rows: r.output.at[b, rows], r.output_gather, r.output_gather[1].shape[1]),
        up=Gather(r.up_shard, block_rows(r.up), r.up_gather, r.up_gather[1].shape[1]),
        down=Gather(
            r.down_shard, lambda b, rows: r.down.at[b, rows], r.down_gather, r.down_gather[1].shape[1]
        ),
    )

    def small_copy(k):
        target = flip(me, k) if k < 3 else flip(flip(me, 1), 2)
        return send(
            r.smalls.at[0], r.smalls.at[k], r.small_sem.at[0, k - 1], r.small_sem.at[1, k - 1],
            FSDP, target,
        )

    r.smalls[0] = r.packed[...]
    ready()
    for k in range(1, fsdp):
        small_copy(k).start()
    gathers.pair.start()
    gathers.query.start()
    for k in range(1, fsdp):
        small_copy(k).wait()
    query_add = jnp.zeros((1, query_width), WIDE)
    value_add = jnp.zeros((1, HD), WIDE)
    for k in range(fsdp):
        block = me if k == 0 else flip(me, k) if k < 3 else flip(flip(me, 1), 2)
        at = pl.ds(pl.multiple_of(block * columns, columns), columns)
        r.vectors[pl.ds(0, 6), at] = r.smalls[k, pl.ds(0, 6), :]
        query_add += r.smalls[k, pl.ds(6, 1), pl.ds(0, query_width)]
        value_add += r.smalls[k, pl.ds(7, 1), pl.ds(0, HD)]
    for q in range(inner // columns):
        total = jnp.zeros((1, columns), WIDE)
        for k in range(fsdp):
            total += r.smalls[k, pl.ds(8 + q, 1), :]
        r.vectors[pl.ds(6, 1), pl.ds(q * columns, columns)] = total
    r.vectors[pl.ds(7, 1), :] = jnp.zeros((1, r.vectors.shape[1]), WIDE)

    def vector(n):
        return r.vectors[pl.ds(n, 1), pl.ds(0, width)]

    stream_load.wait()
    norm_step = min(32, tokens)

    @tiles(tokens, norm_step)
    def _(row):
        rows = pl.ds(row, norm_step)
        unit, scaled = norm_of(r.feed_own[rows, :].astype(WIDE))
        r.grad_branch[rows, :] = (unit * vector(0) + vector(1)).astype(LOW)

    early = (gathers.pair, gathers.query)
    for k in range(2):
        for one in early:
            one.cross(k)
    for k in range(2):
        for one in early:
            one.pass_on(k)
    for one in (gathers.output, gathers.down, gathers.up):
        one.start()
    gathers.pair.ready()
    own_rows = pl.ds(pl.multiple_of(place * tokens, tokens), tokens)
    key_half = mm(r.grad_branch[...], r.pair[...])
    r.pairs[own_rows, pl.ds(0, HD)] = key_half[:, :HD].astype(LOW)
    r.pairs[own_rows, pl.ds(HD, HD)] = (key_half[:, HD:] + value_add).astype(LOW)

    def pair_copy(other):
        return send(
            r.pairs.at[own_rows],
            r.pairs.at[own_rows],
            r.exchange_sem.at[0, other - 1],
            r.exchange_sem.at[1, other - 1],
            CTX,
            lax.rem(place + other, ctx),
        )

    for other in range(1, ctx):
        pair_copy(other).start()
    gathers.query.ready()
    r.queries[...] = (mm(r.grad_branch[...], r.query[...]) + query_add).astype(LOW)
    input_save = pltpu.make_async_copy(r.grad_branch, r.input_one_hbm, r.load_sem.at[2])
    input_save.start()
    gathers.output.cross(0)
    cotangent_load.wait()

    @tiles(tokens, step_rows)
    def _(row):
        rows = pl.ds(row, step_rows)
        slots = place * tokens + row + lax.broadcasted_iota(jnp.int32, (step_rows, width), 0)
        keep = jnp.where(slots < length, 1.0, 0.0)
        r.grad_feed[rows, :] = (keep * r.grad_feed[rows, :].astype(WIDE)).astype(LOW)

    for other in range(1, ctx):
        pair_copy(other).wait_recv()
    gathers.output.pass_on(0)

    share = min(HD, line.half)
    per_share = share // step_rows
    factor = 1.0 / math.sqrt(HD)

    def attend(start):
        rows = pl.ds(start, share)
        keys = r.pairs[:, pl.ds(0, HD)]
        values = r.pairs[:, pl.ds(HD, HD)]
        shape = (share, keys.shape[0])
        query_at = place * tokens + start + lax.broadcasted_iota(jnp.int32, shape, 0)
        key_at = lax.broadcasted_iota(jnp.int32, shape, 1)
        allowed = (key_at <= query_at) & (key_at < length)
        for head in range(heads):
            at = pl.ds(head * HD, HD)
            scores = jnp.where(allowed, mm_nt(r.queries[rows, at], keys) * factor, NEGATIVE)
            peak = jnp.max(scores, -1, keepdims=True)
            soft = jnp.exp(scores - peak)
            total = jnp.sum(soft, -1, keepdims=True)
            r.mixture[rows, at] = mm((soft / total).astype(LOW), values).astype(LOW)
            r.log_total[rows, pl.ds(head, 1)] = peak + jnp.log(total)

    def project(start):
        rows = pl.ds(start, share)
        for block in range(fsdp):
            at = pl.ds(block * columns, columns)
            r.sum_own[rows, at] = mm(r.mixture[rows, :], r.output[block]).astype(LOW)

    branch_sum = LineSum(r.sum_own, r.sum_slots, r.front_sems)
    spread = LineSpread(r.input_two, r.spread_sems)
    r.squares[...] = jnp.zeros_like(r.squares)

    def home(half, k):
        branch = branch_sum.total(half, k) + vector(2)
        middle = r.feed_own[line.at(half, k), :].astype(WIDE) + branch
        r.middle[pl.ds(k * step_rows, step_rows), :] = middle
        unit, scaled = norm_of(middle)
        r.input_two[line.at(half, k), :] = (unit * vector(3) + vector(4)).astype(LOW)
        spread.begin(half, k)
        slot = place * tokens + half * line.half + k * step_rows
        slots = slot + lax.broadcasted_iota(jnp.int32, (step_rows, width), 0)
        keep = jnp.where(slots < length, 1.0, 0.0)
        r.squares[...] += jnp.sum(keep * branch * branch, 0, keepdims=True)

    big = [(gathers.down, k) for k in range(gathers.down.cut)]
    big += [(gathers.up, k) for k in range(gathers.up.cut)]
    events = []
    for index, (one, k) in enumerate(big):
        events.append(functools.partial(one.cross, k))
        if index > 0:
            before, last = big[index - 1]
            events.append(functools.partial(before.pass_on, last))
    events.append(functools.partial(big[-1][0].pass_on, big[-1][1]))

    def move_on(count):
        for event in events[:count]:
            event()
        del events[:count]

    flow = Flow(branch_sum, spread, home, LAG)
    groups = line.half // share
    for group in range(groups):
        for half in range(2):
            start = half * line.half + group * share
            attend(start)
            if group == 0 and half == 0:
                gathers.output.ready()
            project(start)
        flow.launch(per_share * group, per_share * group + per_share)
        if group < groups - 1:
            flow.advance(1)
            move_on(1)
    def hidden_terms(q):
        at = pl.ds(q * columns, columns)
        total = mm_nt(r.grad_feed[:, pl.ds(0, columns)], r.down[0, at, :])
        for block in range(1, fsdp):
            total += mm_nt(r.grad_feed[:, pl.ds(block * columns, columns)], r.down[block, at, :])
        r.grad_pre[:, at] = total.astype(LOW)

    left = list(range(inner // columns))
    while flow.now < flow.steps:
        flow.advance(1)
        if flow.now % 2 == 0:
            move_on(1)
        if left and flow.now >= flow.steps - len(left):
            if left[0] == 0:
                gathers.down.ready()
            hidden_terms(left.pop(0))
    for q in left:
        hidden_terms(q)
    move_on(len(events))
    input_save.wait()
    branch_sum.drain()

    def end():
        for other in range(1, ctx):
            pair_copy(other).wait_send()
        for one in vars(gathers).values():
            one.drain()
        spread.drain()

    return gathers, end


def layer_body(r):
    gathers, front_end = front_part(r)
    back_part(r, gathers, front_end)


def back_part(r, gathers, front_end):
    me, place, zone = lax.axis_index(FSDP), lax.axis_index(CTX), lax.axis_index(TP)
    fsdp, ctx, tp = lax.axis_size(FSDP), lax.axis_size(CTX), lax.axis_size(TP)
    tokens, width = r.input_two.shape
    inner = r.up.shape[1]
    columns = width // fsdp
    share = tokens // tp
    query_width = r.queries.shape[1]
    heads = query_width // HD
    length = r.lengths[0]
    line = Line(tokens)
    step_rows, chunks = line.rows, line.chunks
    step = columns
    blocks = inner // step

    at_end = jnp.where(zone == tp - 1, tokens // 2, 0)
    stream_part = r.stream_hbm.at[pl.ds(pl.multiple_of(at_end, tokens // 2), tokens // 2)]
    stream_load = pltpu.make_async_copy(stream_part, r.stream, r.load_sem.at[0])
    stream_load.start()
    for rows in (r.early, r.late, r.own):
        rows[...] = jnp.zeros_like(rows)
    r.late[pl.ds(3, 1), pl.ds(0, width)] = r.squares[...]
    counted = jnp.clip(length - place * tokens, 0, tokens).astype(WIDE)
    r.late[pl.ds(7, 1), :] = jnp.full((1, r.late.shape[1]), jnp.where(zone == 0, counted, 0.0))
    def vector(n):
        return r.vectors[pl.ds(n, 1), pl.ds(0, width)]

    def note(rows, row, values):
        rows[pl.ds(row, 1), pl.ds(0, width)] += jnp.sum(values, 0, keepdims=True)

    gathers.up.ready()

    @tiles(inner, step)
    def _(q):
        at = pl.ds(q, step)
        r.work_one[...] = mm(r.input_two[...], r.up[:, at])
        bias = r.vectors[pl.ds(6, 1), at]

        @tiles(tokens, 32)
        def _(row):
            here = pl.ds(row, 32)
            v = r.work_one[here, :] + bias
            square = v * v
            reach = math.sqrt(2.0 / math.pi)
            t = jnp.tanh(reach * v * (1.0 + 0.044715 * square))
            gate = 0.5 * (1.0 + t)
            slope = gate + 0.5 * v * (1.0 - t * t) * reach * (1.0 + 3 * 0.044715 * square)
            r.hidden[here, at] = (v * gate).astype(LOW)
            grad = (r.grad_pre[here, at].astype(WIDE) * slope).astype(LOW)
            r.grad_pre[here, at] = grad
            r.own[pl.ds(0, 1), at] += jnp.sum(grad.astype(WIDE), 0, keepdims=True)

    front_end()
    sum_two = LineSum(r.sum_own, r.sum_slots, r.two_sems)
    sum_feed = LineSum(r.feed_own, r.feed_slots, r.feed_sems)
    sum_one = LineSum(r.sum_own, r.sum_slots, r.one_sems)
    spread_branch = LineSpread(r.grad_branch, r.branch_sems)
    spread_result = LineSpread(r.result, r.result_sems)
    spread_stream = LineSpread(r.stream_grad, r.stream_sems)

    @tiles(width, step)
    def _(col):
        at = pl.ds(col, step)
        r.sum_own[:, at] = mm_nt(r.grad_pre[...], r.up[at, :]).astype(LOW)

    for half in range(2):
        sum_two.launch(half)

    def turn(n):
        target = me
        for bit in (1, 2):
            if n & bit:
                target = flip(target, bit)
        return pl.ds(pl.multiple_of(target * columns, columns), columns)

    up_chunks, down_chunks = r.up_sems[1].shape[1], r.down_sems[1].shape[1]
    up_rows, down_rows = columns // up_chunks, inner // down_chunks

    def whole_piece(held, kept, size):
        if held is not None:
            return lambda n, k: held.at[n]
        return lambda n, k: kept.at[:, pl.ds(n * size, size)]

    def stage_part(rows, size):
        return [r.stage_down.at[n, pl.ds(0, rows), pl.ds(0, size)] for n in range(3)]

    sums = types.SimpleNamespace(
        up=PieceSum(
            lambda n, k: r.up.at[pl.ds(n * columns + k * up_rows, up_rows)],
            r.up_near,
            r.up_far,
            r.up_last,
            [r.stage_up.at[n] for n in range(3)],
            r.up_sems,
            up_chunks,
        ),
        down=PieceSum(
            lambda n, k: r.down.at[n, pl.ds(k * down_rows, down_rows)],
            r.down_near,
            r.down_far,
            r.down_last,
            [r.stage_down.at[n] for n in range(3)],
            r.down_sems,
            down_chunks,
        ),
        output=PieceSum(
            whole_piece(getattr(r, "output_piece", None), r.grad_pre, columns),
            r.output_near,
            r.output_far,
            r.output_last,
            stage_part(query_width, columns),
            r.output_sems,
            1,
        ),
        query=PieceSum(
            whole_piece(getattr(r, "query_piece", None), r.hidden, query_width),
            r.query_near,
            r.query_far,
            r.query_last,
            stage_part(columns, query_width),
            r.query_sems,
            1,
        ),
        pair=PieceSum(
            lambda n, k: r.pair_piece.at[n],
            r.pair_near,
            r.pair_far,
            r.pair_last,
            stage_part(columns, 2 * HD),
            r.pair_sems,
            1,
        ),
    )

    def up_terms(n):
        left = r.input_two[:, turn(n)]

        @tiles(inner, step)
        def _(q):
            part = mm_tn(left, r.grad_pre[:, pl.ds(q, step)])
            r.up[pl.ds(n * columns, columns), pl.ds(q, step)] = part.astype(LOW)

    def down_terms(n):
        right = r.grad_feed[:, turn(n)]

        @tiles(inner, step)
        def _(q):
            r.down[n, pl.ds(q, step), :] = mm_tn(r.hidden[:, pl.ds(q, step)], right).astype(LOW)

    def feed_terms(block):
        at = pl.ds(block * columns, columns)
        r.feed_own[:, at] = mm(r.hidden[...], r.down[block]).astype(LOW)

    def home_two(half, k):
        rows = line.at(half, k)
        unit, scaled = norm_of(r.middle[pl.ds(k * step_rows, step_rows), :])
        upstream = sum_two.total(half, k)
        note(r.early, 0, upstream * unit)
        note(r.early, 1, upstream)
        own = r.grad_feed[rows, :].astype(WIDE)
        note(r.early, 3, own)
        grad = own + norm_backward(upstream, unit, scaled, vector(3))
        r.grad_middle[pl.ds(k * step_rows, step_rows), :] = grad
        rounded = grad.astype(LOW)
        note(r.early, 2, rounded.astype(WIDE))
        r.grad_branch[rows, :] = rounded
        spread_branch.begin(half, k)

    tasks, late, held_first, held_second = [], [], [], []

    def flush_first():
        for one, k in held_first:
            one.add_first(k)
            late.append((one, k))
        del held_first[:]

    def first(one, k):
        flush_first()
        one.fetch_first(k)
        held_first.append((one, k))

    def flush_second():
        for one, k in held_second:
            one.add_second(k)
        del held_second[:]

    def fetch_second():
        flush_second()
        for one, k in late[:1]:
            one.fetch_second(k)
            held_second.append((one, k))
        del late[:1]

    def terms_and_start(work, n, one, which):
        work(n)
        one.start(which)

    def begin(one, terms):
        plan(terms_and_start, terms, 1, one, 0)
        plan(terms_and_start, terms, 3, one, 1)
        plan(terms, 2)
        plan(terms, 0)

    def plan(work, *given):
        tasks.append(functools.partial(work, *given))

    def work_on(count):
        for task in tasks[:count]:
            task()
        del tasks[:count]

    begin(sums.up, up_terms)
    for k in range(up_chunks):
        plan(first, sums.up, k)
    plan(flush_first)
    for block in range(fsdp):
        plan(feed_terms, block)
    begin(sums.down, down_terms)
    for k in range(down_chunks):
        plan(first, sums.down, k)
    plan(flush_first)

    work_on(2)
    r.grad_pairs[...] = jnp.zeros_like(r.grad_pairs)

    def home_feed(half, k):
        rows = line.at(half, k)
        feed = sum_feed.total(half, k) + vector(5)
        total = r.middle[pl.ds(k * step_rows, step_rows), :] + feed
        slot = place * tokens + half * line.half + k * step_rows
        slots = slot + lax.broadcasted_iota(jnp.int32, (step_rows, width), 0)
        keep = jnp.where(slots < length, 1.0, 0.0)
        note(r.late, 2, keep * total * total)
        note(r.late, 4, keep * feed * feed)
        r.feed_own[rows, :] = (keep * total).astype(LOW)
        spread_result.begin(half, k, r.feed_own)

    def attend_share(start):
        rows = pl.ds(start, share)
        total = mm_nt(r.grad_branch[rows, pl.ds(0, columns)], r.output[0])
        for block in range(1, fsdp):
            total += mm_nt(r.grad_branch[rows, pl.ds(block * columns, columns)], r.output[block])
        r.grad_mixture[...] = total.astype(LOW)
        keys = r.pairs[:, pl.ds(0, HD)]
        values = r.pairs[:, pl.ds(HD, HD)]
        shape = (share, keys.shape[0])
        query_at = place * tokens + start + lax.broadcasted_iota(jnp.int32, shape, 0)
        key_at = lax.broadcasted_iota(jnp.int32, shape, 1)
        allowed = (key_at <= query_at) & (key_at < length)
        factor = 1.0 / math.sqrt(HD)
        for head in range(heads):
            at = pl.ds(head * HD, HD)
            query = r.queries[rows, at]
            grad_mix = r.grad_mixture[:, at]
            scores = jnp.where(allowed, mm_nt(query, keys) * factor, NEGATIVE)
            soft = jnp.exp(scores - r.log_total[rows, pl.ds(head, 1)])
            grad_soft = mm_nt(grad_mix, values)
            dot_rows = jnp.sum(soft * grad_soft, -1, keepdims=True)
            grad_scores = (soft * (grad_soft - dot_rows) * factor).astype(LOW)
            r.grad_queries[rows, at] = mm(grad_scores, keys).astype(LOW)
            r.grad_pairs[:, pl.ds(0, HD)] += mm_tn(grad_scores, query)
            r.grad_pairs[:, pl.ds(HD, HD)] += mm_tn(soft.astype(LOW), grad_mix)

    every = (TP, FSDP, CTX)
    sum_early = RowSum(r.early, r.early_came, r.row_sems.at[0], every)
    sum_late = RowSum(r.late, r.late_came, r.row_sems.at[1], every)
    sum_rows = RowSum(r.own, r.own_came, r.row_sems.at[2], (FSDP, CTX))
    flow_two = Flow(sum_two, spread_branch, home_two, LAG)
    flow_feed = Flow(sum_feed, spread_result, home_feed, LAG)
    starts = [half * line.half + group * share for group in range(tp // 2) for half in range(2)]
    per_share = share // step_rows
    for n in range(flow_two.steps):
        flow_two.advance(1)
        if n == flow_two.steps - 4:
            flow_feed.launch()
        work_on(1)
        if n % 3 == 1:
            flush_second()
        if n >= 6 and n % 3 == 0:
            fetch_second()
        group = tp // 2 - (len(starts) + 1) // 2
        if starts and n >= flow_two.ready((group + 1) * per_share - 1):
            attend_share(starts.pop(0))
    work_on(len(tasks))
    for start in starts:
        attend_share(start)
        flow_feed.advance(1)
        fetch_second()
    sum_early.start()

    def pair_out(other):
        target = lax.rem(place + other, ctx)
        rows = pl.ds(pl.multiple_of(target * tokens, tokens), tokens)
        r.pair_sent[other - 1] = r.grad_pairs[rows, :].astype(LOW)
        return send(
            r.pair_sent.at[other - 1],
            r.pair_came.at[other - 1],
            r.pair_ctx_sem.at[0, other - 1],
            r.pair_ctx_sem.at[1, other - 1],
            CTX,
            target,
        )

    ctx_copies = [pair_out(other) for other in range(1, ctx)]
    for copy in ctx_copies:
        copy.start()
    sum_two.drain()

    def output_terms(n):
        terms = mm_tn(r.mixture[...], r.grad_branch[:, turn(n)])
        sums.output.piece(n, 0)[...] = terms.astype(LOW)

    def query_terms(n):
        terms = mm_tn(r.input_two[:, turn(n)], r.grad_queries[...])
        sums.query.piece(n, 0)[...] = terms.astype(LOW)

    def pair_terms(n):
        terms = mm_tn(r.input_two[:, turn(n)], r.pair_all[...].reshape(tokens, 2 * HD))
        r.pair_piece[n] = terms.astype(LOW)

    loads_one = pltpu.make_async_copy(r.input_one_hbm, r.input_two, r.load_sem.at[1])
    loads_one.start()
    begin(sums.output, output_terms)
    work_on(2)
    flow_feed.advance(1)
    flush_second()
    for copy in ctx_copies:
        copy.wait()
    own_rows = pl.ds(pl.multiple_of(place * tokens, tokens), tokens)
    own_pairs = r.grad_pairs[own_rows, :]
    for other in range(1, ctx):
        own_pairs += r.pair_came[other - 1].astype(WIDE)
    r.pair_own[...] = own_pairs.astype(LOW).reshape(r.pair_own.shape)

    @tiles(width, step)
    def _(col):
        at = pl.ds(col, step)
        part = mm_nt(r.grad_queries[...], r.query[at, :])
        part += mm_nt(r.pair_own[...].reshape(tokens, 2 * HD), r.pair[at, :])
        r.sum_own[:, at] = part.astype(LOW)

    def pair_line(other):
        target = lax.rem(zone + other, tp)
        return send(
            r.pair_own.at[target],
            r.pair_terms.at[other - 1],
            r.pair_line_sem.at[0, other - 1],
            r.pair_line_sem.at[1, other - 1],
            TP,
            target,
        )

    def pair_spread(other):
        return send(
            r.pair_all.at[zone],
            r.pair_all.at[zone],
            r.pair_line_sem.at[2, other - 1],
            r.pair_line_sem.at[3, other - 1],
            TP,
            lax.rem(zone + other, tp),
        )

    def pair_begin():
        for other in range(1, tp):
            pair_line(other).start()
        r.own[pl.ds(1, 1), pl.ds(0, query_width)] = jnp.sum(
            r.grad_queries[...].astype(WIDE), 0, keepdims=True
        )

    def pair_shares():
        total = r.pair_own[zone].astype(WIDE)
        for other in range(1, tp):
            pair_line(other).wait_recv()
            total += r.pair_terms[other - 1].astype(WIDE)
        r.pair_all[zone] = total.astype(LOW)
        for other in range(1, tp):
            pair_spread(other).start()

    def pair_gathered():
        for other in range(1, tp):
            pair_spread(other).wait_recv()
        values = r.pair_all[...].reshape(tokens, 2 * HD)[:, HD:]
        r.own[pl.ds(2, 1), pl.ds(0, HD)] = jnp.sum(values.astype(WIDE), 0, keepdims=True)

    def home_one(half, k):
        rows = line.at(half, k)
        here = pl.ds(k * step_rows, step_rows)
        unit, scaled = norm_of(r.stream[here, :].astype(WIDE))
        upstream = sum_one.total(half, k)
        note(r.late, 0, upstream * unit)
        note(r.late, 1, upstream)
        grad = r.grad_middle[here, :] + norm_backward(upstream, unit, scaled, vector(0))
        r.sum_own[rows, :] = grad.astype(LOW)
        spread_stream.begin(half, k, r.sum_own)

    flow_one = Flow(sum_one, spread_stream, home_one, LAG)
    flow_one.launch()
    pair_begin()
    plan(first, sums.output, 0)
    plan(flush_first)
    plan(loads_one.wait)
    begin(sums.query, query_terms)
    plan(pair_shares)
    plan(first, sums.query, 0)
    plan(flush_first)
    plan(pair_gathered)
    begin(sums.pair, pair_terms)
    plan(first, sums.pair, 0)
    plan(flush_first)
    plan(sum_rows.start)
    stream_load.wait()
    late_on = False
    for n in range(flow_one.steps):
        flow_one.advance(1)
        flow_feed.advance(1)
        work_on(2)
        if n % 2 == 0:
            fetch_second()
        if n % 2 == 1:
            flush_second()
        if n % 2 == 1:
            sum_early.move()
        sum_rows.move()
        if late_on:
            sum_late.move()
        elif flow_one.all_home() and flow_feed.all_home():
            sum_late.start()
            late_on = True
    work_on(len(tasks))
    flow_feed.advance(flow_feed.steps)
    if not late_on:
        sum_late.start()
    sum_early.finish()
    while late:
        fetch_second()
        flush_second()
        sum_rows.move()
        sum_late.move()
    flush_second()
    sum_rows.finish()
    sum_late.finish()
    mine = pl.ds(pl.multiple_of(me * columns, columns), columns)
    r.small[pl.ds(0, 4), :] = r.early[pl.ds(0, 4), mine]
    r.small[pl.ds(4, 2), :] = r.late[pl.ds(0, 2), mine]
    squares = jnp.sum(r.late[pl.ds(2, 3), pl.ds(0, width)], 1, keepdims=True)
    roots = jnp.sqrt(squares / (r.late[pl.ds(7, 1), pl.ds(0, 1)] * width))
    r.small[pl.ds(8, 3), :] = jnp.broadcast_to(roots, (3, columns))

    for half in range(2):

        @pl.when(line.is_home(half))
        def _():
            rows = pl.ds(half * line.half, line.half)
            copies = [
                pltpu.make_async_copy(r.feed_own.at[rows], r.result.at[rows], r.keep_sem.at[0]),
                pltpu.make_async_copy(r.sum_own.at[rows], r.stream_grad.at[rows], r.keep_sem.at[1]),
            ]
            for copy in copies:
                copy.start()
            for copy in copies:
                copy.wait()

    for one in (sum_feed, sum_one, spread_branch, spread_result, spread_stream):
        one.drain()
    for other in range(1, tp):
        pair_line(other).wait_send()
        pair_spread(other).wait_send()
    for one in vars(sums).values():
        one.finish()


def layer(values):
    fsdp, ctx, tp = lax.axis_size(FSDP), lax.axis_size(CTX), lax.axis_size(TP)
    tokens, width = values.stream.shape
    inner = values.up.shape[1]
    columns = width // fsdp
    share = tokens // tp
    query_width = values.query.shape[1]
    pair_width = 2 * HD
    key_count = ctx * tokens
    dma = pltpu.SemaphoreType.DMA
    wide_row = max(width, inner)
    hops, tp_hops = len(bits_of(FSDP)) + len(bits_of(CTX)), len(bits_of(TP))
    far_outs = dict(
        input_one_hbm=((tokens, width), LOW),
        result=((tokens, width), LOW),
        stream_grad=((tokens, width), LOW),
        up_last=((ctx, columns, inner), LOW),
        up_near=((2, columns, inner), LOW),
        up_far=((columns, inner), LOW),
        down_last=((ctx, inner, columns), LOW),
        down_near=((2, inner, columns), LOW),
        down_far=((inner, columns), LOW),
        output_last=((ctx, query_width, columns), LOW),
        output_near=((2, query_width, columns), LOW),
        output_far=((query_width, columns), LOW),
        query_last=((ctx, columns, query_width), LOW),
        query_near=((2, columns, query_width), LOW),
        query_far=((columns, query_width), LOW),
        pair_last=((ctx, columns, pair_width), LOW),
        pair_near=((2, columns, pair_width), LOW),
        pair_far=((columns, pair_width), LOW),
    )
    scratch = dict(
        up=pltpu.VMEM((width, inner), LOW),
        down=pltpu.VMEM((fsdp, inner, columns), LOW),
        input_two=pltpu.VMEM((tokens, width), LOW),
        grad_feed=pltpu.VMEM((tokens, width), LOW),
        hidden=pltpu.VMEM((tokens, inner), LOW),
        grad_pre=pltpu.VMEM((tokens, inner), LOW),
        work_one=pltpu.VMEM((tokens, columns), WIDE),
        sum_own=pltpu.VMEM((tokens, width), LOW),
        sum_slots=pltpu.VMEM((tokens, width), LOW),
        feed_own=pltpu.VMEM((tokens, width), LOW),
        feed_slots=pltpu.VMEM((tokens, width), LOW),
        grad_branch=pltpu.VMEM((tokens, width), LOW),
        middle=pltpu.VMEM((tokens // 2, width), WIDE),
        grad_middle=pltpu.VMEM((tokens // 2, width), WIDE),
        stream=pltpu.VMEM((tokens // 2, width), LOW),
        output=pltpu.VMEM((fsdp, query_width, columns), LOW),
        query=pltpu.VMEM((width, query_width), LOW),
        pair=pltpu.VMEM((width, pair_width), LOW),
        queries=pltpu.VMEM((tokens, query_width), LOW),
        pairs=pltpu.VMEM((key_count, pair_width), LOW),
        mixture=pltpu.VMEM((tokens, query_width), LOW),
        grad_mixture=pltpu.VMEM((share, query_width), LOW),
        grad_queries=pltpu.VMEM((tokens, query_width), LOW),
        grad_pairs=pltpu.VMEM((key_count, pair_width), WIDE),
        pair_sent=pltpu.VMEM((ctx - 1, tokens, pair_width), LOW),
        pair_came=pltpu.VMEM((ctx - 1, tokens, pair_width), LOW),
        pair_own=pltpu.VMEM((tp, share, pair_width), LOW),
        pair_terms=pltpu.VMEM((tp - 1, share, pair_width), LOW),
        pair_all=pltpu.VMEM((tp, share, pair_width), LOW),
        pair_piece=pltpu.VMEM((fsdp, columns, pair_width), LOW),
        stage_up=pltpu.VMEM((3, columns // 4, inner), LOW),
        stage_down=pltpu.VMEM((3, inner // 4, columns), LOW),
        smalls=pltpu.VMEM((fsdp,) + values.packed.shape, WIDE),
        vectors=pltpu.VMEM((8, wide_row), WIDE),
        squares=pltpu.VMEM((1, width), WIDE),
        log_total=pltpu.VMEM((tokens, query_width // HD), WIDE),
        front_sems=line_sems(tokens),
        spread_sems=line_sems(tokens),
        query_gather=Gather.sems(2),
        pair_gather=Gather.sems(2),
        output_gather=Gather.sems(1),
        up_gather=Gather.sems(2),
        down_gather=Gather.sems(2),
        small_sem=dma((2, fsdp - 1)),
        exchange_sem=dma((2, ctx - 1)),
        load_sem=dma((3,)),
        early=pltpu.VMEM((8, wide_row), WIDE),
        late=pltpu.VMEM((8, wide_row), WIDE),
        early_came=pltpu.VMEM((hops + tp_hops, 8, wide_row), WIDE),
        late_came=pltpu.VMEM((hops + tp_hops, 8, wide_row), WIDE),
        own_came=pltpu.VMEM((hops, 8, wide_row), WIDE),
        row_sems=dma((3, 2, hops + tp_hops)),
        keep_sem=dma((2,)),
        pair_ctx_sem=dma((2, ctx - 1)),
        pair_line_sem=dma((4, tp - 1)),
        two_sems=line_sems(tokens),
        feed_sems=line_sems(tokens),
        one_sems=line_sems(tokens),
        branch_sems=line_sems(tokens),
        result_sems=line_sems(tokens),
        stream_sems=line_sems(tokens),
        up_sems=PieceSum.sems(4),
        down_sems=PieceSum.sems(4),
        output_sems=PieceSum.sems(1),
        query_sems=PieceSum.sems(1),
        pair_sems=PieceSum.sems(1),
    )
    if tokens != query_width or inner < width:
        scratch.update(output_piece=pltpu.VMEM((fsdp, query_width, columns), LOW))
    if tokens != columns or inner < fsdp * query_width:
        scratch.update(query_piece=pltpu.VMEM((fsdp, columns, query_width), LOW))
    return call_kernel(
        layer_body,
        1,
        dict(
            stream_hbm=values.stream,
            cotangent_hbm=values.cotangent,
            query_shard=values.query,
            pair_shard=values.pair,
            output_shard=values.output,
            up_shard=values.up,
            down_shard=values.down,
        ),
        dict(packed=values.packed),
        dict(lengths=values.lengths),
        far_outs,
        dict(small=((16, columns), WIDE), own=((8, wide_row), WIDE)),
        scratch,
    )


def body(
    stream,
    cotangent,
    lengths,
    first_gain,
    first_shift,
    query_weight,
    query_bias,
    pair_weight,
    value_bias,
    output_weight,
    output_bias,
    second_gain,
    second_shift,
    up_weight,
    up_bias,
    down_weight,
    down_bias,
):
    fsdp = lax.axis_size(FSDP)
    me = lax.axis_index(FSDP)
    seq_count, group_len, width = stream.shape
    tokens = seq_count * group_len
    columns, inner = first_gain.shape[0], up_weight.shape[1]

    def placed(bias):
        spots = jnp.arange(fsdp)[None, :, None] == me
        return jnp.where(spots, bias.reshape(-1, 1, bias.shape[-1]).astype(WIDE), 0.0).reshape(-1)

    def row(values):
        return jnp.pad(values.astype(WIDE), (0, columns - values.shape[0]))[None]

    vectors = (first_gain, first_shift, output_bias, second_gain, second_shift, down_bias)
    packed = jnp.concatenate(
        [row(vector) for vector in vectors]
        + [row(placed(query_bias)), row(placed(value_bias.reshape(1, -1)))]
        + [placed(up_bias).reshape(-1, columns)]
    )
    packed = jnp.pad(packed, ((0, -packed.shape[0] % 8), (0, 0)))
    values = types.SimpleNamespace(
        stream=stream.reshape(tokens, width),
        cotangent=cotangent.reshape(tokens, width),
        lengths=lengths,
        packed=packed,
        query=query_weight,
        pair=pair_weight,
        output=output_weight,
        up=up_weight,
        down=down_weight,
    )
    ended = types.SimpleNamespace(**layer(values))
    small, own = ended.small, ended.own
    query_width = query_weight.shape[1]

    def finished(last):
        total = last[0].astype(WIDE)
        for place in range(1, last.shape[0]):
            total += last[place].astype(WIDE)
        return total

    up_bias_all = own[0, :inner].reshape(up_bias.shape[0], fsdp, -1)
    query_bias_all = own[1, :query_width].reshape(query_bias.shape[0], fsdp, -1)
    value_size = value_bias.shape[0]
    return (
        ended.result.reshape(stream.shape),
        ended.stream_grad.reshape(stream.shape),
        small[4],
        small[5],
        finished(ended.query_last),
        lax.dynamic_index_in_dim(query_bias_all, me, 1, False),
        finished(ended.pair_last),
        lax.dynamic_slice_in_dim(own[2], me * value_size, value_size, 0),
        finished(ended.output_last),
        small[2],
        small[0],
        small[1],
        finished(ended.up_last),
        lax.dynamic_index_in_dim(up_bias_all, me, 1, False),
        finished(ended.down_last),
        small[3],
        small[8:11, 0],
    )


def solution(mesh):
    in_specs = (
        P(FSDP, CTX, None),
        P(FSDP, CTX, None),
        P(FSDP),
        P(FSDP),
        P(FSDP),
        P(FSDP, TP),
        P(TP, FSDP),
        P(FSDP, None),
        P(FSDP),
        P(TP, FSDP),
        P(FSDP),
        P(FSDP),
        P(FSDP),
        P(FSDP, TP),
        P(TP, FSDP),
        P(TP, FSDP),
        P(FSDP),
    )
    out_specs = (
        P(FSDP, CTX, None),
        P(FSDP, CTX, None),
        P(FSDP),
        P(FSDP),
        P(FSDP, TP),
        P(TP, FSDP),
        P(FSDP, None),
        P(FSDP),
        P(TP, FSDP),
        P(FSDP),
        P(FSDP),
        P(FSDP),
        P(FSDP, TP),
        P(TP, FSDP),
        P(TP, FSDP),
        P(FSDP),
        P(),
    )
    return jax.shard_map(body, mesh=mesh, in_specs=in_specs, out_specs=out_specs, check_vma=False)
```
